32 devices in a mesh: groups: 2 (over y), ctx: 16 (over z, x, core).
Axes of the slice: x: 2, y: 2, z: 4, core: 2. Of those that a mesh axis runs over, the one named last changes fastest.
Arguments:
- query_feat: bfloat16 [4096, 4096], P(('groups', 'ctx')), parts along dimension 0, may hold values from -6 to 6
- key_feat: bfloat16 [4096, 4096], P(('groups', 'ctx')), parts along dimension 0, may hold values from -6 to 6
- value_raw: bfloat16 [4096, 4096], P(('groups', 'ctx')), parts along dimension 0, may hold values from -6 to 6
- conv_out: bfloat16 [4096, 4096], P(('groups', 'ctx')), parts along dimension 0, may hold values from -6 to 6
- out_grad: bfloat16 [4096, 4096], P(('groups', 'ctx')), parts along dimension 0, may hold values from -11 to 15
- filter_taps: bfloat16 [4096, 2048], P('ctx'), may hold values from -0.75 to 0.75
- short_filter: float32 [3, 4096], replicated, may hold values from -3.5 to 3.5
- skip_gain: float32 [4096], replicated, may hold values from 0.25 to 1.75
Outputs:
- query_grad: bfloat16 [4096, 4096], P(('groups', 'ctx')), parts along dimension 0
- key_grad: bfloat16 [4096, 4096], P(('groups', 'ctx')), parts along dimension 0
- value_grad: bfloat16 [4096, 4096], P(('groups', 'ctx')), parts along dimension 0
- filter_grad: bfloat16 [8192, 2048], P(('groups', 'ctx')), parts along dimension 0
- skip_grad: float32 [8192], P(('groups', 'ctx')), parts along dimension 0
- short_grad: float32 [3, 8192], P(None, ('groups', 'ctx')), parts along dimension 1
The draws below stay inside these ranges and needn't reach their ends.
There are 2 independent parts, one for each index of `groups`. The reference program is written for one: setup_inputs(seed, part) draws one part's arguments, and reference() takes and returns one part's arrays. A program takes and returns all parts, laid end to end along the dimension named above; an argument that names none is the same for every part. Nothing has to cross between parts.
All inputs are finite; a program needn't handle non-finite values.
Results may differ from the reference program's by a relative error of at most 0.0075.
Values may be sent and summed in bfloat16 or wider, within the bound.
No kernel may reach another device: no remote copies, remote signals or barrier semaphores. Data moves between devices by JAX's collectives and lax.ppermute only.
A program may use at most 128 MiB of HBM per device.

```python
import math
import jax
import jax.numpy as jnp
from jax import lax

C = 4096
SEQ = 2048


def draw_out_grad(key, part):
    key = jax.random.fold_in(key, 11)
    key_noise = jax.random.fold_in(key, 0)
    ramp = 0.5 + jnp.arange(SEQ, dtype=jnp.float32)[:, None] / (SEQ - 1)
    noise = jnp.clip(jax.random.normal(key_noise, (SEQ, C), jnp.float32), -4.0, 4.0)
    return (noise * ramp).astype(jnp.bfloat16)


def draw_filter_taps(key, part):
    key = jax.random.fold_in(key, 23)
    key_kind, key_span, key_noise = jax.random.split(key, 3)
    picks = jax.random.uniform(key_kind, (C, 1), jnp.float32)
    spread = jax.random.uniform(key_span, (C, 1), jnp.float32)
    slow_span = 0.5 * SEQ * jnp.exp(spread * math.log(16.0))
    fast_span = 30.0 + 20.0 * spread
    span = jnp.where(picks < 0.35, fast_span, slow_span)
    noise = jnp.clip(jax.random.normal(key_noise, (C, SEQ), jnp.float32), -4.0, 4.0)
    amplitude = 0.7 * jnp.sqrt(2.0 / (span * (1.0 - jnp.exp(-2.0 * SEQ / span))))
    steps = jnp.arange(SEQ, dtype=jnp.float32)[None, :]
    return (amplitude * jnp.exp(-steps / span) * noise).astype(jnp.bfloat16)


def block_scale(rng, dims, cuts, least, top_value):
    factor_of = 1.0
    for position, parts in cuts:
        heights = jax.random.uniform(jax.random.fold_in(jax.random.fold_in(rng, 6), position), (parts,), jnp.float32, least / len(cuts), top_value / len(cuts))
        factor_of = factor_of * jnp.repeat(jnp.exp(heights), dims[position] // parts).reshape((-1,) + (1,) * (len(dims) - 1 - position))
    return factor_of


def normal_values(rng, shape, scale, bound, cuts=(), kind=jnp.bfloat16):
    gain = block_scale(rng, shape, cuts, -0.22, 0.18) if cuts else 1.0
    values = jax.random.normal(rng, shape, jnp.float32) * scale * gain
    return jnp.minimum(jnp.maximum(values, -bound), bound).astype(kind)


def setup_inputs(seed: int = 0, part: int = 0) -> dict:
    seeds = jax.random.split(jax.random.key(seed), 9)
    own_keys = jax.random.split(jax.random.fold_in(seeds[8], part), 9)
    return {
        "query_feat": normal_values(own_keys[0], (SEQ, C), 1.0, 6.0, ((0, 16),)),
        "key_feat": normal_values(own_keys[1], (SEQ, C), 1.0, 6.0, ((0, 16),)),
        "value_raw": normal_values(own_keys[2], (SEQ, C), 1.0, 6.0, ((0, 16),)),
        "conv_out": normal_values(own_keys[3], (SEQ, C), 1.0, 6.0, ((0, 16),)),
        "out_grad": draw_out_grad(jax.random.fold_in(jax.random.fold_in(seeds[8], part), 71), part),
        "filter_taps": draw_filter_taps(jax.random.fold_in(seeds[8], 71), part),
        "short_filter": normal_values(seeds[6], (3, C), 3 ** -0.5, 3.5, (), jnp.float32),
        "skip_gain": jnp.clip(jax.random.uniform(seeds[7], (C,), jnp.float32, 0.25, 1.75), 0.25, 1.75),
    }


def reference(query_feat, key_feat, value_raw, conv_out, out_grad, filter_taps, short_filter, skip_gain):
    raw = value_raw.astype(jnp.float32)
    zero_rows = jnp.zeros((2, raw.shape[1]), jnp.float32)
    padded = jnp.concatenate([zero_rows, raw], 0)
    value_conv = short_filter[0] * padded[2:] + short_filter[1] * padded[1:-1] + short_filter[2] * padded[:-2]
    mixed = (key_feat.astype(jnp.float32) * value_conv).astype(jnp.bfloat16)
    gated = (out_grad.astype(jnp.float32) * query_feat.astype(jnp.float32)).astype(jnp.bfloat16)
    query_grad = (out_grad.astype(jnp.float32) * conv_out.astype(jnp.float32)).astype(jnp.bfloat16)
    skip_grad = jnp.sum(gated.astype(jnp.float32) * mixed.astype(jnp.float32), axis=0)

    gated_rows = gated.astype(jnp.float32).T.reshape(C // 256, 256, SEQ)
    mixed_rows = mixed.astype(jnp.float32).T.reshape(C // 256, 256, SEQ)
    filter_rows = filter_taps.astype(jnp.float32).reshape(C // 256, 256, SEQ)

    def one_block(item):
        gated_block, mixed_block, filter_block = item
        length = 2 * SEQ
        gated_spec = jnp.fft.rfft(gated_block, n=length, axis=1)
        mixed_spec = jnp.fft.rfft(mixed_block, n=length, axis=1)
        filter_spec = jnp.fft.rfft(filter_block, n=length, axis=1)
        back = jnp.fft.irfft(jnp.conj(filter_spec) * gated_spec, n=length, axis=1)[:, :SEQ]
        grads = jnp.fft.irfft(jnp.conj(mixed_spec) * gated_spec, n=length, axis=1)[:, :SEQ]
        return back, grads

    back_rows, grad_rows = lax.map(one_block, (gated_rows, mixed_rows, filter_rows))
    conv_back = back_rows.reshape(C, SEQ).T.astype(jnp.bfloat16)
    filter_grad = grad_rows.reshape(C, SEQ).astype(jnp.bfloat16)

    mixed_grad = conv_back.astype(jnp.float32) + skip_gain * gated.astype(jnp.float32)
    key_grad = (mixed_grad * value_conv).astype(jnp.bfloat16)
    feature_grad = (mixed_grad * key_feat.astype(jnp.float32)).astype(jnp.bfloat16)
    feature_wide = feature_grad.astype(jnp.float32)
    extended = jnp.concatenate([feature_wide, zero_rows], 0)
    value_grad = (short_filter[0] * extended[:-2] + short_filter[1] * extended[1:-1] + short_filter[2] * extended[2:]).astype(jnp.bfloat16)
    short_grad = jnp.stack([
        jnp.sum(feature_wide * padded[2:], axis=0),
        jnp.sum(feature_wide * padded[1:-1], axis=0),
        jnp.sum(feature_wide * padded[:-2], axis=0),
    ])
    return query_grad, key_grad, value_grad, filter_grad, skip_grad, short_grad
```

```python
import functools
import math

import jax
import jax.numpy as jnp
import numpy as np
from jax import lax
from jax.experimental import pallas as pl
from jax.experimental.pallas import tpu as pltpu
from jax.sharding import PartitionSpec as P

PRECISE = lax.Precision.HIGH


def passed_along(block, axis, distance):
    devices = range(lax.axis_size(axis))
    route = [(i - distance, i) for i in devices if i - distance in devices]
    return lax.ppermute(block, axis, route)


def dft_pair(row_count, col_count, period):
    row_index = lax.iota(jnp.int32, row_count)[:, None]
    col_index = lax.iota(jnp.int32, col_count)[None, :]
    phase = (row_index * col_index % period).astype(jnp.float32) * (-2.0 * math.pi / period)
    return (jnp.cos(phase), jnp.sin(phase))


def make_tables(inner, outer):
    half = outer // 2
    outer_cos, outer_sin = dft_pair(outer, half, outer)
    twist_cos, twist_sin = dft_pair(outer, inner, outer * inner)
    inner_cos, inner_sin = dft_pair(inner, inner, inner)
    real_outer = jnp.stack([outer_cos, outer_sin], 1)
    complex_outer = jnp.stack(
        [jnp.stack([outer_cos, -outer_sin], 1), jnp.stack([outer_sin, outer_cos], 1)], 1
    )
    inner_ahead = jnp.block([[inner_cos, inner_sin], [-inner_sin, inner_cos]])
    inner_back = jnp.block([[inner_cos, -inner_sin], [inner_sin, inner_cos]])
    outer_back = jnp.stack(
        [jnp.stack([outer_cos, outer_sin], 0), jnp.stack([-outer_sin, outer_cos], 0)], 0
    )
    return (real_outer, complex_outer, twist_cos, twist_sin, inner_ahead, inner_back, outer_back)


def twist_ahead(values, twist_cos, twist_sin):
    real_part = values[:, :, 0]
    imag_part = values[:, :, 1]
    return jnp.stack(
        [
            real_part * twist_cos - imag_part * twist_sin,
            real_part * twist_sin + imag_part * twist_cos,
        ],
        2,
    )


def twist_back(values, twist_cos, twist_sin):
    real_part = values[:, :, 0]
    imag_part = values[:, :, 1]
    return jnp.stack(
        [
            real_part * twist_cos + imag_part * twist_sin,
            imag_part * twist_cos - real_part * twist_sin,
        ],
        2,
    )


def inner_section(values, table):
    width, outer = (values.shape[0], values.shape[1])
    flat = values.reshape(width, outer, table.shape[0])
    return jnp.einsum(
        "wkc,cd->wkd", flat, table, precision=PRECISE, preferred_element_type=jnp.float32
    )


def real_spectrum(signal, tables):
    real_outer, complex_outer, twist_cos, twist_sin, inner_ahead, inner_back, outer_back = tables
    half = real_outer.shape[2]
    inner = twist_cos.shape[1]
    blocked = signal.reshape(signal.shape[0], half, inner)
    first = jnp.einsum(
        "wab,kra->wkrb", blocked, real_outer, precision=PRECISE, preferred_element_type=jnp.float32
    )
    return inner_section(twist_ahead(first, twist_cos, twist_sin), inner_ahead)


def complex_spectrum(signal_re, signal_im, tables):
    real_outer, complex_outer, twist_cos, twist_sin, inner_ahead, inner_back, outer_back = tables
    half = real_outer.shape[2]
    inner = twist_cos.shape[1]
    width = signal_re.shape[0]
    stacked = jnp.stack(
        [signal_re.reshape(width, half, inner), signal_im.reshape(width, half, inner)], 1
    )
    first = jnp.einsum(
        "wsab,krsa->wkrb",
        stacked,
        complex_outer,
        precision=PRECISE,
        preferred_element_type=jnp.float32,
    )
    return inner_section(twist_ahead(first, twist_cos, twist_sin), inner_ahead)


def inverse_spectrum(packed, tables):
    real_outer, complex_outer, twist_cos, twist_sin, inner_ahead, inner_back, outer_back = tables
    outer = twist_cos.shape[0]
    inner = twist_cos.shape[1]
    half = real_outer.shape[2]
    width = packed.shape[0]
    back = inner_section(packed, inner_back).reshape(width, outer, 2, inner)
    turned = twist_back(back, twist_cos, twist_sin)
    result = jnp.einsum(
        "wksb,rska->wrab", turned, outer_back, precision=PRECISE, preferred_element_type=jnp.float32
    )
    scale = 1.0 / (outer * inner)
    return (
        (result[:, 0] * scale).reshape(width, half * inner),
        (result[:, 1] * scale).reshape(width, half * inner),
    )


def spectral_block(gated_rows, mixed_rows, filter_rows, tables):
    inner = tables[2].shape[1]
    gated_spec = real_spectrum(gated_rows.astype(jnp.float32), tables)
    joint_spec = complex_spectrum(
        filter_rows.astype(jnp.float32), -mixed_rows.astype(jnp.float32), tables
    )
    gated_re = gated_spec[:, :, :inner]
    gated_im = gated_spec[:, :, inner:]
    joint_re = joint_spec[:, :, :inner]
    joint_im = joint_spec[:, :, inner:]
    product_re = joint_re * gated_re + joint_im * gated_im
    product_im = joint_re * gated_im - joint_im * gated_re
    product = jnp.concatenate([product_re, product_im], 2)
    result_re, result_im = inverse_spectrum(product, tables)
    return (result_re.astype(jnp.bfloat16), result_im.astype(jnp.bfloat16))


def general_plan(
    query_feat, key_feat, value_raw, conv_out, out_grad, filter_taps, short_filter, skip_gain
):
    rows = query_feat.shape[0]
    peers = lax.axis_size("ctx")
    before = passed_along(value_raw[rows - 2 :], "ctx", 1)
    padded = jnp.concatenate([before, value_raw], 0).astype(jnp.float32)
    value_conv = (
        short_filter[0] * padded[2:]
        + short_filter[1] * padded[1:-1]
        + short_filter[2] * padded[:-2]
    )
    mixed = (key_feat.astype(jnp.float32) * value_conv).astype(jnp.bfloat16)
    gated = (out_grad.astype(jnp.float32) * query_feat.astype(jnp.float32)).astype(jnp.bfloat16)
    query_grad = (out_grad.astype(jnp.float32) * conv_out.astype(jnp.float32)).astype(jnp.bfloat16)
    skip_part = jnp.sum(gated.astype(jnp.float32) * mixed.astype(jnp.float32), axis=0)
    tables = make_tables(rows, 2 * peers)
    gated_chan = gated.T
    mixed_chan = mixed.T
    sent_gated, sent_mixed = (
        lax.all_to_all(gated_chan, "ctx", split_axis=0, concat_axis=1, tiled=True),
        lax.all_to_all(mixed_chan, "ctx", split_axis=0, concat_axis=1, tiled=True),
    )
    back_rows, filter_grad = spectral_block(sent_gated, sent_mixed, filter_taps, tables)
    back_chan = lax.all_to_all(back_rows, "ctx", split_axis=1, concat_axis=0, tiled=True)
    conv_back = back_chan.T
    mixed_grad = conv_back.astype(jnp.float32) + skip_gain * gated.astype(jnp.float32)
    key_grad = (mixed_grad * value_conv).astype(jnp.bfloat16)
    feature_grad = (mixed_grad * key_feat.astype(jnp.float32)).astype(jnp.bfloat16)
    after = passed_along(feature_grad[:2], "ctx", -1)
    extended = jnp.concatenate([feature_grad, after], 0).astype(jnp.float32)
    value_grad = (
        short_filter[0] * extended[:-2]
        + short_filter[1] * extended[1:-1]
        + short_filter[2] * extended[2:]
    ).astype(jnp.bfloat16)
    feature_wide = extended[:-2]
    short_part = jnp.stack(
        [
            jnp.sum(feature_wide * padded[2:], axis=0),
            jnp.sum(feature_wide * padded[1:-1], axis=0),
            jnp.sum(feature_wide * padded[:-2], axis=0),
        ]
    )
    skip_grad, short_grad = (
        lax.psum_scatter(skip_part, "ctx", scatter_dimension=0, tiled=True),
        lax.psum_scatter(short_part, "ctx", scatter_dimension=1, tiled=True),
    )
    return (query_grad, key_grad, value_grad, filter_grad, skip_grad, short_grad)


INNER = 128


def half_spectrum(values, length):
    if length == 2:
        return [(values[0], None), (values[0], None)]
    even = half_spectrum(values[0::2], length // 2)
    odd = half_spectrum(values[1::2], length // 2)
    quarter = length // 4
    bins = [None] * (length // 2 + 1)
    bins[0] = (even[0][0] + odd[0][0], None)
    bins[length // 2] = (even[0][0] - odd[0][0], None)
    bins[quarter] = (even[quarter][0], -odd[quarter][0])
    for k in range(1, quarter):
        c = math.cos(2.0 * math.pi * k / length)
        s = math.sin(2.0 * math.pi * k / length)
        odd_re, odd_im = odd[k]
        even_re, even_im = even[k]
        if 2 * k == quarter:
            turn_re = (odd_re + odd_im) * c
            turn_im = (odd_im - odd_re) * c
        else:
            turn_re = odd_re * c + odd_im * s
            turn_im = odd_im * c - odd_re * s
        bins[k] = (even_re + turn_re, even_im + turn_im)
        bins[length // 2 - k] = (even_re - turn_re, turn_im - even_im)
    return bins


def first_half(bins, length):
    if length == 2:
        return [bins[0][0] + bins[1][0]]
    half = length // 2
    quarter = length // 4
    even = [None] * (quarter + 1)
    odd = [None] * (quarter + 1)
    even[0] = (bins[0][0] + bins[half][0], None)
    odd[0] = (bins[0][0] - bins[half][0], None)
    even[quarter] = (2.0 * bins[quarter][0], None)
    odd[quarter] = (-2.0 * bins[quarter][1], None)
    for k in range(1, quarter):
        c = math.cos(2.0 * math.pi * k / length)
        s = math.sin(2.0 * math.pi * k / length)
        near_re, near_im = bins[k]
        far_re, far_im = bins[half - k]
        even[k] = (near_re + far_re, near_im - far_im)
        gap_re = near_re - far_re
        gap_im = near_im + far_im
        if 2 * k == quarter:
            odd[k] = ((gap_re - gap_im) * c, (gap_re + gap_im) * c)
        else:
            odd[k] = (gap_re * c - gap_im * s, gap_re * s + gap_im * c)
    result = [None] * half
    result[0::2] = first_half(even, half)
    result[1::2] = first_half(odd, half)
    return result


def spectrum_tables(outer):
    size = outer * INNER
    near = np.arange(outer // 2 + 1)[:, None, None]
    place = np.arange(INNER)
    angle = -2.0 * np.pi * (
        (near * place[None, None, :]) / size + place[None, :, None] * place[None, None, :] / INNER
    )
    c, s = np.cos(angle), np.sin(angle)
    ahead = np.concatenate(
        [np.concatenate([c, -s], 2), np.concatenate([s, c], 2)], 1
    )
    back = np.swapaxes(ahead, 1, 2) / size
    return ahead.astype(jnp.bfloat16), back.astype(jnp.bfloat16)


def outer_ahead(load, z_ref, outer, width):
    def step(chunk, carry):
        row = pl.multiple_of(chunk * 16, 16)
        for lane in range(0, width, 128):
            values = [load(a, row, lane).astype(jnp.float32) for a in range(outer // 2)]
            bins = half_spectrum(values, outer)
            for k, (re, im) in enumerate(bins):
                im = jnp.zeros_like(re) if im is None else im
                z_ref[k, pl.ds(row, 16), lane : lane + 128] = re.astype(jnp.bfloat16)
                z_ref[k, pl.ds(INNER + row, 16), lane : lane + 128] = im.astype(jnp.bfloat16)
        return carry

    lax.fori_loop(0, INNER // 16, step, 0)


def outer_back(u_ref, store, outer, width):
    def step(chunk, carry):
        row = pl.multiple_of(chunk * 16, 16)
        for lane in range(0, width, 128):
            bins = []
            for k in range(outer // 2 + 1):
                re = u_ref[k, pl.ds(row, 16), lane : lane + 128]
                im = u_ref[k, pl.ds(INNER + row, 16), lane : lane + 128]
                bins.append((re, im))
            for a, value in enumerate(first_half(bins, outer)):
                store(a, row, lane, value)
        return carry

    lax.fori_loop(0, INNER // 16, step, 0)


def correlate_bin(first, gated):
    first_re, first_im = first[:INNER], first[INNER:]
    gated_re, gated_im = gated[:INNER], gated[INNER:]
    return jnp.concatenate(
        [
            first_re * gated_re + first_im * gated_im,
            first_re * gated_im - first_im * gated_re,
        ],
        0,
    ).astype(jnp.bfloat16)


def dot32(a, b):
    return jnp.dot(a, b, preferred_element_type=jnp.float32)


def filter_kernel(taps_ref, ahead_ref, spec_ref, rows_ref, z_ref, *, outer, width):
    for a in range(outer // 2):
        piece = taps_ref[:, a * INNER : (a + 1) * INNER].astype(jnp.float32)
        rows_ref[a * INNER : (a + 1) * INNER, :] = piece.T
    outer_ahead(
        lambda a, row, lane: rows_ref[pl.ds(a * INNER + row, 16), lane : lane + 128],
        z_ref, outer, width,
    )

    def one_bin(k, carry):
        spec_ref[k] = dot32(ahead_ref[k], z_ref[k]).astype(jnp.bfloat16)
        return carry

    lax.fori_loop(0, outer // 2 + 1, one_bin, 0)


def conv_kernel(gated_ref, filter_ref, ahead_ref, back_ref, conv_ref, spec_ref, z_ref, u_ref, *, outer, width):
    outer_ahead(
        lambda a, row, lane: gated_ref[pl.ds(a * INNER + row, 16), lane : lane + 128],
        z_ref, outer, width,
    )

    def one_bin(k, carry):
        gated = dot32(ahead_ref[k], z_ref[k])
        spec_ref[k] = gated.astype(jnp.bfloat16)
        product = correlate_bin(filter_ref[k].astype(jnp.float32), gated)
        u_ref[k] = dot32(back_ref[k], product)
        return carry

    lax.fori_loop(0, outer // 2 + 1, one_bin, 0)

    def store(a, row, lane, value):
        conv_ref[pl.ds(a * INNER + row, 16), lane : lane + 128] = value.astype(jnp.bfloat16)

    outer_back(u_ref, store, outer, width)


def grad_kernel(mixed_ref, gated_ref, spec_ref, ahead_ref, back_ref, grad_ref, skip_ref, z_ref, u_ref, rows_ref, *, outer, width):
    outer_ahead(
        lambda a, row, lane: mixed_ref[pl.ds(a * INNER + row, 16), lane : lane + 128],
        z_ref, outer, width,
    )

    def one_bin(k, carry):
        mixed = dot32(ahead_ref[k], z_ref[k])
        product = correlate_bin(mixed, spec_ref[k].astype(jnp.float32))
        u_ref[k] = dot32(back_ref[k], product)
        return carry

    lax.fori_loop(0, outer // 2 + 1, one_bin, 0)

    def store(a, row, lane, value):
        rows_ref[pl.ds(a * INNER + row, 16), lane : lane + 128] = value

    outer_back(u_ref, store, outer, width)
    for a in range(outer // 2):
        grad_ref[:, a * INNER : (a + 1) * INNER] = rows_ref[
            a * INNER : (a + 1) * INNER, :
        ].T.astype(jnp.bfloat16)

    def add(a, total):
        place = pl.ds(pl.multiple_of(a * INNER, INNER), INNER)
        part = gated_ref[place, :].astype(jnp.float32) * mixed_ref[place, :].astype(jnp.float32)
        return total + jnp.sum(part.reshape(INNER // 8, 8, width), axis=0)

    total = lax.fori_loop(0, outer // 2, add, jnp.zeros((8, width), jnp.float32))
    skip_ref[...] = jnp.sum(total, axis=0, keepdims=True)


def later_grad_kernel(mixed_ref, gated_ref, spec_ref, ahead_ref, back_ref, done_ref, *rest, outer, width):
    grad_kernel(mixed_ref, gated_ref, spec_ref, ahead_ref, back_ref, *rest, outer=outer, width=width)


def shifted_down(values, distance, edge):
    moved = pltpu.roll(values, distance, 0)
    row = lax.broadcasted_iota(jnp.int32, values.shape, 0)
    for i in range(distance):
        source = edge.shape[0] - distance + i
        moved = jnp.where(row == i, edge[source : source + 1], moved)
    return moved


def shifted_up(values, distance, edge):
    count = values.shape[0]
    moved = pltpu.roll(values, count - distance, 0)
    row = lax.broadcasted_iota(jnp.int32, values.shape, 0)
    for i in range(distance):
        moved = jnp.where(row == count - distance + i, edge[i : i + 1], moved)
    return moved


def gate_kernel(grad_ref, query_ref, gated_ref, *, width):
    for j in range(gated_ref.shape[0]):
        cols = slice(j * width, (j + 1) * width)
        gated_ref[j] = (
            grad_ref[:, cols].astype(jnp.float32) * query_ref[:, cols].astype(jnp.float32)
        ).astype(jnp.bfloat16)


def mix_kernel(key_ref, value_ref, edge_ref, short_ref, grad_ref, conv_ref, *rest, width, parts):
    mixed_refs, query_grad_ref = rest[:parts], rest[parts]
    piece = width // parts
    for j in range(mixed_refs[0].shape[0]):
        for part in range(parts):
            cols = slice(j * width + part * piece, j * width + (part + 1) * piece)
            value = value_ref[:, cols].astype(jnp.float32)
            edge = edge_ref[:, cols].astype(jnp.float32)
            conv = (
                short_ref[0:1, cols] * value
                + short_ref[1:2, cols] * shifted_down(value, 1, edge)
                + short_ref[2:3, cols] * shifted_down(value, 2, edge)
            )
            mixed_refs[part][j] = (key_ref[:, cols].astype(jnp.float32) * conv).astype(jnp.bfloat16)
            query_grad_ref[:, cols] = (
                grad_ref[:, cols].astype(jnp.float32) * conv_ref[:, cols].astype(jnp.float32)
            ).astype(jnp.bfloat16)


def finish_kernel(
    back_ref, gated_ref, key_ref, value_ref, edge_ref, short_ref, skip_ref,
    key_grad_ref, value_grad_ref, head_ref, tail_ref, part_ref, *, width,
):
    rows = key_ref.shape[0]
    for j in range(back_ref.shape[0]):
        for lane in range(0, width, 128):
            cols = slice(j * width + lane, j * width + lane + 128)
            lanes = slice(lane, lane + 128)
            value = value_ref[:, cols].astype(jnp.float32)
            edge = edge_ref[:, cols].astype(jnp.float32)
            value_1 = shifted_down(value, 1, edge)
            value_2 = shifted_down(value, 2, edge)
            short = [short_ref[i : i + 1, cols] for i in range(3)]
            conv = short[0] * value + short[1] * value_1 + short[2] * value_2
            mixed_grad = back_ref[j, :, lanes].astype(jnp.float32) + skip_ref[:, cols] * gated_ref[
                j, :, lanes
            ].astype(jnp.float32)
            key_grad_ref[:, cols] = (mixed_grad * conv).astype(jnp.bfloat16)
            feature = (mixed_grad * key_ref[:, cols].astype(jnp.float32)).astype(jnp.bfloat16)
            head_ref[:, cols] = feature[:16]
            tail_ref[:, cols] = feature[rows - 16 :]
            feature = feature.astype(jnp.float32)
            zero = jnp.zeros((2, 128), jnp.float32)
            value_grad_ref[:, cols] = (
                short[0] * feature
                + short[1] * shifted_up(feature, 1, zero)
                + short[2] * shifted_up(feature, 2, zero)
            ).astype(jnp.bfloat16)
            for i, other in enumerate((value, value_1, value_2)):
                part_ref[j, i : i + 1, lanes] = jnp.sum(feature * other, axis=0, keepdims=True)
            part_ref[j, 3:8, lanes] = jnp.zeros((5, 128), jnp.float32)


def seam_kernel(tail_ref, head_ref, short_ref, done_ref, value_grad_ref):
    feature = tail_ref[...].astype(jnp.float32)
    head = head_ref[...].astype(jnp.float32)
    value_grad_ref[...] = (
        short_ref[0:1] * feature
        + short_ref[1:2] * shifted_up(feature, 1, head)
        + short_ref[2:3] * shifted_up(feature, 2, head)
    ).astype(jnp.bfloat16)


def exchanged(block):
    return lax.all_to_all(block, "ctx", split_axis=0, concat_axis=0, tiled=True)


def paired(block, distance):
    return lax.ppermute(block, "ctx", [(i, i ^ distance) for i in range(lax.axis_size("ctx"))])


def summed_at_owner(parts):
    peers = lax.axis_size("ctx")
    me = lax.axis_index("ctx")
    inner = 4 if peers % 4 == 0 else 1
    for count, place, step in ((peers // inner, me // inner, inner), (inner, me % inner, 1)):
        if step == inner:
            parts = parts.reshape((count, inner) + parts.shape[1:])
        mine = lax.dynamic_index_in_dim(parts, place, 0, keepdims=False)
        for distance in range(1, count):
            other = lax.dynamic_index_in_dim(parts, place ^ distance, 0, keepdims=False)
            mine = mine + paired(other, distance * step)
        parts = mine
    return parts


def after(value, *others):
    return lax.optimization_barrier((value,) + others)[0]


def params(mib=48):
    return pltpu.CompilerParams(vmem_limit_bytes=mib * 1024 * 1024)


def cost(flops, size):
    return pl.CostEstimate(flops=flops, bytes_accessed=size, transcendentals=0)


def kernel_plan(
    query_feat, key_feat, value_raw, conv_out, out_grad, filter_taps, short_filter, skip_gain
):
    rows, channels = query_feat.shape
    peers = lax.axis_size("ctx")
    width = channels // peers
    seq = rows * peers
    outer = 2 * seq // INNER
    bins = outer // 2 + 1
    steps = 4
    group = peers // steps
    span = group * width
    parts = 2
    piece = width // parts
    bf16, f32 = jnp.bfloat16, jnp.float32
    shape = jax.ShapeDtypeStruct
    skip_row = skip_gain.reshape(1, channels)
    ahead, back = (jnp.asarray(t) for t in spectrum_tables(outer))

    flat = pl.BlockSpec((rows, span), lambda i: (0, i))
    owned = pl.BlockSpec((group, rows, width), lambda i: (i, 0, 0))
    owned_part = pl.BlockSpec((group, rows, piece), lambda i: (i, 0, 0))
    edge_spec = pl.BlockSpec((16, span), lambda i: (0, i))
    short_spec = pl.BlockSpec((3, span), lambda i: (0, i))
    skip_spec = pl.BlockSpec((1, span), lambda i: (0, i))

    gated = pl.pallas_call(
        functools.partial(gate_kernel, width=width),
        grid=(steps,),
        in_specs=[flat, flat],
        out_specs=owned,
        out_shape=shape((peers, rows, width), bf16),
        compiler_params=params(),
        cost_estimate=cost(rows * channels, 6 * rows * channels),
        name="gate",
    )(out_grad, query_feat)

    gated_got = exchanged(gated.reshape(seq, width))

    edge = passed_along(value_raw[rows - 16 :], "ctx", 1)
    *mixed, query_grad = pl.pallas_call(
        functools.partial(mix_kernel, width=width, parts=parts),
        grid=(steps,),
        in_specs=[flat, flat, edge_spec, short_spec, flat, flat],
        out_specs=[owned_part] * parts + [flat],
        out_shape=[shape((peers, rows, piece), bf16)] * parts + [shape((rows, channels), bf16)],
        compiler_params=params(),
        cost_estimate=cost(10 * rows * channels, 12 * rows * channels),
        name="mix",
    )(key_feat, value_raw, edge, short_filter, out_grad, conv_out)

    spec_shape = shape((bins, 2 * INNER, width), bf16)
    z_scratch = pltpu.VMEM((bins, 2 * INNER, width), bf16)
    u_scratch = pltpu.VMEM((bins, 2 * INNER, width), f32)
    table_bytes = 8 * bins * INNER * INNER
    spec_bytes = 4 * bins * INNER * width
    work = 2 * bins * (2 * INNER) ** 2 * width
    filter_spec = pl.pallas_call(
        functools.partial(filter_kernel, outer=outer, width=width),
        out_shape=spec_shape,
        scratch_shapes=[pltpu.VMEM((seq, width), f32), z_scratch],
        compiler_params=params(),
        cost_estimate=cost(work, table_bytes + spec_bytes + 2 * seq * width),
        name="filter_spectrum",
    )(filter_taps, ahead)

    mixed_got = [None] * parts
    mixed_got[0] = exchanged(after(mixed[0], gated_got).reshape(seq, piece))

    conv_back, gated_spec = pl.pallas_call(
        functools.partial(conv_kernel, outer=outer, width=width),
        out_shape=(shape((seq, width), bf16), spec_shape),
        scratch_shapes=[z_scratch, u_scratch],
        compiler_params=params(),
        cost_estimate=cost(2 * work, 2 * table_bytes + 2 * spec_bytes + 4 * seq * width),
        name="conv_back",
    )(gated_got, filter_spec, ahead, back)

    back_got = exchanged(after(conv_back, mixed_got[0])).reshape(peers, rows, width)
    mixed_got[1] = exchanged(after(mixed[1], back_got).reshape(seq, piece))

    key_grad, value_grad, head, tail, short_part = pl.pallas_call(
        functools.partial(finish_kernel, width=width),
        grid=(steps,),
        in_specs=[owned, owned, flat, flat, edge_spec, short_spec, skip_spec],
        out_specs=[flat, flat, edge_spec, edge_spec, pl.BlockSpec((group, 8, width), lambda i: (i, 0, 0))],
        out_shape=[
            shape((rows, channels), bf16),
            shape((rows, channels), bf16),
            shape((16, channels), bf16),
            shape((16, channels), bf16),
            shape((peers, 8, width), f32),
        ],
        compiler_params=params(),
        cost_estimate=cost(30 * rows * channels, 12 * rows * channels),
        name="finish",
    )(back_got, gated, key_feat, value_raw, edge, short_filter, skip_row)

    head_got = passed_along(head, "ctx", -1)
    whole = lambda size: pl.BlockSpec((size, channels), lambda i: (0, 0))
    value_grad = pl.pallas_call(
        seam_kernel,
        grid=(1,),
        in_specs=[whole(16), whole(16), whole(3), pl.BlockSpec(memory_space=pl.ANY)],
        out_specs=pl.BlockSpec((16, channels), lambda i: (rows // 16 - 1, 0)),
        out_shape=shape((rows, channels), bf16),
        input_output_aliases={3: 0},
        compiler_params=params(),
        cost_estimate=cost(5 * 16 * channels, 6 * 16 * channels),
        name="seam",
    )(tail, head_got, short_filter, value_grad)
    short_grad = summed_at_owner(short_part)[:3]

    filter_grad = None
    skip_parts = []
    for part in range(parts):
        at = part
        in_specs = [
            pl.BlockSpec((seq, piece), lambda i: (0, 0)),
            pl.BlockSpec((seq, piece), lambda i, at=at: (0, at)),
            pl.BlockSpec((bins, 2 * INNER, piece), lambda i, at=at: (0, 0, at)),
            pl.BlockSpec((bins, 2 * INNER, 2 * INNER), lambda i: (0, 0, 0)),
            pl.BlockSpec((bins, 2 * INNER, 2 * INNER), lambda i: (0, 0, 0)),
        ]
        operands = [mixed_got[part], gated_got, gated_spec, ahead, back]
        body = functools.partial(grad_kernel, outer=outer, width=piece)
        if part:
            in_specs.append(pl.BlockSpec(memory_space=pl.ANY))
            operands.append(filter_grad)
            body = functools.partial(later_grad_kernel, outer=outer, width=piece)
        filter_grad, skip_part = pl.pallas_call(
            body,
            grid=(1,),
            in_specs=in_specs,
            out_specs=[
                pl.BlockSpec((piece, seq), lambda i, at=at: (at, 0)),
                pl.BlockSpec((1, piece), lambda i: (0, 0)),
            ],
            out_shape=[shape((width, seq), bf16), shape((1, piece), f32)],
            scratch_shapes=[
                pltpu.VMEM((bins, 2 * INNER, piece), bf16),
                pltpu.VMEM((bins, 2 * INNER, piece), f32),
                pltpu.VMEM((seq, piece), f32),
            ],
            input_output_aliases={5: 0} if part else {},
            compiler_params=params(),
            cost_estimate=cost(2 * work // parts, 2 * table_bytes + spec_bytes),
            name=f"filter_grad_{part}",
        )(*operands)
        skip_parts.append(skip_part)
    skip_grad = jnp.concatenate(skip_parts, 1).reshape(width)
    return query_grad, key_grad, value_grad, filter_grad, skip_grad, short_grad


def per_device(query_feat, key_feat, value_raw, conv_out, out_grad, filter_taps, short_filter, skip_gain):
    rows, channels = query_feat.shape
    peers = lax.axis_size("ctx")
    width = channels // peers
    fits = (
        peers % 4 == 0
        and peers & (peers - 1) == 0
        and rows % 16 == 0
        and width % 256 == 0
        and rows * peers in (8 * INNER, 16 * INNER)
    )
    plan = kernel_plan if fits else general_plan
    return plan(query_feat, key_feat, value_raw, conv_out, out_grad, filter_taps, short_filter, skip_gain)


def solution(mesh):
    in_specs = (
        P(("groups", "ctx"), None),
        P(("groups", "ctx"), None),
        P(("groups", "ctx"), None),
        P(("groups", "ctx"), None),
        P(("groups", "ctx"), None),
        P("ctx", None),
        P(),
        P(),
    )
    out_specs = (
        P(("groups", "ctx"), None),
        P(("groups", "ctx"), None),
        P(("groups", "ctx"), None),
        P(("groups", "ctx"), None),
        P(("groups", "ctx")),
        P(None, ("groups", "ctx")),
    )
    return jax.shard_map(
        per_device, mesh=mesh, in_specs=in_specs, out_specs=out_specs, check_vma=False
    )
```

```python
import functools
import math

import jax
import jax.numpy as jnp
import numpy as np
from jax import lax
from jax.experimental import pallas as pl
from jax.experimental.pallas import tpu as pltpu
from jax.sharding import PartitionSpec as P

PRECISE = lax.Precision.HIGH


def passed_along(block, axis, distance):
    devices = range(lax.axis_size(axis))
    route = [(i - distance, i) for i in devices if i - distance in devices]
    return lax.ppermute(block, axis, route)


def dft_pair(row_count, col_count, period):
    row_index = lax.iota(jnp.int32, row_count)[:, None]
    col_index = lax.iota(jnp.int32, col_count)[None, :]
    phase = (row_index * col_index % period).astype(jnp.float32) * (-2.0 * math.pi / period)
    return (jnp.cos(phase), jnp.sin(phase))


def make_tables(inner, outer):
    half = outer // 2
    outer_cos, outer_sin = dft_pair(outer, half, outer)
    twist_cos, twist_sin = dft_pair(outer, inner, outer * inner)
    inner_cos, inner_sin = dft_pair(inner, inner, inner)
    real_outer = jnp.stack([outer_cos, outer_sin], 1)
    complex_outer = jnp.stack(
        [jnp.stack([outer_cos, -outer_sin], 1), jnp.stack([outer_sin, outer_cos], 1)], 1
    )
    inner_ahead = jnp.block([[inner_cos, inner_sin], [-inner_sin, inner_cos]])
    inner_back = jnp.block([[inner_cos, -inner_sin], [inner_sin, inner_cos]])
    outer_back = jnp.stack(
        [jnp.stack([outer_cos, outer_sin], 0), jnp.stack([-outer_sin, outer_cos], 0)], 0
    )
    return (real_outer, complex_outer, twist_cos, twist_sin, inner_ahead, inner_back, outer_back)


def twist_ahead(values, twist_cos, twist_sin):
    real_part = values[:, :, 0]
    imag_part = values[:, :, 1]
    return jnp.stack(
        [
            real_part * twist_cos - imag_part * twist_sin,
            real_part * twist_sin + imag_part * twist_cos,
        ],
        2,
    )


def twist_back(values, twist_cos, twist_sin):
    real_part = values[:, :, 0]
    imag_part = values[:, :, 1]
    return jnp.stack(
        [
            real_part * twist_cos + imag_part * twist_sin,
            imag_part * twist_cos - real_part * twist_sin,
        ],
        2,
    )


def inner_section(values, table):
    width, outer = (values.shape[0], values.shape[1])
    flat = values.reshape(width, outer, table.shape[0])
    return jnp.einsum(
        "wkc,cd->wkd", flat, table, precision=PRECISE, preferred_element_type=jnp.float32
    )


def real_spectrum(signal, tables):
    real_outer, complex_outer, twist_cos, twist_sin, inner_ahead, inner_back, outer_back = tables
    half = real_outer.shape[2]
    inner = twist_cos.shape[1]
    blocked = signal.reshape(signal.shape[0], half, inner)
    first = jnp.einsum(
        "wab,kra->wkrb", blocked, real_outer, precision=PRECISE, preferred_element_type=jnp.float32
    )
    return inner_section(twist_ahead(first, twist_cos, twist_sin), inner_ahead)


def complex_spectrum(signal_re, signal_im, tables):
    real_outer, complex_outer, twist_cos, twist_sin, inner_ahead, inner_back, outer_back = tables
    half = real_outer.shape[2]
    inner = twist_cos.shape[1]
    width = signal_re.shape[0]
    stacked = jnp.stack(
        [signal_re.reshape(width, half, inner), signal_im.reshape(width, half, inner)], 1
    )
    first = jnp.einsum(
        "wsab,krsa->wkrb",
        stacked,
        complex_outer,
        precision=PRECISE,
        preferred_element_type=jnp.float32,
    )
    return inner_section(twist_ahead(first, twist_cos, twist_sin), inner_ahead)


def inverse_spectrum(packed, tables):
    real_outer, complex_outer, twist_cos, twist_sin, inner_ahead, inner_back, outer_back = tables
    outer = twist_cos.shape[0]
    inner = twist_cos.shape[1]
    half = real_outer.shape[2]
    width = packed.shape[0]
    back = inner_section(packed, inner_back).reshape(width, outer, 2, inner)
    turned = twist_back(back, twist_cos, twist_sin)
    result = jnp.einsum(
        "wksb,rska->wrab", turned, outer_back, precision=PRECISE, preferred_element_type=jnp.float32
    )
    scale = 1.0 / (outer * inner)
    return (
        (result[:, 0] * scale).reshape(width, half * inner),
        (result[:, 1] * scale).reshape(width, half * inner),
    )


def spectral_block(gated_rows, mixed_rows, filter_rows, tables):
    inner = tables[2].shape[1]
    gated_spec = real_spectrum(gated_rows.astype(jnp.float32), tables)
    joint_spec = complex_spectrum(
        filter_rows.astype(jnp.float32), -mixed_rows.astype(jnp.float32), tables
    )
    gated_re = gated_spec[:, :, :inner]
    gated_im = gated_spec[:, :, inner:]
    joint_re = joint_spec[:, :, :inner]
    joint_im = joint_spec[:, :, inner:]
    product_re = joint_re * gated_re + joint_im * gated_im
    product_im = joint_re * gated_im - joint_im * gated_re
    product = jnp.concatenate([product_re, product_im], 2)
    result_re, result_im = inverse_spectrum(product, tables)
    return (result_re.astype(jnp.bfloat16), result_im.astype(jnp.bfloat16))


def general_plan(
    query_feat, key_feat, value_raw, conv_out, out_grad, filter_taps, short_filter, skip_gain
):
    rows = query_feat.shape[0]
    peers = lax.axis_size("ctx")
    before = passed_along(value_raw[rows - 2 :], "ctx", 1)
    padded = jnp.concatenate([before, value_raw], 0).astype(jnp.float32)
    value_conv = (
        short_filter[0] * padded[2:]
        + short_filter[1] * padded[1:-1]
        + short_filter[2] * padded[:-2]
    )
    mixed = (key_feat.astype(jnp.float32) * value_conv).astype(jnp.bfloat16)
    gated = (out_grad.astype(jnp.float32) * query_feat.astype(jnp.float32)).astype(jnp.bfloat16)
    query_grad = (out_grad.astype(jnp.float32) * conv_out.astype(jnp.float32)).astype(jnp.bfloat16)
    skip_part = jnp.sum(gated.astype(jnp.float32) * mixed.astype(jnp.float32), axis=0)
    tables = make_tables(rows, 2 * peers)
    gated_chan = gated.T
    mixed_chan = mixed.T
    sent_gated, sent_mixed = (
        lax.all_to_all(gated_chan, "ctx", split_axis=0, concat_axis=1, tiled=True),
        lax.all_to_all(mixed_chan, "ctx", split_axis=0, concat_axis=1, tiled=True),
    )
    back_rows, filter_grad = spectral_block(sent_gated, sent_mixed, filter_taps, tables)
    back_chan = lax.all_to_all(back_rows, "ctx", split_axis=1, concat_axis=0, tiled=True)
    conv_back = back_chan.T
    mixed_grad = conv_back.astype(jnp.float32) + skip_gain * gated.astype(jnp.float32)
    key_grad = (mixed_grad * value_conv).astype(jnp.bfloat16)
    feature_grad = (mixed_grad * key_feat.astype(jnp.float32)).astype(jnp.bfloat16)
    after = passed_along(feature_grad[:2], "ctx", -1)
    extended = jnp.concatenate([feature_grad, after], 0).astype(jnp.float32)
    value_grad = (
        short_filter[0] * extended[:-2]
        + short_filter[1] * extended[1:-1]
        + short_filter[2] * extended[2:]
    ).astype(jnp.bfloat16)
    feature_wide = extended[:-2]
    short_part = jnp.stack(
        [
            jnp.sum(feature_wide * padded[2:], axis=0),
            jnp.sum(feature_wide * padded[1:-1], axis=0),
            jnp.sum(feature_wide * padded[:-2], axis=0),
        ]
    )
    skip_grad, short_grad = (
        lax.psum_scatter(skip_part, "ctx", scatter_dimension=0, tiled=True),
        lax.psum_scatter(short_part, "ctx", scatter_dimension=1, tiled=True),
    )
    return (query_grad, key_grad, value_grad, filter_grad, skip_grad, short_grad)


INNER = 128
INNER_PEERS = 4


def half_spectrum(values, length):
    if length == 2:
        return [(values[0], None), (values[0], None)]
    even = half_spectrum(values[0::2], length // 2)
    odd = half_spectrum(values[1::2], length // 2)
    quarter = length // 4
    bins = [None] * (length // 2 + 1)
    bins[0] = (even[0][0] + odd[0][0], None)
    bins[length // 2] = (even[0][0] - odd[0][0], None)
    bins[quarter] = (even[quarter][0], -odd[quarter][0])
    for k in range(1, quarter):
        c = math.cos(2.0 * math.pi * k / length)
        s = math.sin(2.0 * math.pi * k / length)
        odd_re, odd_im = odd[k]
        even_re, even_im = even[k]
        if 2 * k == quarter:
            turn_re = (odd_re + odd_im) * c
            turn_im = (odd_im - odd_re) * c
        else:
            turn_re = odd_re * c + odd_im * s
            turn_im = odd_im * c - odd_re * s
        bins[k] = (even_re + turn_re, even_im + turn_im)
        bins[length // 2 - k] = (even_re - turn_re, turn_im - even_im)
    return bins


def first_half(bins, length):
    if length == 2:
        return [bins[0][0] + bins[1][0]]
    half = length // 2
    quarter = length // 4
    even = [None] * (quarter + 1)
    odd = [None] * (quarter + 1)
    even[0] = (bins[0][0] + bins[half][0], None)
    odd[0] = (bins[0][0] - bins[half][0], None)
    even[quarter] = (2.0 * bins[quarter][0], None)
    odd[quarter] = (-2.0 * bins[quarter][1], None)
    for k in range(1, quarter):
        c = math.cos(2.0 * math.pi * k / length)
        s = math.sin(2.0 * math.pi * k / length)
        near_re, near_im = bins[k]
        far_re, far_im = bins[half - k]
        even[k] = (near_re + far_re, near_im - far_im)
        gap_re = near_re - far_re
        gap_im = near_im + far_im
        if 2 * k == quarter:
            odd[k] = ((gap_re - gap_im) * c, (gap_re + gap_im) * c)
        else:
            odd[k] = (gap_re * c - gap_im * s, gap_re * s + gap_im * c)
    result = [None] * half
    result[0::2] = first_half(even, half)
    result[1::2] = first_half(odd, half)
    return result


def spectrum_tables(outer):
    size = outer * INNER
    near = np.arange(outer // 2 + 1)[:, None, None]
    place = np.arange(INNER)
    angle = -2.0 * np.pi * (
        (near * place[None, None, :]) / size + place[None, :, None] * place[None, None, :] / INNER
    )
    c, s = np.cos(angle), np.sin(angle)
    ahead = np.concatenate(
        [np.concatenate([c, -s], 2), np.concatenate([s, c], 2)], 1
    )
    back = np.swapaxes(ahead, 1, 2) / size
    return ahead.astype(jnp.bfloat16), back.astype(jnp.bfloat16)


def outer_ahead(load, z_ref, outer, width):
    def step(chunk, carry):
        row = pl.multiple_of(chunk * 16, 16)
        for lane in range(0, width, 128):
            values = [load(a, row, lane).astype(jnp.float32) for a in range(outer // 2)]
            bins = half_spectrum(values, outer)
            for k, (re, im) in enumerate(bins):
                im = jnp.zeros_like(re) if im is None else im
                z_ref[k, pl.ds(row, 16), lane : lane + 128] = re.astype(jnp.bfloat16)
                z_ref[k, pl.ds(INNER + row, 16), lane : lane + 128] = im.astype(jnp.bfloat16)
        return carry

    lax.fori_loop(0, INNER // 16, step, 0)


def outer_back(u_ref, store, outer, width):
    def step(chunk, carry):
        row = pl.multiple_of(chunk * 16, 16)
        for lane in range(0, width, 128):
            bins = []
            for k in range(outer // 2 + 1):
                re = u_ref[k, pl.ds(row, 16), lane : lane + 128]
                im = u_ref[k, pl.ds(INNER + row, 16), lane : lane + 128]
                bins.append((re, im))
            for a, value in enumerate(first_half(bins, outer)):
                store(a, row, lane, value)
        return carry

    lax.fori_loop(0, INNER // 16, step, 0)


def correlate_bin(first, gated):
    first_re, first_im = first[:INNER], first[INNER:]
    gated_re, gated_im = gated[:INNER], gated[INNER:]
    return jnp.concatenate(
        [
            first_re * gated_re + first_im * gated_im,
            first_re * gated_im - first_im * gated_re,
        ],
        0,
    ).astype(jnp.bfloat16)


def dot32(a, b):
    return jnp.dot(a, b, preferred_element_type=jnp.float32)


def filter_kernel(taps_ref, ahead_ref, spec_ref, rows_ref, z_ref, *, outer, width):
    for a in range(outer // 2):
        piece = taps_ref[:, a * INNER : (a + 1) * INNER].astype(jnp.float32)
        rows_ref[a * INNER : (a + 1) * INNER, :] = piece.T
    outer_ahead(
        lambda a, row, lane: rows_ref[pl.ds(a * INNER + row, 16), lane : lane + 128],
        z_ref, outer, width,
    )

    for k in range(outer // 2 + 1):
        spec_ref[k] = dot32(ahead_ref[k], z_ref[k]).astype(jnp.bfloat16)


def begun(source, target, semaphore):
    copy = pltpu.make_async_copy(source, target, semaphore)
    copy.start()
    return copy


def conv_kernel(
    gated_hbm, filter_hbm, ahead_hbm, back_hbm, conv_ref, spec_hbm,
    gated_ref, filter_ref, ahead_ref, back_ref, spec_ref, z_ref, u_ref, sems, *, outer, width,
):
    gated_in = begun(gated_hbm, gated_ref, sems.at[0])
    ahead_in = begun(ahead_hbm, ahead_ref, sems.at[1])
    filter_in = begun(filter_hbm, filter_ref, sems.at[2])
    back_in = begun(back_hbm, back_ref, sems.at[3])
    gated_in.wait()
    outer_ahead(
        lambda a, row, lane: gated_ref[pl.ds(a * INNER + row, 16), lane : lane + 128],
        z_ref, outer, width,
    )
    ahead_in.wait()
    filter_in.wait()
    for k in range(outer // 2 + 1):
        gated = dot32(ahead_ref[k], z_ref[k])
        spec_ref[k] = gated.astype(jnp.bfloat16)
        z_ref[k] = correlate_bin(filter_ref[k].astype(jnp.float32), gated)
    spec_out = begun(spec_ref, spec_hbm, sems.at[4])
    back_in.wait()
    for k in range(outer // 2 + 1):
        u_ref[k] = dot32(back_ref[k], z_ref[k])

    def store(a, row, lane, value):
        conv_ref[pl.ds(a * INNER + row, 16), lane : lane + 128] = value.astype(jnp.bfloat16)

    outer_back(u_ref, store, outer, width)
    spec_out.wait()


def grad_kernel(
    mixed_hbm, gated_hbm, spec_hbm, ahead_hbm, back_hbm, grad_ref, skip_ref,
    mixed_ref, gated_ref, spec_ref, ahead_ref, back_ref, z_ref, u_ref, rows_ref, sems, *, outer, width,
):
    slabs = outer // 2
    mixed_in = begun(mixed_hbm, mixed_ref, sems.at[0])
    ahead_in = begun(ahead_hbm, ahead_ref, sems.at[1])
    spec_in = begun(spec_hbm, spec_ref, sems.at[2])
    back_in = begun(back_hbm, back_ref, sems.at[3])
    gated_in = begun(gated_hbm, gated_ref, sems.at[4])
    mixed_in.wait()
    outer_ahead(
        lambda a, row, lane: mixed_ref[pl.ds(a * INNER + row, 16), lane : lane + 128],
        z_ref, outer, width,
    )
    ahead_in.wait()
    spec_in.wait()
    for k in range(outer // 2 + 1):
        mixed = dot32(ahead_ref[k], z_ref[k])
        z_ref[k] = correlate_bin(mixed, spec_ref[k].astype(jnp.float32))
    back_in.wait()
    for k in range(outer // 2 + 1):
        u_ref[k] = dot32(back_ref[k], z_ref[k])

    def store(a, row, lane, value):
        rows_ref[pl.ds(a * INNER + row, 16), lane : lane + 128] = value

    outer_back(u_ref, store, outer, width)
    for a in range(slabs):
        grad_ref[:, a * INNER : (a + 1) * INNER] = rows_ref[
            a * INNER : (a + 1) * INNER, :
        ].T.astype(jnp.bfloat16)
    gated_in.wait()

    def add(a, total):
        place = pl.ds(pl.multiple_of(a * INNER, INNER), INNER)
        part = gated_ref[place, :].astype(jnp.float32) * mixed_ref[place, :].astype(jnp.float32)
        return total + jnp.sum(part.reshape(INNER // 8, 8, width), axis=0)

    total = lax.fori_loop(0, slabs, add, jnp.zeros((8, width), jnp.float32))
    skip_ref[...] = jnp.sum(total, axis=0, keepdims=True)


def shifted_down(values, distance, edge):
    moved = pltpu.roll(values, distance, 0)
    row = lax.broadcasted_iota(jnp.int32, values.shape, 0)
    for i in range(distance):
        source = edge.shape[0] - distance + i
        moved = jnp.where(row == i, edge[source : source + 1], moved)
    return moved


def shifted_up(values, distance, edge):
    count = values.shape[0]
    moved = pltpu.roll(values, count - distance, 0)
    row = lax.broadcasted_iota(jnp.int32, values.shape, 0)
    for i in range(distance):
        moved = jnp.where(row == count - distance + i, edge[i : i + 1], moved)
    return moved


def gate_kernel(grad_ref, query_ref, gated_ref, *, width):
    for j in range(gated_ref.shape[0]):
        cols = slice(j * width, (j + 1) * width)
        gated_ref[j] = (
            grad_ref[:, cols].astype(jnp.float32) * query_ref[:, cols].astype(jnp.float32)
        ).astype(jnp.bfloat16)


def mixed_values(key_ref, value_ref, short_ref, cols, edge):
    value = value_ref[:, cols].astype(jnp.float32)
    conv = (
        short_ref[0:1, cols] * value
        + short_ref[1:2, cols] * shifted_down(value, 1, edge)
        + short_ref[2:3, cols] * shifted_down(value, 2, edge)
    )
    return (key_ref[:, cols].astype(jnp.float32) * conv).astype(jnp.bfloat16)


def mix_kernel(key_ref, value_ref, short_ref, grad_ref, conv_ref, mixed_ref, query_grad_ref, *, width):
    zero = jnp.zeros((2, 128), jnp.float32)
    for j in range(mixed_ref.shape[0]):
        for lane in range(0, width, 128):
            cols = slice(j * width + lane, j * width + lane + 128)
            mixed_ref[j, :, lane : lane + 128] = mixed_values(
                key_ref, value_ref, short_ref, cols, zero
            )
            query_grad_ref[:, cols] = (
                grad_ref[:, cols].astype(jnp.float32) * conv_ref[:, cols].astype(jnp.float32)
            ).astype(jnp.bfloat16)


def mix_top_kernel(key_ref, value_ref, short_ref, edge_ref, mixed_in, mixed_ref, *, width):
    for j in range(mixed_ref.shape[0]):
        for lane in range(0, width, 128):
            cols = slice(j * width + lane, j * width + lane + 128)
            edge = edge_ref[:, cols].astype(jnp.float32)
            mixed_ref[j, :, lane : lane + 128] = mixed_values(
                key_ref, value_ref, short_ref, cols, edge
            )


def sums_kernel(
    back_ref, gated_ref, key_ref, value_ref, edge_ref, skip_ref, head_ref, tail_ref, *part_refs, width
):
    rows = key_ref.shape[0]
    first = pl.program_id(0) * (back_ref.shape[0] // INNER_PEERS)
    own = lax.axis_index("ctx") // INNER_PEERS
    for j in range(back_ref.shape[0]):
        distance = (first + j // INNER_PEERS) ^ own
        for lane in range(0, width, 128):
            cols = slice(j * width + lane, j * width + lane + 128)
            lanes = slice(lane, lane + 128)
            value = value_ref[:, cols].astype(jnp.float32)
            edge = edge_ref[:, cols].astype(jnp.float32)
            mixed_grad = back_ref[j, :, lanes].astype(jnp.float32) + skip_ref[:, cols] * gated_ref[
                j, :, lanes
            ].astype(jnp.float32)
            feature = (mixed_grad * key_ref[:, cols].astype(jnp.float32)).astype(jnp.bfloat16)
            head_ref[:, cols] = feature[:2]
            tail_ref[:, cols] = feature[rows - 16 :]
            feature = feature.astype(jnp.float32)
            shifted = (value, shifted_down(value, 1, edge), shifted_down(value, 2, edge))
            sums = jnp.concatenate(
                [jnp.sum(feature * other, axis=0, keepdims=True) for other in shifted]
                + [jnp.zeros((5, 128), jnp.float32)],
                0,
            )
            for d, part_ref in enumerate(part_refs):

                @pl.when(distance == d)
                def _(part_ref=part_ref, sums=sums):
                    part_ref[j % INNER_PEERS, :, lanes] = sums


def finish_kernel(
    back_ref, gated_ref, key_ref, value_ref, edge_ref, short_ref, skip_ref, key_grad_ref,
    value_grad_ref, *, width,
):
    for j in range(back_ref.shape[0]):
        for lane in range(0, width, 128):
            cols = slice(j * width + lane, j * width + lane + 128)
            lanes = slice(lane, lane + 128)
            value = value_ref[:, cols].astype(jnp.float32)
            edge = edge_ref[:, cols].astype(jnp.float32)
            short = [short_ref[i : i + 1, cols] for i in range(3)]
            conv = (
                short[0] * value
                + short[1] * shifted_down(value, 1, edge)
                + short[2] * shifted_down(value, 2, edge)
            )
            mixed_grad = back_ref[j, :, lanes].astype(jnp.float32) + skip_ref[:, cols] * gated_ref[
                j, :, lanes
            ].astype(jnp.float32)
            key_grad_ref[:, cols] = (mixed_grad * conv).astype(jnp.bfloat16)
            feature = (mixed_grad * key_ref[:, cols].astype(jnp.float32)).astype(jnp.bfloat16)
            feature = feature.astype(jnp.float32)
            zero = jnp.zeros((2, 128), jnp.float32)
            value_grad_ref[:, cols] = (
                short[0] * feature
                + short[1] * shifted_up(feature, 1, zero)
                + short[2] * shifted_up(feature, 2, zero)
            ).astype(jnp.bfloat16)


def seam_kernel(tail_ref, head_ref, short_ref, done_ref, value_grad_ref):
    feature = tail_ref[...].astype(jnp.float32)
    head = head_ref[...].astype(jnp.float32)
    value_grad_ref[...] = (
        short_ref[0:1] * feature
        + short_ref[1:2] * shifted_up(feature, 1, head)
        + short_ref[2:3] * shifted_up(feature, 2, head)
    ).astype(jnp.bfloat16)


def exchanged(block):
    return lax.all_to_all(block, "ctx", split_axis=0, concat_axis=0, tiled=True)


def paired(block, distance):
    return lax.ppermute(block, "ctx", [(i, i ^ distance) for i in range(lax.axis_size("ctx"))])


def summed_at_owner(parts, *beside):
    place = lax.axis_index("ctx") % INNER_PEERS
    rows = parts[0]
    for distance in range(1, len(parts)):
        rows = rows + paired(parts[distance], distance * INNER_PEERS)
    rows, *beside = lax.optimization_barrier((rows, *beside))
    total = lax.dynamic_index_in_dim(rows, place, 0, keepdims=False)
    for distance in range(1, INNER_PEERS):
        other = lax.dynamic_index_in_dim(rows, place ^ distance, 0, keepdims=False)
        total = total + paired(other, distance)
    return total, *beside


def after(value, *others):
    return lax.optimization_barrier((value,) + others)[0]


def params(mib=63):
    return pltpu.CompilerParams(vmem_limit_bytes=mib * 1024 * 1024)


def cost(flops, size):
    return pl.CostEstimate(flops=flops, bytes_accessed=size, transcendentals=0)


def kernel_plan(
    query_feat, key_feat, value_raw, conv_out, out_grad, filter_taps, short_filter, skip_gain
):
    rows, channels = query_feat.shape
    peers = lax.axis_size("ctx")
    width = channels // peers
    seq = rows * peers
    outer = 2 * seq // INNER
    bins = outer // 2 + 1
    steps = 2
    group = peers // steps
    span = group * width
    far = peers // INNER_PEERS
    hbm = pl.BlockSpec(memory_space=pl.ANY)
    bf16, f32 = jnp.bfloat16, jnp.float32
    shape = jax.ShapeDtypeStruct
    skip_row = skip_gain.reshape(1, channels)
    ahead, back = (jnp.asarray(t) for t in spectrum_tables(outer))

    flat = pl.BlockSpec((rows, span), lambda i: (0, i))
    owned = pl.BlockSpec((group, rows, width), lambda i: (i, 0, 0))
    edge_spec = pl.BlockSpec((2, span), lambda i: (0, i))
    tail_spec = pl.BlockSpec((16, span), lambda i: (0, i))
    short_spec = pl.BlockSpec((3, span), lambda i: (0, i))
    skip_spec = pl.BlockSpec((1, span), lambda i: (0, i))

    gated = pl.pallas_call(
        functools.partial(gate_kernel, width=width),
        grid=(steps,),
        in_specs=[flat, flat],
        out_specs=owned,
        out_shape=shape((peers, rows, width), bf16),
        compiler_params=params(),
        cost_estimate=cost(rows * channels, 6 * rows * channels),
        name="gate",
    )(out_grad, query_feat)

    gated_got = exchanged(gated.reshape(seq, width))

    spec_shape = shape((bins, 2 * INNER, width), bf16)
    z_scratch = pltpu.VMEM((bins, 2 * INNER, width), bf16)
    u_scratch = pltpu.VMEM((bins, 2 * INNER, width), f32)
    table_scratch = pltpu.VMEM((bins, 2 * INNER, 2 * INNER), bf16)
    table_bytes = 8 * bins * INNER * INNER
    spec_bytes = 4 * bins * INNER * width
    work = 2 * bins * (2 * INNER) ** 2 * width
    filter_spec = pl.pallas_call(
        functools.partial(filter_kernel, outer=outer, width=width),
        out_shape=spec_shape,
        scratch_shapes=[pltpu.VMEM((seq, width), f32), z_scratch],
        compiler_params=params(),
        cost_estimate=cost(work, table_bytes + spec_bytes + 2 * seq * width),
        name="filter_spectrum",
    )(filter_taps, ahead)

    whole = lambda size: pl.BlockSpec((size, channels), lambda i: (0, 0))
    mixed, query_grad = pl.pallas_call(
        functools.partial(mix_kernel, width=width),
        grid=(steps,),
        in_specs=[flat, flat, short_spec, flat, flat],
        out_specs=[owned, flat],
        out_shape=[shape((peers, rows, width), bf16), shape((rows, channels), bf16)],
        compiler_params=params(),
        cost_estimate=cost(10 * rows * channels, 12 * rows * channels),
        name="mix",
    )(key_feat, value_raw, short_filter, out_grad, conv_out)
    filter_spec, mixed = lax.optimization_barrier((filter_spec, mixed))
    edge = passed_along(value_raw[rows - 2 :], "ctx", 1)

    conv_back, gated_spec = pl.pallas_call(
        functools.partial(conv_kernel, outer=outer, width=width),
        in_specs=[hbm] * 4,
        out_specs=[pl.BlockSpec(memory_space=pltpu.VMEM), hbm],
        out_shape=(shape((seq, width), bf16), spec_shape),
        scratch_shapes=[pltpu.VMEM((seq, width), bf16), z_scratch, table_scratch, table_scratch, z_scratch]
        + [z_scratch, u_scratch, pltpu.SemaphoreType.DMA((5,))],
        compiler_params=params(),
        cost_estimate=cost(2 * work, 2 * table_bytes + 2 * spec_bytes + 4 * seq * width),
        name="conv_back",
    )(gated_got, filter_spec, ahead, back)

    conv_back, edge = lax.optimization_barrier((conv_back, edge))
    back_got = exchanged(conv_back).reshape(peers, rows, width)
    mixed = pl.pallas_call(
        functools.partial(mix_top_kernel, width=width),
        grid=(1,),
        in_specs=[whole(16), whole(16), whole(3), whole(2), hbm],
        out_specs=pl.BlockSpec((peers, 16, width), lambda i: (0, 0, 0)),
        out_shape=shape((peers, rows, width), bf16),
        input_output_aliases={4: 0},
        compiler_params=params(),
        cost_estimate=cost(10 * 16 * channels, 10 * 16 * channels),
        name="mix_top",
    )(key_feat, value_raw, short_filter, edge, mixed)
    mixed_got = exchanged(after(mixed, back_got).reshape(seq, width))

    head, tail, *short_parts = pl.pallas_call(
        functools.partial(sums_kernel, width=width),
        grid=(steps,),
        in_specs=[owned, owned, flat, flat, edge_spec, skip_spec],
        out_specs=[edge_spec, tail_spec]
        + [pl.BlockSpec((INNER_PEERS, 8, width), lambda i: (0, 0, 0))] * far,
        out_shape=[shape((2, channels), bf16), shape((16, channels), bf16)]
        + [shape((INNER_PEERS, 8, width), f32)] * far,
        compiler_params=params(),
        cost_estimate=cost(20 * rows * channels, 8 * rows * channels),
        name="sums",
    )(back_got, gated, key_feat, value_raw, edge, skip_row)

    key_grad, value_grad = pl.pallas_call(
        functools.partial(finish_kernel, width=width),
        grid=(steps,),
        in_specs=[owned, owned, flat, flat, edge_spec, short_spec, skip_spec],
        out_specs=[flat, flat],
        out_shape=[shape((rows, channels), bf16)] * 2,
        compiler_params=params(),
        cost_estimate=cost(30 * rows * channels, 12 * rows * channels),
        name="finish",
    )(back_got, gated, key_feat, value_raw, edge, short_filter, skip_row)

    head_got = passed_along(head, "ctx", -1)
    value_grad = pl.pallas_call(
        seam_kernel,
        grid=(1,),
        in_specs=[whole(16), whole(2), whole(3), hbm],
        out_specs=pl.BlockSpec((16, channels), lambda i: (rows // 16 - 1, 0)),
        out_shape=shape((rows, channels), bf16),
        input_output_aliases={3: 0},
        compiler_params=params(),
        cost_estimate=cost(5 * 16 * channels, 6 * 16 * channels),
        name="seam",
    )(tail, head_got, short_filter, value_grad)
    short_grad, value_grad, mixed_got = summed_at_owner(short_parts, value_grad, mixed_got)
    filter_grad, skip_grad = pl.pallas_call(
        functools.partial(grad_kernel, outer=outer, width=width),
        in_specs=[hbm] * 5,
        out_shape=[shape((width, seq), bf16), shape((1, width), f32)],
        scratch_shapes=[pltpu.VMEM((seq, width), bf16)] * 2
        + [z_scratch, table_scratch, table_scratch, z_scratch, u_scratch]
        + [pltpu.VMEM((seq, width), f32), pltpu.SemaphoreType.DMA((5,))],
        compiler_params=params(),
        cost_estimate=cost(2 * work, 2 * table_bytes + spec_bytes),
        name="filter_grad",
    )(mixed_got, gated_got, gated_spec, ahead, back)
    return query_grad, key_grad, value_grad, filter_grad, skip_grad.reshape(width), short_grad[:3]


def per_device(query_feat, key_feat, value_raw, conv_out, out_grad, filter_taps, short_filter, skip_gain):
    rows, channels = query_feat.shape
    peers = lax.axis_size("ctx")
    width = channels // peers
    fits = (
        peers % INNER_PEERS == 0
        and peers & (peers - 1) == 0
        and rows == INNER
        and width % 256 == 0
        and peers in (8, 16)
    )
    plan = kernel_plan if fits else general_plan
    return plan(query_feat, key_feat, value_raw, conv_out, out_grad, filter_taps, short_filter, skip_gain)


def solution(mesh):
    in_specs = (
        P(("groups", "ctx"), None),
        P(("groups", "ctx"), None),
        P(("groups", "ctx"), None),
        P(("groups", "ctx"), None),
        P(("groups", "ctx"), None),
        P("ctx", None),
        P(),
        P(),
    )
    out_specs = (
        P(("groups", "ctx"), None),
        P(("groups", "ctx"), None),
        P(("groups", "ctx"), None),
        P(("groups", "ctx"), None),
        P(("groups", "ctx")),
        P(None, ("groups", "ctx")),
    )
    return jax.shard_map(
        per_device, mesh=mesh, in_specs=in_specs, out_specs=out_specs, check_vma=False
    )
```

```python
import functools
import math

import jax
import jax.numpy as jnp
import numpy as np
from jax import lax
from jax.experimental import pallas as pl
from jax.experimental.pallas import tpu as pltpu
from jax.sharding import PartitionSpec as P

PRECISE = lax.Precision.HIGH


def passed_along(block, axis, distance):
    devices = range(lax.axis_size(axis))
    route = [(i - distance, i) for i in devices if i - distance in devices]
    return lax.ppermute(block, axis, route)


def dft_pair(row_count, col_count, period):
    row_index = lax.iota(jnp.int32, row_count)[:, None]
    col_index = lax.iota(jnp.int32, col_count)[None, :]
    phase = (row_index * col_index % period).astype(jnp.float32) * (-2.0 * math.pi / period)
    return (jnp.cos(phase), jnp.sin(phase))


def make_tables(inner, outer):
    half = outer // 2
    outer_cos, outer_sin = dft_pair(outer, half, outer)
    twist_cos, twist_sin = dft_pair(outer, inner, outer * inner)
    inner_cos, inner_sin = dft_pair(inner, inner, inner)
    real_outer = jnp.stack([outer_cos, outer_sin], 1)
    complex_outer = jnp.stack(
        [jnp.stack([outer_cos, -outer_sin], 1), jnp.stack([outer_sin, outer_cos], 1)], 1
    )
    inner_ahead = jnp.block([[inner_cos, inner_sin], [-inner_sin, inner_cos]])
    inner_back = jnp.block([[inner_cos, -inner_sin], [inner_sin, inner_cos]])
    outer_back = jnp.stack(
        [jnp.stack([outer_cos, outer_sin], 0), jnp.stack([-outer_sin, outer_cos], 0)], 0
    )
    return (real_outer, complex_outer, twist_cos, twist_sin, inner_ahead, inner_back, outer_back)


def twist_ahead(values, twist_cos, twist_sin):
    real_part = values[:, :, 0]
    imag_part = values[:, :, 1]
    return jnp.stack(
        [
            real_part * twist_cos - imag_part * twist_sin,
            real_part * twist_sin + imag_part * twist_cos,
        ],
        2,
    )


def twist_back(values, twist_cos, twist_sin):
    real_part = values[:, :, 0]
    imag_part = values[:, :, 1]
    return jnp.stack(
        [
            real_part * twist_cos + imag_part * twist_sin,
            imag_part * twist_cos - real_part * twist_sin,
        ],
        2,
    )


def inner_section(values, table):
    width, outer = (values.shape[0], values.shape[1])
    flat = values.reshape(width, outer, table.shape[0])
    return jnp.einsum(
        "wkc,cd->wkd", flat, table, precision=PRECISE, preferred_element_type=jnp.float32
    )


def real_spectrum(signal, tables):
    real_outer, complex_outer, twist_cos, twist_sin, inner_ahead, inner_back, outer_back = tables
    half = real_outer.shape[2]
    inner = twist_cos.shape[1]
    blocked = signal.reshape(signal.shape[0], half, inner)
    first = jnp.einsum(
        "wab,kra->wkrb", blocked, real_outer, precision=PRECISE, preferred_element_type=jnp.float32
    )
    return inner_section(twist_ahead(first, twist_cos, twist_sin), inner_ahead)


def complex_spectrum(signal_re, signal_im, tables):
    real_outer, complex_outer, twist_cos, twist_sin, inner_ahead, inner_back, outer_back = tables
    half = real_outer.shape[2]
    inner = twist_cos.shape[1]
    width = signal_re.shape[0]
    stacked = jnp.stack(
        [signal_re.reshape(width, half, inner), signal_im.reshape(width, half, inner)], 1
    )
    first = jnp.einsum(
        "wsab,krsa->wkrb",
        stacked,
        complex_outer,
        precision=PRECISE,
        preferred_element_type=jnp.float32,
    )
    return inner_section(twist_ahead(first, twist_cos, twist_sin), inner_ahead)


def inverse_spectrum(packed, tables):
    real_outer, complex_outer, twist_cos, twist_sin, inner_ahead, inner_back, outer_back = tables
    outer = twist_cos.shape[0]
    inner = twist_cos.shape[1]
    half = real_outer.shape[2]
    width = packed.shape[0]
    back = inner_section(packed, inner_back).reshape(width, outer, 2, inner)
    turned = twist_back(back, twist_cos, twist_sin)
    result = jnp.einsum(
        "wksb,rska->wrab", turned, outer_back, precision=PRECISE, preferred_element_type=jnp.float32
    )
    scale = 1.0 / (outer * inner)
    return (
        (result[:, 0] * scale).reshape(width, half * inner),
        (result[:, 1] * scale).reshape(width, half * inner),
    )


def spectral_block(gated_rows, mixed_rows, filter_rows, tables):
    inner = tables[2].shape[1]
    gated_spec = real_spectrum(gated_rows.astype(jnp.float32), tables)
    joint_spec = complex_spectrum(
        filter_rows.astype(jnp.float32), -mixed_rows.astype(jnp.float32), tables
    )
    gated_re = gated_spec[:, :, :inner]
    gated_im = gated_spec[:, :, inner:]
    joint_re = joint_spec[:, :, :inner]
    joint_im = joint_spec[:, :, inner:]
    product_re = joint_re * gated_re + joint_im * gated_im
    product_im = joint_re * gated_im - joint_im * gated_re
    product = jnp.concatenate([product_re, product_im], 2)
    result_re, result_im = inverse_spectrum(product, tables)
    return (result_re.astype(jnp.bfloat16), result_im.astype(jnp.bfloat16))


def general_plan(
    query_feat, key_feat, value_raw, conv_out, out_grad, filter_taps, short_filter, skip_gain
):
    rows = query_feat.shape[0]
    peers = lax.axis_size("ctx")
    before = passed_along(value_raw[rows - 2 :], "ctx", 1)
    padded = jnp.concatenate([before, value_raw], 0).astype(jnp.float32)
    value_conv = (
        short_filter[0] * padded[2:]
        + short_filter[1] * padded[1:-1]
        + short_filter[2] * padded[:-2]
    )
    mixed = (key_feat.astype(jnp.float32) * value_conv).astype(jnp.bfloat16)
    gated = (out_grad.astype(jnp.float32) * query_feat.astype(jnp.float32)).astype(jnp.bfloat16)
    query_grad = (out_grad.astype(jnp.float32) * conv_out.astype(jnp.float32)).astype(jnp.bfloat16)
    skip_part = jnp.sum(gated.astype(jnp.float32) * mixed.astype(jnp.float32), axis=0)
    tables = make_tables(rows, 2 * peers)
    gated_chan = gated.T
    mixed_chan = mixed.T
    sent_gated, sent_mixed = (
        lax.all_to_all(gated_chan, "ctx", split_axis=0, concat_axis=1, tiled=True),
        lax.all_to_all(mixed_chan, "ctx", split_axis=0, concat_axis=1, tiled=True),
    )
    back_rows, filter_grad = spectral_block(sent_gated, sent_mixed, filter_taps, tables)
    back_chan = lax.all_to_all(back_rows, "ctx", split_axis=1, concat_axis=0, tiled=True)
    conv_back = back_chan.T
    mixed_grad = conv_back.astype(jnp.float32) + skip_gain * gated.astype(jnp.float32)
    key_grad = (mixed_grad * value_conv).astype(jnp.bfloat16)
    feature_grad = (mixed_grad * key_feat.astype(jnp.float32)).astype(jnp.bfloat16)
    after = passed_along(feature_grad[:2], "ctx", -1)
    extended = jnp.concatenate([feature_grad, after], 0).astype(jnp.float32)
    value_grad = (
        short_filter[0] * extended[:-2]
        + short_filter[1] * extended[1:-1]
        + short_filter[2] * extended[2:]
    ).astype(jnp.bfloat16)
    feature_wide = extended[:-2]
    short_part = jnp.stack(
        [
            jnp.sum(feature_wide * padded[2:], axis=0),
            jnp.sum(feature_wide * padded[1:-1], axis=0),
            jnp.sum(feature_wide * padded[:-2], axis=0),
        ]
    )
    skip_grad, short_grad = (
        lax.psum_scatter(skip_part, "ctx", scatter_dimension=0, tiled=True),
        lax.psum_scatter(short_part, "ctx", scatter_dimension=1, tiled=True),
    )
    return (query_grad, key_grad, value_grad, filter_grad, skip_grad, short_grad)


INNER = 128
INNER_PEERS = 4


def half_spectrum(values, length):
    if length == 2:
        return [(values[0], None), (values[0], None)]
    even = half_spectrum(values[0::2], length // 2)
    odd = half_spectrum(values[1::2], length // 2)
    quarter = length // 4
    bins = [None] * (length // 2 + 1)
    bins[0] = (even[0][0] + odd[0][0], None)
    bins[length // 2] = (even[0][0] - odd[0][0], None)
    bins[quarter] = (even[quarter][0], -odd[quarter][0])
    for k in range(1, quarter):
        c = math.cos(2.0 * math.pi * k / length)
        s = math.sin(2.0 * math.pi * k / length)
        odd_re, odd_im = odd[k]
        even_re, even_im = even[k]
        if 2 * k == quarter:
            turn_re = (odd_re + odd_im) * c
            turn_im = (odd_im - odd_re) * c
        else:
            turn_re = odd_re * c + odd_im * s
            turn_im = odd_im * c - odd_re * s
        bins[k] = (even_re + turn_re, even_im + turn_im)
        bins[length // 2 - k] = (even_re - turn_re, turn_im - even_im)
    return bins


def first_half(bins, length):
    if length == 2:
        return [bins[0][0] + bins[1][0]]
    half = length // 2
    quarter = length // 4
    even = [None] * (quarter + 1)
    odd = [None] * (quarter + 1)
    even[0] = (bins[0][0] + bins[half][0], None)
    odd[0] = (bins[0][0] - bins[half][0], None)
    even[quarter] = (2.0 * bins[quarter][0], None)
    odd[quarter] = (-2.0 * bins[quarter][1], None)
    for k in range(1, quarter):
        c = math.cos(2.0 * math.pi * k / length)
        s = math.sin(2.0 * math.pi * k / length)
        near_re, near_im = bins[k]
        far_re, far_im = bins[half - k]
        even[k] = (near_re + far_re, near_im - far_im)
        gap_re = near_re - far_re
        gap_im = near_im + far_im
        if 2 * k == quarter:
            odd[k] = ((gap_re - gap_im) * c, (gap_re + gap_im) * c)
        else:
            odd[k] = (gap_re * c - gap_im * s, gap_re * s + gap_im * c)
    result = [None] * half
    result[0::2] = first_half(even, half)
    result[1::2] = first_half(odd, half)
    return result


def spectrum_tables(outer):
    size = outer * INNER
    near = np.arange(outer // 2 + 1)[:, None, None]
    place = np.arange(INNER)
    angle = -2.0 * np.pi * (
        (near * place[None, None, :]) / size + place[None, :, None] * place[None, None, :] / INNER
    )
    c, s = np.cos(angle), np.sin(angle)
    ahead = np.concatenate(
        [np.concatenate([c, -s], 2), np.concatenate([s, c], 2)], 1
    )
    back = np.swapaxes(ahead, 1, 2) / size
    return ahead.astype(jnp.bfloat16), back.astype(jnp.bfloat16)


def outer_ahead(load, z_ref, outer, width):
    def step(chunk, carry):
        row = pl.multiple_of(chunk * 16, 16)
        for lane in range(0, width, 128):
            values = [load(a, row, lane).astype(jnp.float32) for a in range(outer // 2)]
            bins = half_spectrum(values, outer)
            for k, (re, im) in enumerate(bins):
                im = jnp.zeros_like(re) if im is None else im
                z_ref[k, pl.ds(row, 16), lane : lane + 128] = re.astype(jnp.bfloat16)
                z_ref[k, pl.ds(INNER + row, 16), lane : lane + 128] = im.astype(jnp.bfloat16)
        return carry

    lax.fori_loop(0, INNER // 16, step, 0)


def outer_back(u_ref, store, outer, width):
    def step(chunk, carry):
        row = pl.multiple_of(chunk * 16, 16)
        for lane in range(0, width, 128):
            bins = []
            for k in range(outer // 2 + 1):
                re = u_ref[k, pl.ds(row, 16), lane : lane + 128]
                im = u_ref[k, pl.ds(INNER + row, 16), lane : lane + 128]
                bins.append((re, im))
            for a, value in enumerate(first_half(bins, outer)):
                store(a, row, lane, value)
        return carry

    lax.fori_loop(0, INNER // 16, step, 0)


def correlate_bin(first, gated):
    first_re, first_im = first[:INNER], first[INNER:]
    gated_re, gated_im = gated[:INNER], gated[INNER:]
    return jnp.concatenate(
        [
            first_re * gated_re + first_im * gated_im,
            first_re * gated_im - first_im * gated_re,
        ],
        0,
    ).astype(jnp.bfloat16)


def dot32(a, b):
    return jnp.dot(a, b, preferred_element_type=jnp.float32)


def filter_kernel(taps_ref, ahead_ref, spec_ref, rows_ref, z_ref, *, outer, width):
    for a in range(outer // 2):
        piece = taps_ref[:, a * INNER : (a + 1) * INNER].astype(jnp.float32)
        rows_ref[a * INNER : (a + 1) * INNER, :] = piece.T
    outer_ahead(
        lambda a, row, lane: rows_ref[pl.ds(a * INNER + row, 16), lane : lane + 128],
        z_ref, outer, width,
    )

    for k in range(outer // 2 + 1):
        spec_ref[k] = dot32(ahead_ref[k], z_ref[k]).astype(jnp.bfloat16)


def begun(source, target, semaphore):
    copy = pltpu.make_async_copy(source, target, semaphore)
    copy.start()
    return copy


def conv_kernel(
    gated_hbm, filter_hbm, ahead_hbm, back_hbm, conv_ref, spec_hbm,
    gated_ref, filter_ref, ahead_ref, back_ref, spec_ref, z_ref, u_ref, sems, *, outer, width,
):
    gated_in = begun(gated_hbm, gated_ref, sems.at[0])
    ahead_in = begun(ahead_hbm, ahead_ref, sems.at[1])
    filter_in = begun(filter_hbm, filter_ref, sems.at[2])
    back_in = begun(back_hbm, back_ref, sems.at[3])
    gated_in.wait()
    outer_ahead(
        lambda a, row, lane: gated_ref[pl.ds(a * INNER + row, 16), lane : lane + 128],
        z_ref, outer, width,
    )
    ahead_in.wait()
    filter_in.wait()
    for k in range(outer // 2 + 1):
        gated = dot32(ahead_ref[k], z_ref[k])
        spec_ref[k] = gated.astype(jnp.bfloat16)
        z_ref[k] = correlate_bin(filter_ref[k].astype(jnp.float32), gated)
    spec_out = begun(spec_ref, spec_hbm, sems.at[4])
    back_in.wait()
    for k in range(outer // 2 + 1):
        u_ref[k] = dot32(back_ref[k], z_ref[k])

    def store(a, row, lane, value):
        conv_ref[pl.ds(a * INNER + row, 16), lane : lane + 128] = value.astype(jnp.bfloat16)

    outer_back(u_ref, store, outer, width)
    spec_out.wait()


def grad_kernel(*refs, outer, width):
    far = outer // 2 // INNER_PEERS
    place_hbm, refs = refs[:far], refs[far:]
    near_hbm, refs = refs[: INNER_PEERS - 1], refs[INNER_PEERS - 1 :]
    far_hbm, refs = refs[: far - 1], refs[far - 1 :]
    gated_hbm, spec_hbm, ahead_hbm, back_hbm, grad_ref, skip_ref = refs[:6]
    mixed_ref, gated_ref, spec_ref, ahead_ref, back_ref, z_ref, u_ref, rows_ref, sems = refs[6:]
    slabs = outer // 2
    me = lax.axis_index("ctx")
    own_row, own_place = me // INNER_PEERS, me % INNER_PEERS
    mixed_in = []
    for d in range(far):
        for e in range(INNER_PEERS):
            if e == 0:
                source = place_hbm[d]
            elif d == 0:
                source = near_hbm[e - 1].at[own_row]
            else:
                source = far_hbm[d - 1].at[e - 1]
            slab = (own_row ^ d) * INNER_PEERS + (own_place ^ e)
            mixed_in.append(begun(source, mixed_ref.at[slab], sems.at[4 + len(mixed_in)]))
    ahead_in = begun(ahead_hbm, ahead_ref, sems.at[0])
    spec_in = begun(spec_hbm, spec_ref, sems.at[1])
    back_in = begun(back_hbm, back_ref, sems.at[2])
    gated_in = begun(gated_hbm, gated_ref, sems.at[3])
    for copy in mixed_in:
        copy.wait()
    outer_ahead(
        lambda a, row, lane: mixed_ref[a, pl.ds(row, 16), lane : lane + 128],
        z_ref, outer, width,
    )
    ahead_in.wait()
    spec_in.wait()
    for k in range(outer // 2 + 1):
        mixed = dot32(ahead_ref[k], z_ref[k])
        z_ref[k] = correlate_bin(mixed, spec_ref[k].astype(jnp.float32))
    back_in.wait()
    for k in range(outer // 2 + 1):
        u_ref[k] = dot32(back_ref[k], z_ref[k])

    def store(a, row, lane, value):
        rows_ref[pl.ds(a * INNER + row, 16), lane : lane + 128] = value

    outer_back(u_ref, store, outer, width)
    for a in range(slabs):
        grad_ref[:, a * INNER : (a + 1) * INNER] = rows_ref[
            a * INNER : (a + 1) * INNER, :
        ].T.astype(jnp.bfloat16)
    gated_in.wait()

    def add(a, total):
        place = pl.ds(pl.multiple_of(a * INNER, INNER), INNER)
        part = gated_ref[place, :].astype(jnp.float32) * mixed_ref[a].astype(jnp.float32)
        return total + jnp.sum(part.reshape(INNER // 8, 8, width), axis=0)

    total = lax.fori_loop(0, slabs, add, jnp.zeros((8, width), jnp.float32))
    skip_ref[...] = jnp.sum(total, axis=0, keepdims=True)


def regroup_kernel(*refs):
    near, far = refs[: INNER_PEERS - 1], refs[INNER_PEERS - 1 :]
    own_row = lax.axis_index("ctx") // INNER_PEERS
    for d in range(1, len(far) + 1):
        for e in range(1, INNER_PEERS):
            far[d - 1][e - 1] = near[e - 1][own_row ^ d]


def shifted_down(values, distance, edge):
    moved = pltpu.roll(values, distance, 0)
    row = lax.broadcasted_iota(jnp.int32, values.shape, 0)
    for i in range(distance):
        source = edge.shape[0] - distance + i
        moved = jnp.where(row == i, edge[source : source + 1], moved)
    return moved


def shifted_up(values, distance, edge):
    count = values.shape[0]
    moved = pltpu.roll(values, count - distance, 0)
    row = lax.broadcasted_iota(jnp.int32, values.shape, 0)
    for i in range(distance):
        moved = jnp.where(row == count - distance + i, edge[i : i + 1], moved)
    return moved


def gate_kernel(grad_ref, query_ref, gated_ref, *, width):
    for j in range(gated_ref.shape[0]):
        cols = slice(j * width, (j + 1) * width)
        gated_ref[j] = (
            grad_ref[:, cols].astype(jnp.float32) * query_ref[:, cols].astype(jnp.float32)
        ).astype(jnp.bfloat16)


def mix_kernel(key_ref, value_ref, edge_ref, short_ref, grad_ref, conv_ref, *rest, width):
    near_refs, place_refs = rest[: INNER_PEERS - 1], rest[INNER_PEERS - 1 : -3]
    query_grad_ref, behind, mixed_ref = rest[-3:]
    rows = key_ref.shape[0]
    owners = key_ref.shape[1] // width
    step = pl.program_id(0)
    for j in range(owners):
        for lane in range(0, width, 128):
            slot = (j * width + lane) // 128 % 2
            cols = slice(j * width + lane, j * width + lane + 128)
            value = value_ref[:, cols].astype(jnp.float32)
            behind[slot, 6:8] = edge_ref[:, cols].astype(jnp.float32)
            behind[slot, 8 : 8 + rows] = value
            conv = (
                short_ref[0:1, cols] * value
                + short_ref[1:2, cols] * behind[slot, 7 : 7 + rows]
                + short_ref[2:3, cols] * behind[slot, 6 : 6 + rows]
            )
            mixed_ref[step * owners + j, :, lane : lane + 128] = (
                key_ref[:, cols].astype(jnp.float32) * conv
            ).astype(jnp.bfloat16)
            query_grad_ref[:, cols] = (
                grad_ref[:, cols].astype(jnp.float32) * conv_ref[:, cols].astype(jnp.float32)
            ).astype(jnp.bfloat16)

    @pl.when(step == pl.num_programs(0) - 1)
    def _():
        me = lax.axis_index("ctx")
        own_row, place = me // INNER_PEERS, me % INNER_PEERS
        for e, near_ref in enumerate(near_refs, 1):
            for row in range(near_ref.shape[0]):
                near_ref[row] = mixed_ref[row * INNER_PEERS + (place ^ e)]
        for d, place_ref in enumerate(place_refs):
            place_ref[...] = mixed_ref[(own_row ^ d) * INNER_PEERS + place]


def finish_kernel(
    back_ref, gated_ref, key_ref, value_ref, edge_ref, short_ref, skip_ref,
    key_grad_ref, value_grad_ref, head_ref, tail_ref, *rest, width,
):
    part_refs, behind, ahead, sums_ref = rest[:-3], rest[-3], rest[-2], rest[-1]
    rows = key_ref.shape[0]
    owners = back_ref.shape[0]
    step = pl.program_id(0)
    for j in range(owners):
        for lane in range(0, width, 128):
            slot = (j * width + lane) // 128 % 2
            cols = slice(j * width + lane, j * width + lane + 128)
            lanes = slice(lane, lane + 128)
            short = [short_ref[i : i + 1, cols] for i in range(3)]
            value = value_ref[:, cols].astype(jnp.float32)
            behind[slot, 6:8] = edge_ref[:, cols].astype(jnp.float32)
            behind[slot, 8 : 8 + rows] = value
            value_1 = behind[slot, 7 : 7 + rows]
            value_2 = behind[slot, 6 : 6 + rows]
            mixed_grad = back_ref[j, :, lanes].astype(jnp.float32) + skip_ref[:, cols] * gated_ref[
                j, :, lanes
            ].astype(jnp.float32)
            conv = short[0] * value + short[1] * value_1 + short[2] * value_2
            key_grad_ref[:, cols] = (mixed_grad * conv).astype(jnp.bfloat16)
            feature = (mixed_grad * key_ref[:, cols].astype(jnp.float32)).astype(jnp.bfloat16)
            head_ref[:, cols] = feature[:2]
            tail_ref[:, cols] = feature[rows - 16 :]
            feature = feature.astype(jnp.float32)
            ahead[slot, 0:rows] = feature
            ahead[slot, rows : rows + 8] = jnp.zeros((8, 128), jnp.float32)
            value_grad_ref[:, cols] = (
                short[0] * feature
                + short[1] * ahead[slot, 1 : 1 + rows]
                + short[2] * ahead[slot, 2 : 2 + rows]
            ).astype(jnp.bfloat16)
            sums = jnp.concatenate(
                [
                    jnp.sum(feature * other, axis=0, keepdims=True)
                    for other in (value, value_1, value_2)
                ]
                + [jnp.zeros((5, 128), jnp.float32)],
                0,
            )
            sums_ref[step * owners + j, :, lanes] = sums

    @pl.when(step == pl.num_programs(0) - 1)
    def _():
        own = lax.axis_index("ctx") // INNER_PEERS
        for d, part_ref in enumerate(part_refs):
            part_ref[...] = sums_ref[pl.ds((own ^ d) * INNER_PEERS, INNER_PEERS)]


def seam_kernel(tail_ref, head_ref, short_ref, done_ref, value_grad_ref):
    feature = tail_ref[...].astype(jnp.float32)
    head = head_ref[...].astype(jnp.float32)
    value_grad_ref[...] = (
        short_ref[0:1] * feature
        + short_ref[1:2] * shifted_up(feature, 1, head)
        + short_ref[2:3] * shifted_up(feature, 2, head)
    ).astype(jnp.bfloat16)


def exchanged(block):
    return lax.all_to_all(block, "ctx", split_axis=0, concat_axis=0, tiled=True)


def paired(block, distance):
    return lax.ppermute(block, "ctx", [(i, i ^ distance) for i in range(lax.axis_size("ctx"))])


def summed_at_owner(parts, *beside):
    place = lax.axis_index("ctx") % INNER_PEERS
    got = [parts[0]] + [paired(parts[d], d * INNER_PEERS) for d in range(1, len(parts))]
    rows = sum(got[1:], got[0])
    rows, beside = lax.optimization_barrier((rows, beside))
    total = lax.dynamic_index_in_dim(rows, place, 0, keepdims=False)
    for distance in range(1, INNER_PEERS):
        other = lax.dynamic_index_in_dim(rows, place ^ distance, 0, keepdims=False)
        total = total + paired(other, distance)
    return total, *beside


def after(value, *others):
    return lax.optimization_barrier((value,) + others)[0]


def params(mib=63):
    return pltpu.CompilerParams(vmem_limit_bytes=mib * 1024 * 1024)


def cost(flops, size):
    return pl.CostEstimate(flops=flops, bytes_accessed=size, transcendentals=0)


def kernel_plan(
    query_feat, key_feat, value_raw, conv_out, out_grad, filter_taps, short_filter, skip_gain
):
    rows, channels = query_feat.shape
    peers = lax.axis_size("ctx")
    width = channels // peers
    seq = rows * peers
    outer = 2 * seq // INNER
    bins = outer // 2 + 1
    steps = 2
    group = peers // steps
    span = group * width
    far = peers // INNER_PEERS
    any_place = pl.BlockSpec(memory_space=pl.ANY)
    hbm = pl.BlockSpec(memory_space=pltpu.HBM)
    bf16, f32 = jnp.bfloat16, jnp.float32
    shape = jax.ShapeDtypeStruct
    skip_row = skip_gain.reshape(1, channels)
    ahead, back = (jnp.asarray(t) for t in spectrum_tables(outer))

    flat = pl.BlockSpec((rows, span), lambda i: (0, i))
    owned = pl.BlockSpec((group, rows, width), lambda i: (i, 0, 0))
    edge_spec = pl.BlockSpec((2, span), lambda i: (0, i))
    tail_spec = pl.BlockSpec((16, span), lambda i: (0, i))
    short_spec = pl.BlockSpec((3, span), lambda i: (0, i))
    skip_spec = pl.BlockSpec((1, span), lambda i: (0, i))

    gated = pl.pallas_call(
        functools.partial(gate_kernel, width=width),
        grid=(steps,),
        in_specs=[flat, flat],
        out_specs=owned,
        out_shape=shape((peers, rows, width), bf16),
        compiler_params=params(),
        cost_estimate=cost(rows * channels, 6 * rows * channels),
        name="gate",
    )(out_grad, query_feat)

    gated_got = exchanged(gated.reshape(seq, width))

    spec_shape = shape((bins, 2 * INNER, width), bf16)
    z_scratch = pltpu.VMEM((bins, 2 * INNER, width), bf16)
    u_scratch = pltpu.VMEM((bins, 2 * INNER, width), f32)
    table_scratch = pltpu.VMEM((bins, 2 * INNER, 2 * INNER), bf16)
    table_bytes = 8 * bins * INNER * INNER
    spec_bytes = 4 * bins * INNER * width
    work = 2 * bins * (2 * INNER) ** 2 * width
    edge = passed_along(value_raw[rows - 2 :], "ctx", 1)
    whole = lambda size: pl.BlockSpec((size, channels), lambda i: (0, 0))
    shift_scratch = pltpu.VMEM((2, rows + 8, 128), f32)
    near_spec = pl.BlockSpec((far, rows, width), lambda i: (0, 0, 0))
    far_spec = pl.BlockSpec((INNER_PEERS - 1, rows, width), lambda i: (0, 0, 0))
    place_spec = pl.BlockSpec((rows, width), lambda i: (0, 0))
    *mixed, query_grad = pl.pallas_call(
        functools.partial(mix_kernel, width=width),
        grid=(steps,),
        in_specs=[flat, flat, edge_spec, short_spec, flat, flat],
        out_specs=[near_spec] * (INNER_PEERS - 1) + [place_spec] * far + [flat],
        out_shape=[shape((far, rows, width), bf16)] * (INNER_PEERS - 1)
        + [shape((rows, width), bf16)] * far
        + [shape((rows, channels), bf16)],
        scratch_shapes=[shift_scratch, pltpu.VMEM((peers, rows, width), bf16)],
        compiler_params=params(),
        cost_estimate=cost(40000000000, 12 * rows * channels),
        name="mix",
    )(key_feat, value_raw, edge, short_filter, out_grad, conv_out)
    near = [paired(mixed[e - 1], e) for e in range(1, INNER_PEERS)]
    placed = mixed[INNER_PEERS - 1 :]

    placed = [placed[0]] + [paired(placed[d], d * INNER_PEERS) for d in range(1, far)]
    across = pl.pallas_call(
        regroup_kernel,
        grid=(1,),
        in_specs=[near_spec] * (INNER_PEERS - 1),
        out_specs=[far_spec] * (far - 1),
        out_shape=[shape((INNER_PEERS - 1, rows, width), bf16)] * (far - 1),
        compiler_params=params(),
        cost_estimate=cost(0, 4 * seq * width),
        name="regroup",
    )(*near)
    filter_taps, query_grad = lax.optimization_barrier((filter_taps, query_grad))
    filter_spec = pl.pallas_call(
        functools.partial(filter_kernel, outer=outer, width=width),
        out_shape=spec_shape,
        scratch_shapes=[pltpu.VMEM((seq, width), f32), z_scratch],
        compiler_params=params(),
        cost_estimate=cost(40000000000, table_bytes + spec_bytes + 2 * seq * width),
        name="filter_spectrum",
    )(filter_taps, ahead)


    *across, gated_got = lax.optimization_barrier((*across, gated_got))
    across = [paired(across[d - 1], d * INNER_PEERS) for d in range(1, far)]

    conv_back, gated_spec = pl.pallas_call(
        functools.partial(conv_kernel, outer=outer, width=width),
        in_specs=[hbm] * 4,
        out_specs=[pl.BlockSpec(memory_space=pltpu.VMEM), hbm],
        out_shape=(shape((seq, width), bf16), spec_shape),
        scratch_shapes=[pltpu.VMEM((seq, width), bf16), z_scratch, table_scratch, table_scratch, z_scratch]
        + [z_scratch, u_scratch, pltpu.SemaphoreType.DMA((5,))],
        compiler_params=params(),
        cost_estimate=cost(40000000000, 2 * table_bytes + 2 * spec_bytes + 4 * seq * width),
        name="conv_back",
    )(gated_got, filter_spec, ahead, back)

    back_got = exchanged(conv_back).reshape(peers, rows, width)


    filter_grad, skip_grad = pl.pallas_call(
        functools.partial(grad_kernel, outer=outer, width=width),
        in_specs=[hbm] * (INNER_PEERS + 2 * far + 2),
        out_shape=[shape((width, seq), bf16), shape((1, width), f32)],
        scratch_shapes=[
            pltpu.VMEM((peers, rows, width), bf16),
            pltpu.VMEM((seq, width), bf16),
            z_scratch,
            table_scratch,
            table_scratch,
            z_scratch,
            u_scratch,
            pltpu.VMEM((seq, width), f32),
            pltpu.SemaphoreType.DMA((peers + 4,)),
        ],
        compiler_params=params(),
        cost_estimate=cost(100000000000, 2 * table_bytes + spec_bytes),
        name="filter_grad",
    )(*placed, *near, *across, gated_got, gated_spec, ahead, back)
    back_got, filter_grad, skip_grad = lax.optimization_barrier((back_got, filter_grad, skip_grad))

    key_grad, value_grad, head, tail, *short_parts = pl.pallas_call(
        functools.partial(finish_kernel, width=width),
        grid=(steps,),
        in_specs=[owned, owned, flat, flat, edge_spec, short_spec, skip_spec],
        out_specs=[flat, flat, edge_spec, tail_spec]
        + [pl.BlockSpec((INNER_PEERS, 8, width), lambda i: (0, 0, 0))] * far,
        out_shape=[shape((rows, channels), bf16)] * 2
        + [shape((2, channels), bf16), shape((16, channels), bf16)]
        + [shape((INNER_PEERS, 8, width), f32)] * far,
        scratch_shapes=[pltpu.VMEM((2, rows + 8, 128), f32)] * 2 + [pltpu.VMEM((peers, 8, width), f32)],
        compiler_params=params(),
        cost_estimate=cost(30 * rows * channels, 12 * rows * channels),
        name="finish",
    )(back_got, gated, key_feat, value_raw, edge, short_filter, skip_row)

    head_got = passed_along(head, "ctx", -1)
    short_grad, head_got, value_grad = summed_at_owner(short_parts, head_got, value_grad)
    value_grad = pl.pallas_call(
        seam_kernel,
        grid=(1,),
        in_specs=[whole(16), whole(2), whole(3), hbm],
        out_specs=pl.BlockSpec((16, channels), lambda i: (rows // 16 - 1, 0)),
        out_shape=shape((rows, channels), bf16),
        input_output_aliases={3: 0},
        compiler_params=params(),
        cost_estimate=cost(5 * 16 * channels, 6 * 16 * channels),
        name="seam",
    )(tail, head_got, short_filter, value_grad)
    return query_grad, key_grad, value_grad, filter_grad, skip_grad.reshape(width), short_grad[:3]


def per_device(query_feat, key_feat, value_raw, conv_out, out_grad, filter_taps, short_filter, skip_gain):
    rows, channels = query_feat.shape
    peers = lax.axis_size("ctx")
    width = channels // peers
    fits = (
        peers % INNER_PEERS == 0
        and peers & (peers - 1) == 0
        and rows == INNER
        and width % 256 == 0
        and peers in (8, 16)
    )
    plan = kernel_plan if fits else general_plan
    return plan(query_feat, key_feat, value_raw, conv_out, out_grad, filter_taps, short_filter, skip_gain)


def solution(mesh):
    in_specs = (
        P(("groups", "ctx"), None),
        P(("groups", "ctx"), None),
        P(("groups", "ctx"), None),
        P(("groups", "ctx"), None),
        P(("groups", "ctx"), None),
        P("ctx", None),
        P(),
        P(),
    )
    out_specs = (
        P(("groups", "ctx"), None),
        P(("groups", "ctx"), None),
        P(("groups", "ctx"), None),
        P(("groups", "ctx"), None),
        P(("groups", "ctx")),
        P(None, ("groups", "ctx")),
    )
    return jax.shard_map(
        per_device, mesh=mesh, in_specs=in_specs, out_specs=out_specs, check_vma=False
    )
```

```python
import functools
import math

import jax
import jax.numpy as jnp
import numpy as np
from jax import lax
from jax.experimental import pallas as pl
from jax.experimental.pallas import tpu as pltpu
from jax.sharding import PartitionSpec as P

PRECISE = lax.Precision.HIGH


def passed_along(block, axis, distance):
    devices = range(lax.axis_size(axis))
    route = [(i - distance, i) for i in devices if i - distance in devices]
    return lax.ppermute(block, axis, route)


def dft_pair(row_count, col_count, period):
    row_index = lax.iota(jnp.int32, row_count)[:, None]
    col_index = lax.iota(jnp.int32, col_count)[None, :]
    phase = (row_index * col_index % period).astype(jnp.float32) * (-2.0 * math.pi / period)
    return (jnp.cos(phase), jnp.sin(phase))


def make_tables(inner, outer):
    half = outer // 2
    outer_cos, outer_sin = dft_pair(outer, half, outer)
    twist_cos, twist_sin = dft_pair(outer, inner, outer * inner)
    inner_cos, inner_sin = dft_pair(inner, inner, inner)
    real_outer = jnp.stack([outer_cos, outer_sin], 1)
    complex_outer = jnp.stack(
        [jnp.stack([outer_cos, -outer_sin], 1), jnp.stack([outer_sin, outer_cos], 1)], 1
    )
    inner_ahead = jnp.block([[inner_cos, inner_sin], [-inner_sin, inner_cos]])
    inner_back = jnp.block([[inner_cos, -inner_sin], [inner_sin, inner_cos]])
    outer_back = jnp.stack(
        [jnp.stack([outer_cos, outer_sin], 0), jnp.stack([-outer_sin, outer_cos], 0)], 0
    )
    return (real_outer, complex_outer, twist_cos, twist_sin, inner_ahead, inner_back, outer_back)


def twist_ahead(values, twist_cos, twist_sin):
    real_part = values[:, :, 0]
    imag_part = values[:, :, 1]
    return jnp.stack(
        [
            real_part * twist_cos - imag_part * twist_sin,
            real_part * twist_sin + imag_part * twist_cos,
        ],
        2,
    )


def twist_back(values, twist_cos, twist_sin):
    real_part = values[:, :, 0]
    imag_part = values[:, :, 1]
    return jnp.stack(
        [
            real_part * twist_cos + imag_part * twist_sin,
            imag_part * twist_cos - real_part * twist_sin,
        ],
        2,
    )


def inner_section(values, table):
    width, outer = (values.shape[0], values.shape[1])
    flat = values.reshape(width, outer, table.shape[0])
    return jnp.einsum(
        "wkc,cd->wkd", flat, table, precision=PRECISE, preferred_element_type=jnp.float32
    )


def real_spectrum(signal, tables):
    real_outer, complex_outer, twist_cos, twist_sin, inner_ahead, inner_back, outer_back = tables
    half = real_outer.shape[2]
    inner = twist_cos.shape[1]
    blocked = signal.reshape(signal.shape[0], half, inner)
    first = jnp.einsum(
        "wab,kra->wkrb", blocked, real_outer, precision=PRECISE, preferred_element_type=jnp.float32
    )
    return inner_section(twist_ahead(first, twist_cos, twist_sin), inner_ahead)


def complex_spectrum(signal_re, signal_im, tables):
    real_outer, complex_outer, twist_cos, twist_sin, inner_ahead, inner_back, outer_back = tables
    half = real_outer.shape[2]
    inner = twist_cos.shape[1]
    width = signal_re.shape[0]
    stacked = jnp.stack(
        [signal_re.reshape(width, half, inner), signal_im.reshape(width, half, inner)], 1
    )
    first = jnp.einsum(
        "wsab,krsa->wkrb",
        stacked,
        complex_outer,
        precision=PRECISE,
        preferred_element_type=jnp.float32,
    )
    return inner_section(twist_ahead(first, twist_cos, twist_sin), inner_ahead)


def inverse_spectrum(packed, tables):
    real_outer, complex_outer, twist_cos, twist_sin, inner_ahead, inner_back, outer_back = tables
    outer = twist_cos.shape[0]
    inner = twist_cos.shape[1]
    half = real_outer.shape[2]
    width = packed.shape[0]
    back = inner_section(packed, inner_back).reshape(width, outer, 2, inner)
    turned = twist_back(back, twist_cos, twist_sin)
    result = jnp.einsum(
        "wksb,rska->wrab", turned, outer_back, precision=PRECISE, preferred_element_type=jnp.float32
    )
    scale = 1.0 / (outer * inner)
    return (
        (result[:, 0] * scale).reshape(width, half * inner),
        (result[:, 1] * scale).reshape(width, half * inner),
    )


def spectral_block(gated_rows, mixed_rows, filter_rows, tables):
    inner = tables[2].shape[1]
    gated_spec = real_spectrum(gated_rows.astype(jnp.float32), tables)
    joint_spec = complex_spectrum(
        filter_rows.astype(jnp.float32), -mixed_rows.astype(jnp.float32), tables
    )
    gated_re = gated_spec[:, :, :inner]
    gated_im = gated_spec[:, :, inner:]
    joint_re = joint_spec[:, :, :inner]
    joint_im = joint_spec[:, :, inner:]
    product_re = joint_re * gated_re + joint_im * gated_im
    product_im = joint_re * gated_im - joint_im * gated_re
    product = jnp.concatenate([product_re, product_im], 2)
    result_re, result_im = inverse_spectrum(product, tables)
    return (result_re.astype(jnp.bfloat16), result_im.astype(jnp.bfloat16))


def general_plan(
    query_feat, key_feat, value_raw, conv_out, out_grad, filter_taps, short_filter, skip_gain
):
    rows = query_feat.shape[0]
    peers = lax.axis_size("ctx")
    before = passed_along(value_raw[rows - 2 :], "ctx", 1)
    padded = jnp.concatenate([before, value_raw], 0).astype(jnp.float32)
    value_conv = (
        short_filter[0] * padded[2:]
        + short_filter[1] * padded[1:-1]
        + short_filter[2] * padded[:-2]
    )
    mixed = (key_feat.astype(jnp.float32) * value_conv).astype(jnp.bfloat16)
    gated = (out_grad.astype(jnp.float32) * query_feat.astype(jnp.float32)).astype(jnp.bfloat16)
    query_grad = (out_grad.astype(jnp.float32) * conv_out.astype(jnp.float32)).astype(jnp.bfloat16)
    skip_part = jnp.sum(gated.astype(jnp.float32) * mixed.astype(jnp.float32), axis=0)
    tables = make_tables(rows, 2 * peers)
    gated_chan = gated.T
    mixed_chan = mixed.T
    sent_gated, sent_mixed = (
        lax.all_to_all(gated_chan, "ctx", split_axis=0, concat_axis=1, tiled=True),
        lax.all_to_all(mixed_chan, "ctx", split_axis=0, concat_axis=1, tiled=True),
    )
    back_rows, filter_grad = spectral_block(sent_gated, sent_mixed, filter_taps, tables)
    back_chan = lax.all_to_all(back_rows, "ctx", split_axis=1, concat_axis=0, tiled=True)
    conv_back = back_chan.T
    mixed_grad = conv_back.astype(jnp.float32) + skip_gain * gated.astype(jnp.float32)
    key_grad = (mixed_grad * value_conv).astype(jnp.bfloat16)
    feature_grad = (mixed_grad * key_feat.astype(jnp.float32)).astype(jnp.bfloat16)
    after = passed_along(feature_grad[:2], "ctx", -1)
    extended = jnp.concatenate([feature_grad, after], 0).astype(jnp.float32)
    value_grad = (
        short_filter[0] * extended[:-2]
        + short_filter[1] * extended[1:-1]
        + short_filter[2] * extended[2:]
    ).astype(jnp.bfloat16)
    feature_wide = extended[:-2]
    short_part = jnp.stack(
        [
            jnp.sum(feature_wide * padded[2:], axis=0),
            jnp.sum(feature_wide * padded[1:-1], axis=0),
            jnp.sum(feature_wide * padded[:-2], axis=0),
        ]
    )
    skip_grad, short_grad = (
        lax.psum_scatter(skip_part, "ctx", scatter_dimension=0, tiled=True),
        lax.psum_scatter(short_part, "ctx", scatter_dimension=1, tiled=True),
    )
    return (query_grad, key_grad, value_grad, filter_grad, skip_grad, short_grad)


INNER = 128
INNER_PEERS = 4


def half_spectrum(values, length):
    if length == 2:
        return [(values[0], None), (values[0], None)]
    even = half_spectrum(values[0::2], length // 2)
    odd = half_spectrum(values[1::2], length // 2)
    quarter = length // 4
    bins = [None] * (length // 2 + 1)
    bins[0] = (even[0][0] + odd[0][0], None)
    bins[length // 2] = (even[0][0] - odd[0][0], None)
    bins[quarter] = (even[quarter][0], -odd[quarter][0])
    for k in range(1, quarter):
        c = math.cos(2.0 * math.pi * k / length)
        s = math.sin(2.0 * math.pi * k / length)
        odd_re, odd_im = odd[k]
        even_re, even_im = even[k]
        if 2 * k == quarter:
            turn_re = (odd_re + odd_im) * c
            turn_im = (odd_im - odd_re) * c
        else:
            turn_re = odd_re * c + odd_im * s
            turn_im = odd_im * c - odd_re * s
        bins[k] = (even_re + turn_re, even_im + turn_im)
        bins[length // 2 - k] = (even_re - turn_re, turn_im - even_im)
    return bins


def first_half(bins, length):
    if length == 2:
        return [bins[0][0] + bins[1][0]]
    half = length // 2
    quarter = length // 4
    even = [None] * (quarter + 1)
    odd = [None] * (quarter + 1)
    even[0] = (bins[0][0] + bins[half][0], None)
    odd[0] = (bins[0][0] - bins[half][0], None)
    even[quarter] = (2.0 * bins[quarter][0], None)
    odd[quarter] = (-2.0 * bins[quarter][1], None)
    for k in range(1, quarter):
        c = math.cos(2.0 * math.pi * k / length)
        s = math.sin(2.0 * math.pi * k / length)
        near_re, near_im = bins[k]
        far_re, far_im = bins[half - k]
        even[k] = (near_re + far_re, near_im - far_im)
        gap_re = near_re - far_re
        gap_im = near_im + far_im
        if 2 * k == quarter:
            odd[k] = ((gap_re - gap_im) * c, (gap_re + gap_im) * c)
        else:
            odd[k] = (gap_re * c - gap_im * s, gap_re * s + gap_im * c)
    result = [None] * half
    result[0::2] = first_half(even, half)
    result[1::2] = first_half(odd, half)
    return result


def spectrum_tables(outer):
    size = outer * INNER
    near = np.arange(outer // 2 + 1)[:, None, None]
    place = np.arange(INNER)
    angle = -2.0 * np.pi * (
        (near * place[None, None, :]) / size + place[None, :, None] * place[None, None, :] / INNER
    )
    c, s = np.cos(angle), np.sin(angle)
    ahead = np.concatenate(
        [np.concatenate([c, -s], 2), np.concatenate([s, c], 2)], 1
    )
    back = np.swapaxes(ahead, 1, 2) / size
    return ahead.astype(jnp.bfloat16), back.astype(jnp.bfloat16)


def outer_ahead(load, z_ref, outer, width):
    def step(chunk, carry):
        row = pl.multiple_of(chunk * 16, 16)
        for lane in range(0, width, 128):
            values = [load(a, row, lane).astype(jnp.float32) for a in range(outer // 2)]
            bins = half_spectrum(values, outer)
            for k, (re, im) in enumerate(bins):
                im = jnp.zeros_like(re) if im is None else im
                z_ref[k, pl.ds(row, 16), lane : lane + 128] = re.astype(jnp.bfloat16)
                z_ref[k, pl.ds(INNER + row, 16), lane : lane + 128] = im.astype(jnp.bfloat16)
        return carry

    lax.fori_loop(0, INNER // 16, step, 0)


def outer_back(u_ref, store, outer, width):
    def step(chunk, carry):
        row = pl.multiple_of(chunk * 16, 16)
        for lane in range(0, width, 128):
            bins = []
            for k in range(outer // 2 + 1):
                re = u_ref[k, pl.ds(row, 16), lane : lane + 128]
                im = u_ref[k, pl.ds(INNER + row, 16), lane : lane + 128]
                bins.append((re, im))
            for a, value in enumerate(first_half(bins, outer)):
                store(a, row, lane, value)
        return carry

    lax.fori_loop(0, INNER // 16, step, 0)


def correlate_bin(first, gated):
    first_re, first_im = first[:INNER], first[INNER:]
    gated_re, gated_im = gated[:INNER], gated[INNER:]
    return jnp.concatenate(
        [
            first_re * gated_re + first_im * gated_im,
            first_re * gated_im - first_im * gated_re,
        ],
        0,
    ).astype(jnp.bfloat16)


def dot32(a, b):
    return jnp.dot(a, b, preferred_element_type=jnp.float32)


def filter_kernel(taps_ref, ahead_ref, spec_ref, rows_ref, z_ref, *, outer, width):
    for a in range(outer // 2):
        piece = taps_ref[:, a * INNER : (a + 1) * INNER].astype(jnp.float32)
        rows_ref[a * INNER : (a + 1) * INNER, :] = piece.T
    outer_ahead(
        lambda a, row, lane: rows_ref[pl.ds(a * INNER + row, 16), lane : lane + 128],
        z_ref, outer, width,
    )

    for k in range(outer // 2 + 1):
        spec_ref[k] = dot32(ahead_ref[k], z_ref[k]).astype(jnp.bfloat16)


def begun(source, target, semaphore):
    copy = pltpu.make_async_copy(source, target, semaphore)
    copy.start()
    return copy


def conv_kernel(
    gated_hbm, filter_hbm, ahead_hbm, back_hbm, conv_ref, spec_hbm,
    gated_ref, filter_ref, ahead_ref, back_ref, spec_ref, z_ref, u_ref, sems, *, outer, width,
):
    gated_in = begun(gated_hbm, gated_ref, sems.at[0])
    ahead_in = begun(ahead_hbm, ahead_ref, sems.at[1])
    filter_in = begun(filter_hbm, filter_ref, sems.at[2])
    back_in = begun(back_hbm, back_ref, sems.at[3])
    gated_in.wait()
    outer_ahead(
        lambda a, row, lane: gated_ref[pl.ds(a * INNER + row, 16), lane : lane + 128],
        z_ref, outer, width,
    )
    ahead_in.wait()
    filter_in.wait()
    for k in range(outer // 2 + 1):
        gated = dot32(ahead_ref[k], z_ref[k])
        spec_ref[k] = gated.astype(jnp.bfloat16)
        z_ref[k] = correlate_bin(filter_ref[k].astype(jnp.float32), gated)
    spec_out = begun(spec_ref, spec_hbm, sems.at[4])
    back_in.wait()
    for k in range(outer // 2 + 1):
        u_ref[k] = dot32(back_ref[k], z_ref[k])

    def store(a, row, lane, value):
        conv_ref[pl.ds(a * INNER + row, 16), lane : lane + 128] = value.astype(jnp.bfloat16)

    outer_back(u_ref, store, outer, width)
    spec_out.wait()


def grad_kernel(*refs, outer, width):
    far = outer // 2 // INNER_PEERS
    place_hbm, refs = refs[:far], refs[far:]
    near_hbm, refs = refs[: INNER_PEERS - 1], refs[INNER_PEERS - 1 :]
    far_hbm, refs = refs[: far - 1], refs[far - 1 :]
    gated_hbm, spec_hbm, ahead_hbm, back_hbm, grad_ref, skip_ref = refs[:6]
    mixed_ref, gated_ref, spec_ref, ahead_ref, back_ref, z_ref, u_ref, rows_ref, sems = refs[6:]
    slabs = outer // 2
    me = lax.axis_index("ctx")
    own_row, own_place = me // INNER_PEERS, me % INNER_PEERS
    mixed_in = []
    for d in range(far):
        for e in range(INNER_PEERS):
            if e == 0:
                source = place_hbm[d]
            elif d == 0:
                source = near_hbm[e - 1].at[own_row]
            else:
                source = far_hbm[d - 1].at[e - 1]
            slab = (own_row ^ d) * INNER_PEERS + (own_place ^ e)
            mixed_in.append(begun(source, mixed_ref.at[slab], sems.at[4 + len(mixed_in)]))
    ahead_in = begun(ahead_hbm, ahead_ref, sems.at[0])
    spec_in = begun(spec_hbm, spec_ref, sems.at[1])
    back_in = begun(back_hbm, back_ref, sems.at[2])
    gated_in = begun(gated_hbm, gated_ref, sems.at[3])
    for copy in mixed_in:
        copy.wait()
    outer_ahead(
        lambda a, row, lane: mixed_ref[a, pl.ds(row, 16), lane : lane + 128],
        z_ref, outer, width,
    )
    ahead_in.wait()
    spec_in.wait()
    for k in range(outer // 2 + 1):
        mixed = dot32(ahead_ref[k], z_ref[k])
        z_ref[k] = correlate_bin(mixed, spec_ref[k].astype(jnp.float32))
    back_in.wait()
    for k in range(outer // 2 + 1):
        u_ref[k] = dot32(back_ref[k], z_ref[k])

    def store(a, row, lane, value):
        rows_ref[pl.ds(a * INNER + row, 16), lane : lane + 128] = value

    outer_back(u_ref, store, outer, width)
    for a in range(slabs):
        grad_ref[:, a * INNER : (a + 1) * INNER] = rows_ref[
            a * INNER : (a + 1) * INNER, :
        ].T.astype(jnp.bfloat16)
    gated_in.wait()

    def add(a, total):
        place = pl.ds(pl.multiple_of(a * INNER, INNER), INNER)
        part = gated_ref[place, :].astype(jnp.float32) * mixed_ref[a].astype(jnp.float32)
        return total + jnp.sum(part.reshape(INNER // 8, 8, width), axis=0)

    total = lax.fori_loop(0, slabs, add, jnp.zeros((8, width), jnp.float32))
    skip_ref[...] = jnp.sum(total, axis=0, keepdims=True)


def regroup_kernel(*refs):
    near, far = refs[: INNER_PEERS - 1], refs[INNER_PEERS - 1 :]
    own_row = lax.axis_index("ctx") // INNER_PEERS
    for d in range(1, len(far) + 1):
        for e in range(1, INNER_PEERS):
            far[d - 1][e - 1] = near[e - 1][own_row ^ d]


def shifted_down(values, distance, edge):
    moved = pltpu.roll(values, distance, 0)
    row = lax.broadcasted_iota(jnp.int32, values.shape, 0)
    for i in range(distance):
        source = edge.shape[0] - distance + i
        moved = jnp.where(row == i, edge[source : source + 1], moved)
    return moved


def shifted_up(values, distance, edge):
    count = values.shape[0]
    moved = pltpu.roll(values, count - distance, 0)
    row = lax.broadcasted_iota(jnp.int32, values.shape, 0)
    for i in range(distance):
        moved = jnp.where(row == count - distance + i, edge[i : i + 1], moved)
    return moved


def gate_kernel(grad_ref, query_ref, value_ref, gated_ref, last_ref, *, width):
    last_ref[...] = value_ref[value_ref.shape[0] - 2 :]
    for j in range(gated_ref.shape[0]):
        cols = slice(j * width, (j + 1) * width)
        gated_ref[j] = (
            grad_ref[:, cols].astype(jnp.float32) * query_ref[:, cols].astype(jnp.float32)
        ).astype(jnp.bfloat16)


def mix_kernel(key_ref, value_ref, edge_ref, short_ref, grad_ref, conv_ref, *rest, width):
    near_refs, place_refs = rest[: INNER_PEERS - 1], rest[INNER_PEERS - 1 : -3]
    query_grad_ref, behind, mixed_ref = rest[-3:]
    rows = key_ref.shape[0]
    owners = key_ref.shape[1] // width
    step = pl.program_id(0)
    for j in range(owners):
        for lane in range(0, width, 128):
            slot = (j * width + lane) // 128 % 2
            cols = slice(j * width + lane, j * width + lane + 128)
            value = value_ref[:, cols].astype(jnp.float32)
            behind[slot, 6:8] = edge_ref[:, cols].astype(jnp.float32)
            behind[slot, 8 : 8 + rows] = value
            conv = (
                short_ref[0:1, cols] * value
                + short_ref[1:2, cols] * behind[slot, 7 : 7 + rows]
                + short_ref[2:3, cols] * behind[slot, 6 : 6 + rows]
            )
            mixed_ref[step * owners + j, :, lane : lane + 128] = (
                key_ref[:, cols].astype(jnp.float32) * conv
            ).astype(jnp.bfloat16)
            query_grad_ref[:, cols] = (
                grad_ref[:, cols].astype(jnp.float32) * conv_ref[:, cols].astype(jnp.float32)
            ).astype(jnp.bfloat16)

    @pl.when(step == pl.num_programs(0) - 1)
    def _():
        me = lax.axis_index("ctx")
        own_row, place = me // INNER_PEERS, me % INNER_PEERS
        for e, near_ref in enumerate(near_refs, 1):
            for row in range(near_ref.shape[0]):
                near_ref[row] = mixed_ref[row * INNER_PEERS + (place ^ e)]
        for d, place_ref in enumerate(place_refs):
            place_ref[...] = mixed_ref[(own_row ^ d) * INNER_PEERS + place]


def finish_kernel(
    back_ref, gated_ref, key_ref, value_ref, edge_ref, short_ref, skip_ref,
    key_grad_ref, value_grad_ref, head_ref, tail_ref, *rest, width,
):
    part_refs, behind, ahead, sums_ref = rest[:-3], rest[-3], rest[-2], rest[-1]
    rows = key_ref.shape[0]
    owners = back_ref.shape[0]
    step = pl.program_id(0)
    for j in range(owners):
        for lane in range(0, width, 128):
            slot = (j * width + lane) // 128 % 2
            cols = slice(j * width + lane, j * width + lane + 128)
            lanes = slice(lane, lane + 128)
            short = [short_ref[i : i + 1, cols] for i in range(3)]
            value = value_ref[:, cols].astype(jnp.float32)
            behind[slot, 6:8] = edge_ref[:, cols].astype(jnp.float32)
            behind[slot, 8 : 8 + rows] = value
            value_1 = behind[slot, 7 : 7 + rows]
            value_2 = behind[slot, 6 : 6 + rows]
            mixed_grad = back_ref[j, :, lanes].astype(jnp.float32) + skip_ref[:, cols] * gated_ref[
                j, :, lanes
            ].astype(jnp.float32)
            conv = short[0] * value + short[1] * value_1 + short[2] * value_2
            key_grad_ref[:, cols] = (mixed_grad * conv).astype(jnp.bfloat16)
            feature = (mixed_grad * key_ref[:, cols].astype(jnp.float32)).astype(jnp.bfloat16)
            head_ref[:, cols] = feature[:2]
            tail_ref[:, cols] = feature[rows - 16 :]
            feature = feature.astype(jnp.float32)
            ahead[slot, 0:rows] = feature
            ahead[slot, rows : rows + 8] = jnp.zeros((8, 128), jnp.float32)
            value_grad_ref[:, cols] = (
                short[0] * feature
                + short[1] * ahead[slot, 1 : 1 + rows]
                + short[2] * ahead[slot, 2 : 2 + rows]
            ).astype(jnp.bfloat16)
            sums = jnp.concatenate(
                [
                    jnp.sum(feature * other, axis=0, keepdims=True)
                    for other in (value, value_1, value_2)
                ]
                + [jnp.zeros((5, 128), jnp.float32)],
                0,
            )
            sums_ref[step * owners + j, :, lanes] = sums

    @pl.when(step == pl.num_programs(0) - 1)
    def _():
        own = lax.axis_index("ctx") // INNER_PEERS
        for d, part_ref in enumerate(part_refs):
            part_ref[...] = sums_ref[pl.ds((own ^ d) * INNER_PEERS, INNER_PEERS)]


def seam_kernel(tail_ref, head_ref, short_ref, done_ref, value_grad_ref):
    feature = tail_ref[...].astype(jnp.float32)
    head = head_ref[...].astype(jnp.float32)
    value_grad_ref[...] = (
        short_ref[0:1] * feature
        + short_ref[1:2] * shifted_up(feature, 1, head)
        + short_ref[2:3] * shifted_up(feature, 2, head)
    ).astype(jnp.bfloat16)


def exchanged(block):
    return lax.all_to_all(block, "ctx", split_axis=0, concat_axis=0, tiled=True)


def paired(block, distance):
    return lax.ppermute(block, "ctx", [(i, i ^ distance) for i in range(lax.axis_size("ctx"))])


def summed_at_owner(parts, *beside):
    place = lax.axis_index("ctx") % INNER_PEERS
    got = [parts[0]] + [paired(parts[d], d * INNER_PEERS) for d in range(1, len(parts))]
    rows = sum(got[1:], got[0])
    rows, beside = lax.optimization_barrier((rows, beside))
    total = lax.dynamic_index_in_dim(rows, place, 0, keepdims=False)
    for distance in range(1, INNER_PEERS):
        other = lax.dynamic_index_in_dim(rows, place ^ distance, 0, keepdims=False)
        total = total + paired(other, distance)
    return total, *beside


def after(value, *others):
    return lax.optimization_barrier((value,) + others)[0]


def params(mib=63):
    return pltpu.CompilerParams(vmem_limit_bytes=mib * 1024 * 1024)


def cost(flops, size):
    return pl.CostEstimate(flops=flops, bytes_accessed=size, transcendentals=0)


def kernel_plan(
    query_feat, key_feat, value_raw, conv_out, out_grad, filter_taps, short_filter, skip_gain
):
    rows, channels = query_feat.shape
    peers = lax.axis_size("ctx")
    width = channels // peers
    seq = rows * peers
    outer = 2 * seq // INNER
    bins = outer // 2 + 1
    steps = 2
    group = peers // steps
    span = group * width
    far = peers // INNER_PEERS
    any_place = pl.BlockSpec(memory_space=pl.ANY)
    hbm = pl.BlockSpec(memory_space=pltpu.HBM)
    bf16, f32 = jnp.bfloat16, jnp.float32
    shape = jax.ShapeDtypeStruct
    skip_row = skip_gain.reshape(1, channels)
    ahead, back = (jnp.asarray(t) for t in spectrum_tables(outer))

    flat = pl.BlockSpec((rows, span), lambda i: (0, i))
    owned = pl.BlockSpec((group, rows, width), lambda i: (i, 0, 0))
    edge_spec = pl.BlockSpec((2, span), lambda i: (0, i))
    tail_spec = pl.BlockSpec((16, span), lambda i: (0, i))
    short_spec = pl.BlockSpec((3, span), lambda i: (0, i))
    skip_spec = pl.BlockSpec((1, span), lambda i: (0, i))

    gated, last = pl.pallas_call(
        functools.partial(gate_kernel, width=width),
        grid=(steps,),
        in_specs=[flat, flat, pl.BlockSpec((16, span), lambda i: (rows // 16 - 1, i))],
        out_specs=[owned, edge_spec],
        out_shape=[shape((peers, rows, width), bf16), shape((2, channels), bf16)],
        compiler_params=params(),
        cost_estimate=cost(rows * channels, 6 * rows * channels),
        name="gate",
    )(out_grad, query_feat, value_raw)

    gated_got = exchanged(gated.reshape(seq, width))

    spec_shape = shape((bins, 2 * INNER, width), bf16)
    z_scratch = pltpu.VMEM((bins, 2 * INNER, width), bf16)
    u_scratch = pltpu.VMEM((bins, 2 * INNER, width), f32)
    table_scratch = pltpu.VMEM((bins, 2 * INNER, 2 * INNER), bf16)
    table_bytes = 8 * bins * INNER * INNER
    spec_bytes = 4 * bins * INNER * width
    work = 2 * bins * (2 * INNER) ** 2 * width
    edge = passed_along(last, "ctx", 1)
    whole = lambda size: pl.BlockSpec((size, channels), lambda i: (0, 0))
    shift_scratch = pltpu.VMEM((2, rows + 8, 128), f32)
    near_spec = pl.BlockSpec((far, rows, width), lambda i: (0, 0, 0))
    far_spec = pl.BlockSpec((INNER_PEERS - 1, rows, width), lambda i: (0, 0, 0))
    place_spec = pl.BlockSpec((rows, width), lambda i: (0, 0))
    *mixed, query_grad = pl.pallas_call(
        functools.partial(mix_kernel, width=width),
        grid=(steps,),
        in_specs=[flat, flat, edge_spec, short_spec, flat, flat],
        out_specs=[near_spec] * (INNER_PEERS - 1) + [place_spec] * far + [flat],
        out_shape=[shape((far, rows, width), bf16)] * (INNER_PEERS - 1)
        + [shape((rows, width), bf16)] * far
        + [shape((rows, channels), bf16)],
        scratch_shapes=[shift_scratch, pltpu.VMEM((peers, rows, width), bf16)],
        compiler_params=params(),
        cost_estimate=cost(40000000000, 12 * rows * channels),
        name="mix",
    )(key_feat, value_raw, edge, short_filter, out_grad, conv_out)
    near = [paired(mixed[e - 1], e) for e in range(1, INNER_PEERS)]
    placed = mixed[INNER_PEERS - 1 :]

    placed = [placed[0]] + [paired(placed[d], d * INNER_PEERS) for d in range(1, far)]
    across = pl.pallas_call(
        regroup_kernel,
        grid=(1,),
        in_specs=[near_spec] * (INNER_PEERS - 1),
        out_specs=[far_spec] * (far - 1),
        out_shape=[shape((INNER_PEERS - 1, rows, width), bf16)] * (far - 1),
        compiler_params=params(),
        cost_estimate=cost(0, 4 * seq * width),
        name="regroup",
    )(*near)
    filter_taps, query_grad = lax.optimization_barrier((filter_taps, query_grad))
    filter_spec = pl.pallas_call(
        functools.partial(filter_kernel, outer=outer, width=width),
        out_shape=spec_shape,
        scratch_shapes=[pltpu.VMEM((seq, width), f32), z_scratch],
        compiler_params=params(),
        cost_estimate=cost(40000000000, table_bytes + spec_bytes + 2 * seq * width),
        name="filter_spectrum",
    )(filter_taps, ahead)


    *across, gated_got = lax.optimization_barrier((*across, gated_got))
    across = [paired(across[d - 1], d * INNER_PEERS) for d in range(1, far)]

    conv_back, gated_spec = pl.pallas_call(
        functools.partial(conv_kernel, outer=outer, width=width),
        in_specs=[hbm] * 4,
        out_specs=[pl.BlockSpec(memory_space=pltpu.VMEM), hbm],
        out_shape=(shape((seq, width), bf16), spec_shape),
        scratch_shapes=[pltpu.VMEM((seq, width), bf16), z_scratch, table_scratch, table_scratch, z_scratch]
        + [z_scratch, u_scratch, pltpu.SemaphoreType.DMA((5,))],
        compiler_params=params(),
        cost_estimate=cost(40000000000, 2 * table_bytes + 2 * spec_bytes + 4 * seq * width),
        name="conv_back",
    )(gated_got, filter_spec, ahead, back)

    back_got = exchanged(conv_back).reshape(peers, rows, width)


    filter_grad, skip_grad = pl.pallas_call(
        functools.partial(grad_kernel, outer=outer, width=width),
        in_specs=[hbm] * (INNER_PEERS + 2 * far + 2),
        out_shape=[shape((width, seq), bf16), shape((1, width), f32)],
        scratch_shapes=[
            pltpu.VMEM((peers, rows, width), bf16),
            pltpu.VMEM((seq, width), bf16),
            z_scratch,
            table_scratch,
            table_scratch,
            z_scratch,
            u_scratch,
            pltpu.VMEM((seq, width), f32),
            pltpu.SemaphoreType.DMA((peers + 4,)),
        ],
        compiler_params=params(63),
        cost_estimate=cost(100000000000, 2 * table_bytes + spec_bytes),
        name="filter_grad",
    )(*placed, *near, *across, gated_got, gated_spec, ahead, back)
    back_got, filter_grad, skip_grad = lax.optimization_barrier((back_got, filter_grad, skip_grad))

    key_grad, value_grad, head, tail, *short_parts = pl.pallas_call(
        functools.partial(finish_kernel, width=width),
        grid=(steps,),
        in_specs=[owned, owned, flat, flat, edge_spec, short_spec, skip_spec],
        out_specs=[flat, flat, edge_spec, tail_spec]
        + [pl.BlockSpec((INNER_PEERS, 8, width), lambda i: (0, 0, 0))] * far,
        out_shape=[shape((rows, channels), bf16)] * 2
        + [shape((2, channels), bf16), shape((16, channels), bf16)]
        + [shape((INNER_PEERS, 8, width), f32)] * far,
        scratch_shapes=[pltpu.VMEM((2, rows + 8, 128), f32)] * 2 + [pltpu.VMEM((peers, 8, width), f32)],
        compiler_params=params(63),
        cost_estimate=cost(30 * rows * channels, 12 * rows * channels),
        name="finish",
    )(back_got, gated, key_feat, value_raw, edge, short_filter, skip_row)

    head_got = passed_along(head, "ctx", -1)
    short_grad, head_got, value_grad = summed_at_owner(short_parts, head_got, value_grad)
    value_grad = pl.pallas_call(
        seam_kernel,
        grid=(1,),
        in_specs=[whole(16), whole(2), whole(3), hbm],
        out_specs=pl.BlockSpec((16, channels), lambda i: (rows // 16 - 1, 0)),
        out_shape=shape((rows, channels), bf16),
        input_output_aliases={3: 0},
        compiler_params=params(),
        cost_estimate=cost(5 * 16 * channels, 6 * 16 * channels),
        name="seam",
    )(tail, head_got, short_filter, value_grad)
    return query_grad, key_grad, value_grad, filter_grad, skip_grad.reshape(width), short_grad[:3]


def per_device(query_feat, key_feat, value_raw, conv_out, out_grad, filter_taps, short_filter, skip_gain):
    rows, channels = query_feat.shape
    peers = lax.axis_size("ctx")
    width = channels // peers
    fits = (
        peers % INNER_PEERS == 0
        and peers & (peers - 1) == 0
        and rows == INNER
        and width % 256 == 0
        and peers in (8, 16)
    )
    plan = kernel_plan if fits else general_plan
    return plan(query_feat, key_feat, value_raw, conv_out, out_grad, filter_taps, short_filter, skip_gain)


def solution(mesh):
    in_specs = (
        P(("groups", "ctx"), None),
        P(("groups", "ctx"), None),
        P(("groups", "ctx"), None),
        P(("groups", "ctx"), None),
        P(("groups", "ctx"), None),
        P("ctx", None),
        P(),
        P(),
    )
    out_specs = (
        P(("groups", "ctx"), None),
        P(("groups", "ctx"), None),
        P(("groups", "ctx"), None),
        P(("groups", "ctx"), None),
        P(("groups", "ctx")),
        P(None, ("groups", "ctx")),
    )
    return jax.shard_map(
        per_device, mesh=mesh, in_specs=in_specs, out_specs=out_specs, check_vma=False
    )
```

```python
import functools
import math

import jax
import jax.numpy as jnp
import numpy as np
from jax import lax
from jax.experimental import pallas as pl
from jax.experimental.pallas import tpu as pltpu
from jax.sharding import PartitionSpec as P

PRECISE = lax.Precision.HIGH


def passed_along(block, axis, distance):
    devices = range(lax.axis_size(axis))
    route = [(i - distance, i) for i in devices if i - distance in devices]
    return lax.ppermute(block, axis, route)


def dft_pair(row_count, col_count, period):
    row_index = lax.iota(jnp.int32, row_count)[:, None]
    col_index = lax.iota(jnp.int32, col_count)[None, :]
    phase = (row_index * col_index % period).astype(jnp.float32) * (-2.0 * math.pi / period)
    return (jnp.cos(phase), jnp.sin(phase))


def make_tables(inner, outer):
    half = outer // 2
    outer_cos, outer_sin = dft_pair(outer, half, outer)
    twist_cos, twist_sin = dft_pair(outer, inner, outer * inner)
    inner_cos, inner_sin = dft_pair(inner, inner, inner)
    real_outer = jnp.stack([outer_cos, outer_sin], 1)
    complex_outer = jnp.stack(
        [jnp.stack([outer_cos, -outer_sin], 1), jnp.stack([outer_sin, outer_cos], 1)], 1
    )
    inner_ahead = jnp.block([[inner_cos, inner_sin], [-inner_sin, inner_cos]])
    inner_back = jnp.block([[inner_cos, -inner_sin], [inner_sin, inner_cos]])
    outer_back = jnp.stack(
        [jnp.stack([outer_cos, outer_sin], 0), jnp.stack([-outer_sin, outer_cos], 0)], 0
    )
    return (real_outer, complex_outer, twist_cos, twist_sin, inner_ahead, inner_back, outer_back)


def twist_ahead(values, twist_cos, twist_sin):
    real_part = values[:, :, 0]
    imag_part = values[:, :, 1]
    return jnp.stack(
        [
            real_part * twist_cos - imag_part * twist_sin,
            real_part * twist_sin + imag_part * twist_cos,
        ],
        2,
    )


def twist_back(values, twist_cos, twist_sin):
    real_part = values[:, :, 0]
    imag_part = values[:, :, 1]
    return jnp.stack(
        [
            real_part * twist_cos + imag_part * twist_sin,
            imag_part * twist_cos - real_part * twist_sin,
        ],
        2,
    )


def inner_section(values, table):
    width, outer = (values.shape[0], values.shape[1])
    flat = values.reshape(width, outer, table.shape[0])
    return jnp.einsum(
        "wkc,cd->wkd", flat, table, precision=PRECISE, preferred_element_type=jnp.float32
    )


def real_spectrum(signal, tables):
    real_outer, complex_outer, twist_cos, twist_sin, inner_ahead, inner_back, outer_back = tables
    half = real_outer.shape[2]
    inner = twist_cos.shape[1]
    blocked = signal.reshape(signal.shape[0], half, inner)
    first = jnp.einsum(
        "wab,kra->wkrb", blocked, real_outer, precision=PRECISE, preferred_element_type=jnp.float32
    )
    return inner_section(twist_ahead(first, twist_cos, twist_sin), inner_ahead)


def complex_spectrum(signal_re, signal_im, tables):
    real_outer, complex_outer, twist_cos, twist_sin, inner_ahead, inner_back, outer_back = tables
    half = real_outer.shape[2]
    inner = twist_cos.shape[1]
    width = signal_re.shape[0]
    stacked = jnp.stack(
        [signal_re.reshape(width, half, inner), signal_im.reshape(width, half, inner)], 1
    )
    first = jnp.einsum(
        "wsab,krsa->wkrb",
        stacked,
        complex_outer,
        precision=PRECISE,
        preferred_element_type=jnp.float32,
    )
    return inner_section(twist_ahead(first, twist_cos, twist_sin), inner_ahead)


def inverse_spectrum(packed, tables):
    real_outer, complex_outer, twist_cos, twist_sin, inner_ahead, inner_back, outer_back = tables
    outer = twist_cos.shape[0]
    inner = twist_cos.shape[1]
    half = real_outer.shape[2]
    width = packed.shape[0]
    back = inner_section(packed, inner_back).reshape(width, outer, 2, inner)
    turned = twist_back(back, twist_cos, twist_sin)
    result = jnp.einsum(
        "wksb,rska->wrab", turned, outer_back, precision=PRECISE, preferred_element_type=jnp.float32
    )
    scale = 1.0 / (outer * inner)
    return (
        (result[:, 0] * scale).reshape(width, half * inner),
        (result[:, 1] * scale).reshape(width, half * inner),
    )


def spectral_block(gated_rows, mixed_rows, filter_rows, tables):
    inner = tables[2].shape[1]
    gated_spec = real_spectrum(gated_rows.astype(jnp.float32), tables)
    joint_spec = complex_spectrum(
        filter_rows.astype(jnp.float32), -mixed_rows.astype(jnp.float32), tables
    )
    gated_re = gated_spec[:, :, :inner]
    gated_im = gated_spec[:, :, inner:]
    joint_re = joint_spec[:, :, :inner]
    joint_im = joint_spec[:, :, inner:]
    product_re = joint_re * gated_re + joint_im * gated_im
    product_im = joint_re * gated_im - joint_im * gated_re
    product = jnp.concatenate([product_re, product_im], 2)
    result_re, result_im = inverse_spectrum(product, tables)
    return (result_re.astype(jnp.bfloat16), result_im.astype(jnp.bfloat16))


def general_plan(
    query_feat, key_feat, value_raw, conv_out, out_grad, filter_taps, short_filter, skip_gain
):
    rows = query_feat.shape[0]
    peers = lax.axis_size("ctx")
    before = passed_along(value_raw[rows - 2 :], "ctx", 1)
    padded = jnp.concatenate([before, value_raw], 0).astype(jnp.float32)
    value_conv = (
        short_filter[0] * padded[2:]
        + short_filter[1] * padded[1:-1]
        + short_filter[2] * padded[:-2]
    )
    mixed = (key_feat.astype(jnp.float32) * value_conv).astype(jnp.bfloat16)
    gated = (out_grad.astype(jnp.float32) * query_feat.astype(jnp.float32)).astype(jnp.bfloat16)
    query_grad = (out_grad.astype(jnp.float32) * conv_out.astype(jnp.float32)).astype(jnp.bfloat16)
    skip_part = jnp.sum(gated.astype(jnp.float32) * mixed.astype(jnp.float32), axis=0)
    tables = make_tables(rows, 2 * peers)
    gated_chan = gated.T
    mixed_chan = mixed.T
    sent_gated, sent_mixed = (
        lax.all_to_all(gated_chan, "ctx", split_axis=0, concat_axis=1, tiled=True),
        lax.all_to_all(mixed_chan, "ctx", split_axis=0, concat_axis=1, tiled=True),
    )
    back_rows, filter_grad = spectral_block(sent_gated, sent_mixed, filter_taps, tables)
    back_chan = lax.all_to_all(back_rows, "ctx", split_axis=1, concat_axis=0, tiled=True)
    conv_back = back_chan.T
    mixed_grad = conv_back.astype(jnp.float32) + skip_gain * gated.astype(jnp.float32)
    key_grad = (mixed_grad * value_conv).astype(jnp.bfloat16)
    feature_grad = (mixed_grad * key_feat.astype(jnp.float32)).astype(jnp.bfloat16)
    after = passed_along(feature_grad[:2], "ctx", -1)
    extended = jnp.concatenate([feature_grad, after], 0).astype(jnp.float32)
    value_grad = (
        short_filter[0] * extended[:-2]
        + short_filter[1] * extended[1:-1]
        + short_filter[2] * extended[2:]
    ).astype(jnp.bfloat16)
    feature_wide = extended[:-2]
    short_part = jnp.stack(
        [
            jnp.sum(feature_wide * padded[2:], axis=0),
            jnp.sum(feature_wide * padded[1:-1], axis=0),
            jnp.sum(feature_wide * padded[:-2], axis=0),
        ]
    )
    skip_grad, short_grad = (
        lax.psum_scatter(skip_part, "ctx", scatter_dimension=0, tiled=True),
        lax.psum_scatter(short_part, "ctx", scatter_dimension=1, tiled=True),
    )
    return (query_grad, key_grad, value_grad, filter_grad, skip_grad, short_grad)


INNER = 128
INNER_PEERS = 4


def half_spectrum(values, length):
    if length == 2:
        return [(values[0], None), (values[0], None)]
    even = half_spectrum(values[0::2], length // 2)
    odd = half_spectrum(values[1::2], length // 2)
    quarter = length // 4
    bins = [None] * (length // 2 + 1)
    bins[0] = (even[0][0] + odd[0][0], None)
    bins[length // 2] = (even[0][0] - odd[0][0], None)
    bins[quarter] = (even[quarter][0], -odd[quarter][0])
    for k in range(1, quarter):
        c = math.cos(2.0 * math.pi * k / length)
        s = math.sin(2.0 * math.pi * k / length)
        odd_re, odd_im = odd[k]
        even_re, even_im = even[k]
        if 2 * k == quarter:
            turn_re = (odd_re + odd_im) * c
            turn_im = (odd_im - odd_re) * c
        else:
            turn_re = odd_re * c + odd_im * s
            turn_im = odd_im * c - odd_re * s
        bins[k] = (even_re + turn_re, even_im + turn_im)
        bins[length // 2 - k] = (even_re - turn_re, turn_im - even_im)
    return bins


def first_half(bins, length):
    if length == 2:
        return [bins[0][0] + bins[1][0]]
    half = length // 2
    quarter = length // 4
    even = [None] * (quarter + 1)
    odd = [None] * (quarter + 1)
    even[0] = (bins[0][0] + bins[half][0], None)
    odd[0] = (bins[0][0] - bins[half][0], None)
    even[quarter] = (2.0 * bins[quarter][0], None)
    odd[quarter] = (-2.0 * bins[quarter][1], None)
    for k in range(1, quarter):
        c = math.cos(2.0 * math.pi * k / length)
        s = math.sin(2.0 * math.pi * k / length)
        near_re, near_im = bins[k]
        far_re, far_im = bins[half - k]
        even[k] = (near_re + far_re, near_im - far_im)
        gap_re = near_re - far_re
        gap_im = near_im + far_im
        if 2 * k == quarter:
            odd[k] = ((gap_re - gap_im) * c, (gap_re + gap_im) * c)
        else:
            odd[k] = (gap_re * c - gap_im * s, gap_re * s + gap_im * c)
    result = [None] * half
    result[0::2] = first_half(even, half)
    result[1::2] = first_half(odd, half)
    return result


def spectrum_tables(outer):
    size = outer * INNER
    near = np.arange(outer // 2 + 1)[:, None, None]
    place = np.arange(INNER)
    angle = -2.0 * np.pi * (
        (near * place[None, None, :]) / size + place[None, :, None] * place[None, None, :] / INNER
    )
    c, s = np.cos(angle), np.sin(angle)
    ahead = np.concatenate(
        [np.concatenate([c, -s], 2), np.concatenate([s, c], 2)], 1
    )
    back = np.swapaxes(ahead, 1, 2) / size
    return ahead.astype(jnp.bfloat16), back.astype(jnp.bfloat16)


def outer_ahead(load, z_ref, outer, width):
    def step(chunk, carry):
        row = pl.multiple_of(chunk * 16, 16)
        for lane in range(0, width, 128):
            values = [load(a, row, lane).astype(jnp.float32) for a in range(outer // 2)]
            bins = half_spectrum(values, outer)
            for k, (re, im) in enumerate(bins):
                im = jnp.zeros_like(re) if im is None else im
                z_ref[k, pl.ds(row, 16), lane : lane + 128] = re.astype(jnp.bfloat16)
                z_ref[k, pl.ds(INNER + row, 16), lane : lane + 128] = im.astype(jnp.bfloat16)
        return carry

    lax.fori_loop(0, INNER // 16, step, 0)


def outer_back(u_ref, store, outer, width):
    def step(chunk, carry):
        row = pl.multiple_of(chunk * 16, 16)
        for lane in range(0, width, 128):
            bins = []
            for k in range(outer // 2 + 1):
                re = u_ref[k, pl.ds(row, 16), lane : lane + 128]
                im = u_ref[k, pl.ds(INNER + row, 16), lane : lane + 128]
                bins.append((re, im))
            for a, value in enumerate(first_half(bins, outer)):
                store(a, row, lane, value)
        return carry

    lax.fori_loop(0, INNER // 16, step, 0)


def correlate_bin(first, gated):
    first_re, first_im = first[:INNER], first[INNER:]
    gated_re, gated_im = gated[:INNER], gated[INNER:]
    return jnp.concatenate(
        [
            first_re * gated_re + first_im * gated_im,
            first_re * gated_im - first_im * gated_re,
        ],
        0,
    ).astype(jnp.bfloat16)


def dot32(a, b):
    return jnp.dot(a, b, preferred_element_type=jnp.float32)


def filter_kernel(taps_ref, ahead_ref, spec_ref, rows_ref, z_ref, *, outer, width):
    for a in range(outer // 2):
        piece = taps_ref[:, a * INNER : (a + 1) * INNER].astype(jnp.float32)
        rows_ref[a * INNER : (a + 1) * INNER, :] = piece.T
    outer_ahead(
        lambda a, row, lane: rows_ref[pl.ds(a * INNER + row, 16), lane : lane + 128],
        z_ref, outer, width,
    )

    for k in range(outer // 2 + 1):
        spec_ref[k] = dot32(ahead_ref[k], z_ref[k]).astype(jnp.bfloat16)


def begun(source, target, semaphore):
    copy = pltpu.make_async_copy(source, target, semaphore)
    copy.start()
    return copy


def conv_kernel(
    gated_hbm, filter_hbm, ahead_hbm, back_hbm, conv_ref, spec_hbm,
    gated_ref, filter_ref, ahead_ref, back_ref, spec_ref, z_ref, u_ref, sems, *, outer, width,
):
    gated_in = begun(gated_hbm, gated_ref, sems.at[0])
    ahead_in = begun(ahead_hbm, ahead_ref, sems.at[1])
    filter_in = begun(filter_hbm, filter_ref, sems.at[2])
    back_in = begun(back_hbm, back_ref, sems.at[3])
    gated_in.wait()
    outer_ahead(
        lambda a, row, lane: gated_ref[pl.ds(a * INNER + row, 16), lane : lane + 128],
        z_ref, outer, width,
    )
    ahead_in.wait()
    filter_in.wait()
    for k in range(outer // 2 + 1):
        gated = dot32(ahead_ref[k], z_ref[k])
        spec_ref[k] = gated.astype(jnp.bfloat16)
        z_ref[k] = correlate_bin(filter_ref[k].astype(jnp.float32), gated)
    spec_out = begun(spec_ref, spec_hbm, sems.at[4])
    back_in.wait()
    for k in range(outer // 2 + 1):
        u_ref[k] = dot32(back_ref[k], z_ref[k])

    def store(a, row, lane, value):
        conv_ref[pl.ds(a * INNER + row, 16), lane : lane + 128] = value.astype(jnp.bfloat16)

    outer_back(u_ref, store, outer, width)
    spec_out.wait()


def grad_kernel(*refs, outer, width):
    far = outer // 2 // INNER_PEERS
    place_hbm, refs = refs[:far], refs[far:]
    near_hbm, refs = refs[: INNER_PEERS - 1], refs[INNER_PEERS - 1 :]
    far_hbm, refs = refs[: far - 1], refs[far - 1 :]
    gated_hbm, spec_hbm, ahead_hbm, back_hbm, grad_ref, skip_ref = refs[:6]
    mixed_ref, gated_ref, spec_ref, ahead_ref, back_ref, z_ref, u_ref, rows_ref, sems = refs[6:]
    slabs = outer // 2
    me = lax.axis_index("ctx")
    own_row, own_place = me // INNER_PEERS, me % INNER_PEERS
    mixed_in = []
    for d in range(far):
        for e in range(INNER_PEERS):
            if e == 0:
                source = place_hbm[d]
            elif d == 0:
                source = near_hbm[e - 1].at[own_row]
            else:
                source = far_hbm[d - 1].at[e - 1]
            slab = (own_row ^ d) * INNER_PEERS + (own_place ^ e)
            mixed_in.append(begun(source, mixed_ref.at[slab], sems.at[4 + len(mixed_in)]))
    ahead_in = begun(ahead_hbm, ahead_ref, sems.at[0])
    spec_in = begun(spec_hbm, spec_ref, sems.at[1])
    back_in = begun(back_hbm, back_ref, sems.at[2])
    gated_in = begun(gated_hbm, gated_ref, sems.at[3])
    for copy in mixed_in:
        copy.wait()
    outer_ahead(
        lambda a, row, lane: mixed_ref[a, pl.ds(row, 16), lane : lane + 128],
        z_ref, outer, width,
    )
    ahead_in.wait()
    spec_in.wait()
    for k in range(outer // 2 + 1):
        mixed = dot32(ahead_ref[k], z_ref[k])
        z_ref[k] = correlate_bin(mixed, spec_ref[k].astype(jnp.float32))
    back_in.wait()
    for k in range(outer // 2 + 1):
        u_ref[k] = dot32(back_ref[k], z_ref[k])

    def store(a, row, lane, value):
        rows_ref[pl.ds(a * INNER + row, 16), lane : lane + 128] = value

    outer_back(u_ref, store, outer, width)
    for a in range(slabs):
        grad_ref[:, a * INNER : (a + 1) * INNER] = rows_ref[
            a * INNER : (a + 1) * INNER, :
        ].T.astype(jnp.bfloat16)
    gated_in.wait()

    def add(a, total):
        place = pl.ds(pl.multiple_of(a * INNER, INNER), INNER)
        part = gated_ref[place, :].astype(jnp.float32) * mixed_ref[a].astype(jnp.float32)
        return total + jnp.sum(part.reshape(INNER // 8, 8, width), axis=0)

    total = lax.fori_loop(0, slabs, add, jnp.zeros((8, width), jnp.float32))
    skip_ref[...] = jnp.sum(total, axis=0, keepdims=True)


def regroup_kernel(*refs):
    near, far = refs[: INNER_PEERS - 1], refs[INNER_PEERS - 1 :]
    own_row = lax.axis_index("ctx") // INNER_PEERS
    for d in range(1, len(far) + 1):
        for e in range(1, INNER_PEERS):
            far[d - 1][e - 1] = near[e - 1][own_row ^ d]


def shifted_down(values, distance, edge):
    moved = pltpu.roll(values, distance, 0)
    row = lax.broadcasted_iota(jnp.int32, values.shape, 0)
    for i in range(distance):
        source = edge.shape[0] - distance + i
        moved = jnp.where(row == i, edge[source : source + 1], moved)
    return moved


def shifted_up(values, distance, edge):
    count = values.shape[0]
    moved = pltpu.roll(values, count - distance, 0)
    row = lax.broadcasted_iota(jnp.int32, values.shape, 0)
    for i in range(distance):
        moved = jnp.where(row == count - distance + i, edge[i : i + 1], moved)
    return moved


def gate_kernel(grad_ref, query_ref, value_ref, gated_ref, last_ref, *, width):
    last_ref[...] = value_ref[...].astype(jnp.float32)[value_ref.shape[0] - 2 :]
    for j in range(gated_ref.shape[0]):
        cols = slice(j * width, (j + 1) * width)
        gated_ref[j] = (
            grad_ref[:, cols].astype(jnp.float32) * query_ref[:, cols].astype(jnp.float32)
        ).astype(jnp.bfloat16)


def mix_kernel(key_ref, value_ref, edge_ref, short_ref, grad_ref, conv_ref, *rest, width):
    near_refs, place_refs = rest[: INNER_PEERS - 1], rest[INNER_PEERS - 1 : -3]
    query_grad_ref, behind, mixed_ref = rest[-3:]
    rows = key_ref.shape[0]
    owners = key_ref.shape[1] // width
    step = pl.program_id(0)
    for j in range(owners):
        for lane in range(0, width, 128):
            slot = (j * width + lane) // 128 % 2
            cols = slice(j * width + lane, j * width + lane + 128)
            value = value_ref[:, cols].astype(jnp.float32)
            behind[slot, 6:8] = edge_ref[:, cols]
            behind[slot, 8 : 8 + rows] = value
            conv = (
                short_ref[0:1, cols] * value
                + short_ref[1:2, cols] * behind[slot, 7 : 7 + rows]
                + short_ref[2:3, cols] * behind[slot, 6 : 6 + rows]
            )
            mixed_ref[step * owners + j, :, lane : lane + 128] = (
                key_ref[:, cols].astype(jnp.float32) * conv
            ).astype(jnp.bfloat16)
            query_grad_ref[:, cols] = (
                grad_ref[:, cols].astype(jnp.float32) * conv_ref[:, cols].astype(jnp.float32)
            ).astype(jnp.bfloat16)

    @pl.when(step == pl.num_programs(0) - 1)
    def _():
        me = lax.axis_index("ctx")
        own_row, place = me // INNER_PEERS, me % INNER_PEERS
        for e, near_ref in enumerate(near_refs, 1):
            for row in range(near_ref.shape[0]):
                near_ref[row] = mixed_ref[row * INNER_PEERS + (place ^ e)]
        for d, place_ref in enumerate(place_refs):
            place_ref[...] = mixed_ref[(own_row ^ d) * INNER_PEERS + place]


def finish_kernel(
    back_ref, gated_ref, key_ref, value_ref, edge_ref, short_ref, skip_ref,
    key_grad_ref, value_grad_ref, head_ref, tail_ref, *rest, width,
):
    part_refs, behind, ahead, sums_ref = rest[:-3], rest[-3], rest[-2], rest[-1]
    rows = key_ref.shape[0]
    owners = back_ref.shape[0]
    step = pl.program_id(0)
    for j in range(owners):
        for lane in range(0, width, 128):
            slot = (j * width + lane) // 128 % 2
            cols = slice(j * width + lane, j * width + lane + 128)
            lanes = slice(lane, lane + 128)
            short = [short_ref[i : i + 1, cols] for i in range(3)]
            value = value_ref[:, cols].astype(jnp.float32)
            behind[slot, 6:8] = edge_ref[:, cols]
            behind[slot, 8 : 8 + rows] = value
            value_1 = behind[slot, 7 : 7 + rows]
            value_2 = behind[slot, 6 : 6 + rows]
            mixed_grad = back_ref[j, :, lanes].astype(jnp.float32) + skip_ref[:, cols] * gated_ref[
                j, :, lanes
            ].astype(jnp.float32)
            conv = short[0] * value + short[1] * value_1 + short[2] * value_2
            key_grad_ref[:, cols] = (mixed_grad * conv).astype(jnp.bfloat16)
            feature = (mixed_grad * key_ref[:, cols].astype(jnp.float32)).astype(jnp.bfloat16)
            tail_ref[:, cols] = feature[rows - 16 :]
            feature = feature.astype(jnp.float32)
            head_ref[:, cols] = feature[:2]
            ahead[slot, 0:rows] = feature
            ahead[slot, rows : rows + 8] = jnp.zeros((8, 128), jnp.float32)
            value_grad_ref[:, cols] = (
                short[0] * feature
                + short[1] * ahead[slot, 1 : 1 + rows]
                + short[2] * ahead[slot, 2 : 2 + rows]
            ).astype(jnp.bfloat16)
            sums = jnp.concatenate(
                [
                    jnp.sum(feature * other, axis=0, keepdims=True)
                    for other in (value, value_1, value_2)
                ]
                + [jnp.zeros((5, 128), jnp.float32)],
                0,
            )
            sums_ref[step * owners + j, :, lanes] = sums

    @pl.when(step == pl.num_programs(0) - 1)
    def _():
        own = lax.axis_index("ctx") // INNER_PEERS
        for d, part_ref in enumerate(part_refs):
            part_ref[...] = sums_ref[pl.ds((own ^ d) * INNER_PEERS, INNER_PEERS)]


def seam_kernel(tail_ref, head_ref, short_ref, done_ref, value_grad_ref):
    feature = tail_ref[...].astype(jnp.float32)
    head = head_ref[...]
    value_grad_ref[...] = (
        short_ref[0:1] * feature
        + short_ref[1:2] * shifted_up(feature, 1, head)
        + short_ref[2:3] * shifted_up(feature, 2, head)
    ).astype(jnp.bfloat16)


def exchanged(block):
    return lax.all_to_all(block, "ctx", split_axis=0, concat_axis=0, tiled=True)


def paired(block, distance):
    return lax.ppermute(block, "ctx", [(i, i ^ distance) for i in range(lax.axis_size("ctx"))])


def summed_at_owner(parts, *beside):
    place = lax.axis_index("ctx") % INNER_PEERS
    got = [parts[0]] + [paired(parts[d], d * INNER_PEERS) for d in range(1, len(parts))]
    rows = sum(got[1:], got[0])
    rows, beside = lax.optimization_barrier((rows, beside))
    total = lax.dynamic_index_in_dim(rows, place, 0, keepdims=False)
    for distance in range(1, INNER_PEERS):
        other = lax.dynamic_index_in_dim(rows, place ^ distance, 0, keepdims=False)
        total = total + paired(other, distance)
    return total, *beside


def after(value, *others):
    return lax.optimization_barrier((value,) + others)[0]


def params(mib=63):
    return pltpu.CompilerParams(vmem_limit_bytes=mib * 1024 * 1024)


BESIDE_EXCHANGE = 40_000_000_000
WHOLE_EXCHANGE = 100_000_000_000


def cost(flops, size):
    return pl.CostEstimate(flops=flops, bytes_accessed=size, transcendentals=0)


def kernel_plan(
    query_feat, key_feat, value_raw, conv_out, out_grad, filter_taps, short_filter, skip_gain
):
    rows, channels = query_feat.shape
    peers = lax.axis_size("ctx")
    width = channels // peers
    seq = rows * peers
    outer = 2 * seq // INNER
    bins = outer // 2 + 1
    steps = 2
    group = peers // steps
    span = group * width
    far = peers // INNER_PEERS
    any_place = pl.BlockSpec(memory_space=pl.ANY)
    hbm = pl.BlockSpec(memory_space=pltpu.HBM)
    bf16, f32 = jnp.bfloat16, jnp.float32
    shape = jax.ShapeDtypeStruct
    skip_row = skip_gain.reshape(1, channels)
    ahead, back = (jnp.asarray(t) for t in spectrum_tables(outer))

    flat = pl.BlockSpec((rows, span), lambda i: (0, i))
    owned = pl.BlockSpec((group, rows, width), lambda i: (i, 0, 0))
    edge_spec = pl.BlockSpec((2, span), lambda i: (0, i))
    tail_spec = pl.BlockSpec((16, span), lambda i: (0, i))
    short_spec = pl.BlockSpec((3, span), lambda i: (0, i))
    skip_spec = pl.BlockSpec((1, span), lambda i: (0, i))

    gated, last = pl.pallas_call(
        functools.partial(gate_kernel, width=width),
        grid=(steps,),
        in_specs=[flat, flat, pl.BlockSpec((16, span), lambda i: (rows // 16 - 1, i))],
        out_specs=[owned, edge_spec],
        out_shape=[shape((peers, rows, width), bf16), shape((2, channels), f32)],
        compiler_params=params(),
        cost_estimate=cost(rows * channels, 6 * rows * channels),
        name="gate",
    )(out_grad, query_feat, value_raw)

    gated_got = exchanged(gated.reshape(seq, width))

    spec_shape = shape((bins, 2 * INNER, width), bf16)
    z_scratch = pltpu.VMEM((bins, 2 * INNER, width), bf16)
    u_scratch = pltpu.VMEM((bins, 2 * INNER, width), f32)
    table_scratch = pltpu.VMEM((bins, 2 * INNER, 2 * INNER), bf16)
    table_bytes = 8 * bins * INNER * INNER
    spec_bytes = 4 * bins * INNER * width
    work = 2 * bins * (2 * INNER) ** 2 * width
    edge = passed_along(last, "ctx", 1)
    whole = lambda size: pl.BlockSpec((size, channels), lambda i: (0, 0))
    shift_scratch = pltpu.VMEM((2, rows + 8, 128), f32)
    near_spec = pl.BlockSpec((far, rows, width), lambda i: (0, 0, 0))
    far_spec = pl.BlockSpec((INNER_PEERS - 1, rows, width), lambda i: (0, 0, 0))
    place_spec = pl.BlockSpec((rows, width), lambda i: (0, 0))
    *mixed, query_grad = pl.pallas_call(
        functools.partial(mix_kernel, width=width),
        grid=(steps,),
        in_specs=[flat, flat, edge_spec, short_spec, flat, flat],
        out_specs=[near_spec] * (INNER_PEERS - 1) + [place_spec] * far + [flat],
        out_shape=[shape((far, rows, width), bf16)] * (INNER_PEERS - 1)
        + [shape((rows, width), bf16)] * far
        + [shape((rows, channels), bf16)],
        scratch_shapes=[shift_scratch, pltpu.VMEM((peers, rows, width), bf16)],
        compiler_params=params(),
        cost_estimate=cost(BESIDE_EXCHANGE, 12 * rows * channels),
        name="mix",
    )(key_feat, value_raw, edge, short_filter, out_grad, conv_out)
    near = [paired(mixed[e - 1], e) for e in range(1, INNER_PEERS)]
    placed = mixed[INNER_PEERS - 1 :]
    placed = [placed[0]] + [paired(placed[d], d * INNER_PEERS) for d in range(1, far)]
    across = pl.pallas_call(
        regroup_kernel,
        grid=(1,),
        in_specs=[near_spec] * (INNER_PEERS - 1),
        out_specs=[far_spec] * (far - 1),
        out_shape=[shape((INNER_PEERS - 1, rows, width), bf16)] * (far - 1),
        compiler_params=params(),
        cost_estimate=cost(0, 4 * seq * width),
        name="regroup",
    )(*near)
    filter_taps, query_grad = lax.optimization_barrier((filter_taps, query_grad))
    filter_spec = pl.pallas_call(
        functools.partial(filter_kernel, outer=outer, width=width),
        out_shape=spec_shape,
        scratch_shapes=[pltpu.VMEM((seq, width), f32), z_scratch],
        compiler_params=params(),
        cost_estimate=cost(BESIDE_EXCHANGE, table_bytes + spec_bytes + 2 * seq * width),
        name="filter_spectrum",
    )(filter_taps, ahead)


    *across, gated_got = lax.optimization_barrier((*across, gated_got))
    across = [paired(across[d - 1], d * INNER_PEERS) for d in range(1, far)]

    conv_back, gated_spec = pl.pallas_call(
        functools.partial(conv_kernel, outer=outer, width=width),
        in_specs=[hbm] * 4,
        out_specs=[pl.BlockSpec(memory_space=pltpu.VMEM), hbm],
        out_shape=(shape((seq, width), bf16), spec_shape),
        scratch_shapes=[pltpu.VMEM((seq, width), bf16), z_scratch, table_scratch, table_scratch, z_scratch]
        + [z_scratch, u_scratch, pltpu.SemaphoreType.DMA((5,))],
        compiler_params=params(),
        cost_estimate=cost(BESIDE_EXCHANGE, 2 * table_bytes + 2 * spec_bytes + 4 * seq * width),
        name="conv_back",
    )(gated_got, filter_spec, ahead, back)

    back_got = exchanged(conv_back).reshape(peers, rows, width)

    filter_grad, skip_grad = pl.pallas_call(
        functools.partial(grad_kernel, outer=outer, width=width),
        in_specs=[hbm] * (INNER_PEERS + 2 * far + 2),
        out_shape=[shape((width, seq), bf16), shape((1, width), f32)],
        scratch_shapes=[
            pltpu.VMEM((peers, rows, width), bf16),
            pltpu.VMEM((seq, width), bf16),
            z_scratch,
            table_scratch,
            table_scratch,
            z_scratch,
            u_scratch,
            pltpu.VMEM((seq, width), f32),
            pltpu.SemaphoreType.DMA((peers + 4,)),
        ],
        compiler_params=params(),
        cost_estimate=cost(WHOLE_EXCHANGE, 2 * table_bytes + spec_bytes),
        name="filter_grad",
    )(*placed, *near, *across, gated_got, gated_spec, ahead, back)
    back_got, filter_grad, skip_grad = lax.optimization_barrier((back_got, filter_grad, skip_grad))

    key_grad, value_grad, head, tail, *short_parts = pl.pallas_call(
        functools.partial(finish_kernel, width=width),
        grid=(steps,),
        in_specs=[owned, owned, flat, flat, edge_spec, short_spec, skip_spec],
        out_specs=[flat, flat, edge_spec, tail_spec]
        + [pl.BlockSpec((INNER_PEERS, 8, width), lambda i: (0, 0, 0))] * far,
        out_shape=[shape((rows, channels), bf16)] * 2
        + [shape((2, channels), f32), shape((16, channels), bf16)]
        + [shape((INNER_PEERS, 8, width), f32)] * far,
        scratch_shapes=[pltpu.VMEM((2, rows + 8, 128), f32)] * 2 + [pltpu.VMEM((peers, 8, width), f32)],
        compiler_params=params(),
        cost_estimate=cost(30 * rows * channels, 12 * rows * channels),
        name="finish",
    )(back_got, gated, key_feat, value_raw, edge, short_filter, skip_row)

    head_got = passed_along(head, "ctx", -1)
    short_grad, head_got, value_grad = summed_at_owner(short_parts, head_got, value_grad)
    value_grad = pl.pallas_call(
        seam_kernel,
        grid=(1,),
        in_specs=[whole(16), whole(2), whole(3), hbm],
        out_specs=pl.BlockSpec((16, channels), lambda i: (rows // 16 - 1, 0)),
        out_shape=shape((rows, channels), bf16),
        input_output_aliases={3: 0},
        compiler_params=params(),
        cost_estimate=cost(5 * 16 * channels, 6 * 16 * channels),
        name="seam",
    )(tail, head_got, short_filter, value_grad)
    return query_grad, key_grad, value_grad, filter_grad, skip_grad.reshape(width), short_grad[:3]


def per_device(query_feat, key_feat, value_raw, conv_out, out_grad, filter_taps, short_filter, skip_gain):
    rows, channels = query_feat.shape
    peers = lax.axis_size("ctx")
    width = channels // peers
    fits = (
        peers % INNER_PEERS == 0
        and peers & (peers - 1) == 0
        and rows == INNER
        and width % 256 == 0
        and peers in (8, 16)
    )
    plan = kernel_plan if fits else general_plan
    return plan(query_feat, key_feat, value_raw, conv_out, out_grad, filter_taps, short_filter, skip_gain)


def solution(mesh):
    in_specs = (
        P(("groups", "ctx"), None),
        P(("groups", "ctx"), None),
        P(("groups", "ctx"), None),
        P(("groups", "ctx"), None),
        P(("groups", "ctx"), None),
        P("ctx", None),
        P(),
        P(),
    )
    out_specs = (
        P(("groups", "ctx"), None),
        P(("groups", "ctx"), None),
        P(("groups", "ctx"), None),
        P(("groups", "ctx"), None),
        P(("groups", "ctx")),
        P(None, ("groups", "ctx")),
    )
    return jax.shard_map(
        per_device, mesh=mesh, in_specs=in_specs, out_specs=out_specs, check_vma=False
    )
```

```python
import functools
import math

import jax
import jax.numpy as jnp
import numpy as np
from jax import lax
from jax.experimental import pallas as pl
from jax.experimental.pallas import tpu as pltpu
from jax.sharding import PartitionSpec as P

PRECISE = lax.Precision.HIGH


def passed_along(block, axis, distance):
    devices = range(lax.axis_size(axis))
    route = [(i - distance, i) for i in devices if i - distance in devices]
    return lax.ppermute(block, axis, route)


def dft_pair(row_count, col_count, period):
    row_index = lax.iota(jnp.int32, row_count)[:, None]
    col_index = lax.iota(jnp.int32, col_count)[None, :]
    phase = (row_index * col_index % period).astype(jnp.float32) * (-2.0 * math.pi / period)
    return (jnp.cos(phase), jnp.sin(phase))


def make_tables(inner, outer):
    half = outer // 2
    outer_cos, outer_sin = dft_pair(outer, half, outer)
    twist_cos, twist_sin = dft_pair(outer, inner, outer * inner)
    inner_cos, inner_sin = dft_pair(inner, inner, inner)
    real_outer = jnp.stack([outer_cos, outer_sin], 1)
    complex_outer = jnp.stack(
        [jnp.stack([outer_cos, -outer_sin], 1), jnp.stack([outer_sin, outer_cos], 1)], 1
    )
    inner_ahead = jnp.block([[inner_cos, inner_sin], [-inner_sin, inner_cos]])
    inner_back = jnp.block([[inner_cos, -inner_sin], [inner_sin, inner_cos]])
    outer_back = jnp.stack(
        [jnp.stack([outer_cos, outer_sin], 0), jnp.stack([-outer_sin, outer_cos], 0)], 0
    )
    return (real_outer, complex_outer, twist_cos, twist_sin, inner_ahead, inner_back, outer_back)


def twist_ahead(values, twist_cos, twist_sin):
    real_part = values[:, :, 0]
    imag_part = values[:, :, 1]
    return jnp.stack(
        [
            real_part * twist_cos - imag_part * twist_sin,
            real_part * twist_sin + imag_part * twist_cos,
        ],
        2,
    )


def twist_back(values, twist_cos, twist_sin):
    real_part = values[:, :, 0]
    imag_part = values[:, :, 1]
    return jnp.stack(
        [
            real_part * twist_cos + imag_part * twist_sin,
            imag_part * twist_cos - real_part * twist_sin,
        ],
        2,
    )


def inner_section(values, table):
    width, outer = (values.shape[0], values.shape[1])
    flat = values.reshape(width, outer, table.shape[0])
    return jnp.einsum(
        "wkc,cd->wkd", flat, table, precision=PRECISE, preferred_element_type=jnp.float32
    )


def real_spectrum(signal, tables):
    real_outer, complex_outer, twist_cos, twist_sin, inner_ahead, inner_back, outer_back = tables
    half = real_outer.shape[2]
    inner = twist_cos.shape[1]
    blocked = signal.reshape(signal.shape[0], half, inner)
    first = jnp.einsum(
        "wab,kra->wkrb", blocked, real_outer, precision=PRECISE, preferred_element_type=jnp.float32
    )
    return inner_section(twist_ahead(first, twist_cos, twist_sin), inner_ahead)


def complex_spectrum(signal_re, signal_im, tables):
    real_outer, complex_outer, twist_cos, twist_sin, inner_ahead, inner_back, outer_back = tables
    half = real_outer.shape[2]
    inner = twist_cos.shape[1]
    width = signal_re.shape[0]
    stacked = jnp.stack(
        [signal_re.reshape(width, half, inner), signal_im.reshape(width, half, inner)], 1
    )
    first = jnp.einsum(
        "wsab,krsa->wkrb",
        stacked,
        complex_outer,
        precision=PRECISE,
        preferred_element_type=jnp.float32,
    )
    return inner_section(twist_ahead(first, twist_cos, twist_sin), inner_ahead)


def inverse_spectrum(packed, tables):
    real_outer, complex_outer, twist_cos, twist_sin, inner_ahead, inner_back, outer_back = tables
    outer = twist_cos.shape[0]
    inner = twist_cos.shape[1]
    half = real_outer.shape[2]
    width = packed.shape[0]
    back = inner_section(packed, inner_back).reshape(width, outer, 2, inner)
    turned = twist_back(back, twist_cos, twist_sin)
    result = jnp.einsum(
        "wksb,rska->wrab", turned, outer_back, precision=PRECISE, preferred_element_type=jnp.float32
    )
    scale = 1.0 / (outer * inner)
    return (
        (result[:, 0] * scale).reshape(width, half * inner),
        (result[:, 1] * scale).reshape(width, half * inner),
    )


def spectral_block(gated_rows, mixed_rows, filter_rows, tables):
    inner = tables[2].shape[1]
    gated_spec = real_spectrum(gated_rows.astype(jnp.float32), tables)
    joint_spec = complex_spectrum(
        filter_rows.astype(jnp.float32), -mixed_rows.astype(jnp.float32), tables
    )
    gated_re = gated_spec[:, :, :inner]
    gated_im = gated_spec[:, :, inner:]
    joint_re = joint_spec[:, :, :inner]
    joint_im = joint_spec[:, :, inner:]
    product_re = joint_re * gated_re + joint_im * gated_im
    product_im = joint_re * gated_im - joint_im * gated_re
    product = jnp.concatenate([product_re, product_im], 2)
    result_re, result_im = inverse_spectrum(product, tables)
    return (result_re.astype(jnp.bfloat16), result_im.astype(jnp.bfloat16))


def general_plan(
    query_feat, key_feat, value_raw, conv_out, out_grad, filter_taps, short_filter, skip_gain
):
    rows = query_feat.shape[0]
    peers = lax.axis_size("ctx")
    before = passed_along(value_raw[rows - 2 :], "ctx", 1)
    padded = jnp.concatenate([before, value_raw], 0).astype(jnp.float32)
    value_conv = (
        short_filter[0] * padded[2:]
        + short_filter[1] * padded[1:-1]
        + short_filter[2] * padded[:-2]
    )
    mixed = (key_feat.astype(jnp.float32) * value_conv).astype(jnp.bfloat16)
    gated = (out_grad.astype(jnp.float32) * query_feat.astype(jnp.float32)).astype(jnp.bfloat16)
    query_grad = (out_grad.astype(jnp.float32) * conv_out.astype(jnp.float32)).astype(jnp.bfloat16)
    skip_part = jnp.sum(gated.astype(jnp.float32) * mixed.astype(jnp.float32), axis=0)
    tables = make_tables(rows, 2 * peers)
    gated_chan = gated.T
    mixed_chan = mixed.T
    sent_gated, sent_mixed = (
        lax.all_to_all(gated_chan, "ctx", split_axis=0, concat_axis=1, tiled=True),
        lax.all_to_all(mixed_chan, "ctx", split_axis=0, concat_axis=1, tiled=True),
    )
    back_rows, filter_grad = spectral_block(sent_gated, sent_mixed, filter_taps, tables)
    back_chan = lax.all_to_all(back_rows, "ctx", split_axis=1, concat_axis=0, tiled=True)
    conv_back = back_chan.T
    mixed_grad = conv_back.astype(jnp.float32) + skip_gain * gated.astype(jnp.float32)
    key_grad = (mixed_grad * value_conv).astype(jnp.bfloat16)
    feature_grad = (mixed_grad * key_feat.astype(jnp.float32)).astype(jnp.bfloat16)
    after = passed_along(feature_grad[:2], "ctx", -1)
    extended = jnp.concatenate([feature_grad, after], 0).astype(jnp.float32)
    value_grad = (
        short_filter[0] * extended[:-2]
        + short_filter[1] * extended[1:-1]
        + short_filter[2] * extended[2:]
    ).astype(jnp.bfloat16)
    feature_wide = extended[:-2]
    short_part = jnp.stack(
        [
            jnp.sum(feature_wide * padded[2:], axis=0),
            jnp.sum(feature_wide * padded[1:-1], axis=0),
            jnp.sum(feature_wide * padded[:-2], axis=0),
        ]
    )
    skip_grad, short_grad = (
        lax.psum_scatter(skip_part, "ctx", scatter_dimension=0, tiled=True),
        lax.psum_scatter(short_part, "ctx", scatter_dimension=1, tiled=True),
    )
    return (query_grad, key_grad, value_grad, filter_grad, skip_grad, short_grad)


INNER = 128
INNER_PEERS = 4


def half_spectrum(values, length):
    if length == 2:
        return [(values[0], None), (values[0], None)]
    even = half_spectrum(values[0::2], length // 2)
    odd = half_spectrum(values[1::2], length // 2)
    quarter = length // 4
    bins = [None] * (length // 2 + 1)
    bins[0] = (even[0][0] + odd[0][0], None)
    bins[length // 2] = (even[0][0] - odd[0][0], None)
    bins[quarter] = (even[quarter][0], -odd[quarter][0])
    for k in range(1, quarter):
        c = math.cos(2.0 * math.pi * k / length)
        s = math.sin(2.0 * math.pi * k / length)
        odd_re, odd_im = odd[k]
        even_re, even_im = even[k]
        if 2 * k == quarter:
            turn_re = (odd_re + odd_im) * c
            turn_im = (odd_im - odd_re) * c
        else:
            turn_re = odd_re * c + odd_im * s
            turn_im = odd_im * c - odd_re * s
        bins[k] = (even_re + turn_re, even_im + turn_im)
        bins[length // 2 - k] = (even_re - turn_re, turn_im - even_im)
    return bins


def first_half(bins, length):
    if length == 2:
        return [bins[0][0] + bins[1][0]]
    half = length // 2
    quarter = length // 4
    even = [None] * (quarter + 1)
    odd = [None] * (quarter + 1)
    even[0] = (bins[0][0] + bins[half][0], None)
    odd[0] = (bins[0][0] - bins[half][0], None)
    even[quarter] = (2.0 * bins[quarter][0], None)
    odd[quarter] = (-2.0 * bins[quarter][1], None)
    for k in range(1, quarter):
        c = math.cos(2.0 * math.pi * k / length)
        s = math.sin(2.0 * math.pi * k / length)
        near_re, near_im = bins[k]
        far_re, far_im = bins[half - k]
        even[k] = (near_re + far_re, near_im - far_im)
        gap_re = near_re - far_re
        gap_im = near_im + far_im
        if 2 * k == quarter:
            odd[k] = ((gap_re - gap_im) * c, (gap_re + gap_im) * c)
        else:
            odd[k] = (gap_re * c - gap_im * s, gap_re * s + gap_im * c)
    result = [None] * half
    result[0::2] = first_half(even, half)
    result[1::2] = first_half(odd, half)
    return result


def spectrum_tables(outer):
    size = outer * INNER
    near = np.arange(outer // 2 + 1)[:, None, None]
    place = np.arange(INNER)
    angle = -2.0 * np.pi * (
        (near * place[None, None, :]) / size + place[None, :, None] * place[None, None, :] / INNER
    )
    c, s = np.cos(angle), np.sin(angle)
    ahead = np.concatenate(
        [np.concatenate([c, -s], 2), np.concatenate([s, c], 2)], 1
    )
    back = np.swapaxes(ahead, 1, 2) / size
    return ahead.astype(jnp.bfloat16), back.astype(jnp.bfloat16)


def outer_ahead(load, z_ref, outer, width):
    def step(chunk, carry):
        row = pl.multiple_of(chunk * 16, 16)
        for lane in range(0, width, 128):
            values = [load(a, row, lane).astype(jnp.float32) for a in range(outer // 2)]
            bins = half_spectrum(values, outer)
            for k, (re, im) in enumerate(bins):
                im = jnp.zeros_like(re) if im is None else im
                z_ref[k, pl.ds(row, 16), lane : lane + 128] = re.astype(jnp.bfloat16)
                z_ref[k, pl.ds(INNER + row, 16), lane : lane + 128] = im.astype(jnp.bfloat16)
        return carry

    lax.fori_loop(0, INNER // 16, step, 0)


def outer_back(u_ref, store, outer, width):
    def step(chunk, carry):
        row = pl.multiple_of(chunk * 16, 16)
        for lane in range(0, width, 128):
            bins = []
            for k in range(outer // 2 + 1):
                re = u_ref[k, pl.ds(row, 16), lane : lane + 128]
                im = u_ref[k, pl.ds(INNER + row, 16), lane : lane + 128]
                bins.append((re, im))
            for a, value in enumerate(first_half(bins, outer)):
                store(a, row, lane, value)
        return carry

    lax.fori_loop(0, INNER // 16, step, 0)


def correlate_bin(first, gated):
    first_re, first_im = first[:INNER], first[INNER:]
    gated_re, gated_im = gated[:INNER], gated[INNER:]
    return jnp.concatenate(
        [
            first_re * gated_re + first_im * gated_im,
            first_re * gated_im - first_im * gated_re,
        ],
        0,
    ).astype(jnp.bfloat16)


def dot32(a, b):
    return jnp.dot(a, b, preferred_element_type=jnp.float32)


def filter_kernel(taps_ref, ahead_ref, spec_ref, rows_ref, z_ref, *, outer, width):
    for a in range(outer // 2):
        piece = taps_ref[:, a * INNER : (a + 1) * INNER].astype(jnp.float32)
        rows_ref[a * INNER : (a + 1) * INNER, :] = piece.T
    outer_ahead(
        lambda a, row, lane: rows_ref[pl.ds(a * INNER + row, 16), lane : lane + 128],
        z_ref, outer, width,
    )

    for k in range(outer // 2 + 1):
        spec_ref[k] = dot32(ahead_ref[k], z_ref[k]).astype(jnp.bfloat16)


def begun(source, target, semaphore):
    copy = pltpu.make_async_copy(source, target, semaphore)
    copy.start()
    return copy


def conv_kernel(
    gated_hbm, filter_hbm, ahead_hbm, back_hbm, skip_ref, conv_ref, spec_hbm,
    gated_ref, filter_ref, ahead_ref, back_ref, spec_ref, z_ref, u_ref, sems, *, outer, width,
):
    gated_in = begun(gated_hbm, gated_ref, sems.at[0])
    ahead_in = begun(ahead_hbm, ahead_ref, sems.at[1])
    filter_in = begun(filter_hbm, filter_ref, sems.at[2])
    back_in = begun(back_hbm, back_ref, sems.at[3])
    gated_in.wait()
    outer_ahead(
        lambda a, row, lane: gated_ref[pl.ds(a * INNER + row, 16), lane : lane + 128],
        z_ref, outer, width,
    )
    ahead_in.wait()
    filter_in.wait()
    for k in range(outer // 2 + 1):
        gated = dot32(ahead_ref[k], z_ref[k])
        spec_ref[k] = gated.astype(jnp.bfloat16)
        z_ref[k] = correlate_bin(filter_ref[k].astype(jnp.float32), gated)
    spec_out = begun(spec_ref, spec_hbm, sems.at[4])
    back_in.wait()
    for k in range(outer // 2 + 1):
        u_ref[k] = dot32(back_ref[k], z_ref[k])

    first = lax.axis_index("ctx") * width

    def store(a, row, lane, value):
        place = pl.ds(a * INNER + row, 16)
        skip = skip_ref[:, pl.ds(pl.multiple_of(first + lane, 128), 128)]
        gated = gated_ref[place, lane : lane + 128].astype(jnp.float32)
        conv_ref[place, lane : lane + 128] = (value + skip * gated).astype(jnp.bfloat16)

    outer_back(u_ref, store, outer, width)
    spec_out.wait()


def grad_kernel(*refs, outer, width):
    far = outer // 2 // INNER_PEERS
    place_hbm, refs = refs[:far], refs[far:]
    near_hbm, refs = refs[: INNER_PEERS - 1], refs[INNER_PEERS - 1 :]
    far_hbm, refs = refs[: far - 1], refs[far - 1 :]
    gated_hbm, spec_hbm, ahead_hbm, back_hbm, grad_ref, skip_ref = refs[:6]
    mixed_ref, gated_ref, spec_ref, ahead_ref, back_ref, z_ref, u_ref, rows_ref, sems = refs[6:]
    slabs = outer // 2
    me = lax.axis_index("ctx")
    own_row, own_place = me // INNER_PEERS, me % INNER_PEERS
    mixed_in = []
    for d in range(far):
        for e in range(INNER_PEERS):
            if e == 0:
                source = place_hbm[d]
            elif d == 0:
                source = near_hbm[e - 1].at[own_row]
            else:
                source = far_hbm[d - 1].at[e - 1]
            slab = (own_row ^ d) * INNER_PEERS + (own_place ^ e)
            mixed_in.append(begun(source, mixed_ref.at[slab], sems.at[4 + len(mixed_in)]))
    ahead_in = begun(ahead_hbm, ahead_ref, sems.at[0])
    spec_in = begun(spec_hbm, spec_ref, sems.at[1])
    back_in = begun(back_hbm, back_ref, sems.at[2])
    gated_in = begun(gated_hbm, gated_ref, sems.at[3])
    for copy in mixed_in:
        copy.wait()
    outer_ahead(
        lambda a, row, lane: mixed_ref[a, pl.ds(row, 16), lane : lane + 128],
        z_ref, outer, width,
    )
    ahead_in.wait()
    spec_in.wait()
    for k in range(outer // 2 + 1):
        mixed = dot32(ahead_ref[k], z_ref[k])
        z_ref[k] = correlate_bin(mixed, spec_ref[k].astype(jnp.float32))
    back_in.wait()
    for k in range(outer // 2 + 1):
        u_ref[k] = dot32(back_ref[k], z_ref[k])

    def store(a, row, lane, value):
        rows_ref[pl.ds(a * INNER + row, 16), lane : lane + 128] = value

    outer_back(u_ref, store, outer, width)
    for a in range(slabs):
        grad_ref[:, a * INNER : (a + 1) * INNER] = rows_ref[
            a * INNER : (a + 1) * INNER, :
        ].T.astype(jnp.bfloat16)
    gated_in.wait()

    def add(a, total):
        place = pl.ds(pl.multiple_of(a * INNER, INNER), INNER)
        part = gated_ref[place, :].astype(jnp.float32) * mixed_ref[a].astype(jnp.float32)
        return total + jnp.sum(part.reshape(INNER // 8, 8, width), axis=0)

    total = lax.fori_loop(0, slabs, add, jnp.zeros((8, width), jnp.float32))
    skip_ref[...] = jnp.sum(total, axis=0, keepdims=True)


def regroup_kernel(*refs):
    near, far = refs[: INNER_PEERS - 1], refs[INNER_PEERS - 1 :]
    own_row = lax.axis_index("ctx") // INNER_PEERS
    for d in range(1, len(far) + 1):
        for e in range(1, INNER_PEERS):
            far[d - 1][e - 1] = near[e - 1][own_row ^ d]


def shifted_down(values, distance, edge):
    moved = pltpu.roll(values, distance, 0)
    row = lax.broadcasted_iota(jnp.int32, values.shape, 0)
    for i in range(distance):
        source = edge.shape[0] - distance + i
        moved = jnp.where(row == i, edge[source : source + 1], moved)
    return moved


def shifted_up(values, distance, edge):
    count = values.shape[0]
    moved = pltpu.roll(values, count - distance, 0)
    row = lax.broadcasted_iota(jnp.int32, values.shape, 0)
    for i in range(distance):
        moved = jnp.where(row == count - distance + i, edge[i : i + 1], moved)
    return moved


def gate_kernel(grad_ref, query_ref, value_ref, gated_ref, last_ref, *, width):
    last_ref[...] = value_ref[...].astype(jnp.float32)[value_ref.shape[0] - 2 :]
    for j in range(gated_ref.shape[0]):
        cols = slice(j * width, (j + 1) * width)
        gated_ref[j] = (
            grad_ref[:, cols].astype(jnp.float32) * query_ref[:, cols].astype(jnp.float32)
        ).astype(jnp.bfloat16)


def mix_kernel(key_ref, value_ref, edge_ref, short_ref, grad_ref, conv_ref, *rest, width):
    near_refs, place_refs = rest[: INNER_PEERS - 1], rest[INNER_PEERS - 1 : -3]
    query_grad_ref, behind, mixed_ref = rest[-3:]
    rows = key_ref.shape[0]
    owners = key_ref.shape[1] // width
    step = pl.program_id(0)
    for j in range(owners):
        for lane in range(0, width, 128):
            slot = (j * width + lane) // 128 % 2
            cols = slice(j * width + lane, j * width + lane + 128)
            value = value_ref[:, cols].astype(jnp.float32)
            behind[slot, 6:8] = edge_ref[:, cols]
            behind[slot, 8 : 8 + rows] = value
            conv = (
                short_ref[0:1, cols] * value
                + short_ref[1:2, cols] * behind[slot, 7 : 7 + rows]
                + short_ref[2:3, cols] * behind[slot, 6 : 6 + rows]
            )
            mixed_ref[step * owners + j, :, lane : lane + 128] = (
                key_ref[:, cols].astype(jnp.float32) * conv
            ).astype(jnp.bfloat16)
            query_grad_ref[:, cols] = (
                grad_ref[:, cols].astype(jnp.float32) * conv_ref[:, cols].astype(jnp.float32)
            ).astype(jnp.bfloat16)

    @pl.when(step == pl.num_programs(0) - 1)
    def _():
        me = lax.axis_index("ctx")
        own_row, place = me // INNER_PEERS, me % INNER_PEERS
        for e, near_ref in enumerate(near_refs, 1):
            for row in range(near_ref.shape[0]):
                near_ref[row] = mixed_ref[row * INNER_PEERS + (place ^ e)]
        for d, place_ref in enumerate(place_refs):
            place_ref[...] = mixed_ref[(own_row ^ d) * INNER_PEERS + place]


def sums_kernel(
    back_ref, key_ref, value_ref, edge_ref, head_ref, tail_ref, *rest, width
):
    part_refs, behind, sums_ref = rest[:-2], rest[-2], rest[-1]
    rows = key_ref.shape[0]
    owners = back_ref.shape[0]
    step = pl.program_id(0)
    for j in range(owners):
        for lane in range(0, width, 128):
            slot = (j * width + lane) // 128 % 2
            cols = slice(j * width + lane, j * width + lane + 128)
            lanes = slice(lane, lane + 128)
            value = value_ref[:, cols].astype(jnp.float32)
            behind[slot, 6:8] = edge_ref[:, cols]
            behind[slot, 8 : 8 + rows] = value
            mixed_grad = back_ref[j, :, lanes].astype(jnp.float32)
            feature = (mixed_grad * key_ref[:, cols].astype(jnp.float32)).astype(jnp.bfloat16)
            tail_ref[:, cols] = feature[rows - 16 :]
            feature = feature.astype(jnp.float32)
            head_ref[:, cols] = feature[:2]
            shifted = (value, behind[slot, 7 : 7 + rows], behind[slot, 6 : 6 + rows])
            sums_ref[step * owners + j, :, lanes] = jnp.concatenate(
                [jnp.sum(feature * other, axis=0, keepdims=True) for other in shifted]
                + [jnp.zeros((5, 128), jnp.float32)],
                0,
            )

    @pl.when(step == pl.num_programs(0) - 1)
    def _():
        own = lax.axis_index("ctx") // INNER_PEERS
        for d, part_ref in enumerate(part_refs):
            part_ref[...] = sums_ref[pl.ds((own ^ d) * INNER_PEERS, INNER_PEERS)]


def finish_kernel(
    back_ref, key_ref, value_ref, edge_ref, short_ref,
    key_grad_ref, value_grad_ref, behind, ahead, *, width,
):
    rows = key_ref.shape[0]
    for j in range(back_ref.shape[0]):
        for lane in range(0, width, 128):
            slot = (j * width + lane) // 128 % 2
            cols = slice(j * width + lane, j * width + lane + 128)
            lanes = slice(lane, lane + 128)
            short = [short_ref[i : i + 1, cols] for i in range(3)]
            value = value_ref[:, cols].astype(jnp.float32)
            behind[slot, 6:8] = edge_ref[:, cols]
            behind[slot, 8 : 8 + rows] = value
            mixed_grad = back_ref[j, :, lanes].astype(jnp.float32)
            conv = (
                short[0] * value
                + short[1] * behind[slot, 7 : 7 + rows]
                + short[2] * behind[slot, 6 : 6 + rows]
            )
            key_grad_ref[:, cols] = (mixed_grad * conv).astype(jnp.bfloat16)
            feature = (mixed_grad * key_ref[:, cols].astype(jnp.float32)).astype(jnp.bfloat16)
            feature = feature.astype(jnp.float32)
            ahead[slot, 0:rows] = feature
            ahead[slot, rows : rows + 8] = jnp.zeros((8, 128), jnp.float32)
            value_grad_ref[:, cols] = (
                short[0] * feature
                + short[1] * ahead[slot, 1 : 1 + rows]
                + short[2] * ahead[slot, 2 : 2 + rows]
            ).astype(jnp.bfloat16)


def seam_kernel(tail_ref, head_ref, short_ref, done_ref, value_grad_ref):
    feature = tail_ref[...].astype(jnp.float32)
    head = head_ref[...]
    value_grad_ref[...] = (
        short_ref[0:1] * feature
        + short_ref[1:2] * shifted_up(feature, 1, head)
        + short_ref[2:3] * shifted_up(feature, 2, head)
    ).astype(jnp.bfloat16)


def exchanged(block):
    return lax.all_to_all(block, "ctx", split_axis=0, concat_axis=0, tiled=True)


def paired(block, distance):
    return lax.ppermute(block, "ctx", [(i, i ^ distance) for i in range(lax.axis_size("ctx"))])


def summed_at_owner(parts, *beside):
    place = lax.axis_index("ctx") % INNER_PEERS
    got = [parts[0]] + [paired(parts[d], d * INNER_PEERS) for d in range(1, len(parts))]
    rows = sum(got[1:], got[0])
    rows, beside = lax.optimization_barrier((rows, beside))
    total = lax.dynamic_index_in_dim(rows, place, 0, keepdims=False)
    for distance in range(1, INNER_PEERS):
        other = lax.dynamic_index_in_dim(rows, place ^ distance, 0, keepdims=False)
        total = total + paired(other, distance)
    return total, *beside


def after(value, *others):
    return lax.optimization_barrier((value,) + others)[0]


def in_hbm(*values):
    return [pltpu.with_memory_space_constraint(value, pltpu.HBM) for value in values]


def params(mib=63):
    return pltpu.CompilerParams(vmem_limit_bytes=mib * 1024 * 1024)


BESIDE_EXCHANGE = 40_000_000_000
WHOLE_EXCHANGE = 100_000_000_000


def cost(flops, size):
    return pl.CostEstimate(flops=flops, bytes_accessed=size, transcendentals=0)


def kernel_plan(
    query_feat, key_feat, value_raw, conv_out, out_grad, filter_taps, short_filter, skip_gain
):
    rows, channels = query_feat.shape
    peers = lax.axis_size("ctx")
    width = channels // peers
    seq = rows * peers
    outer = 2 * seq // INNER
    bins = outer // 2 + 1
    steps = 2
    group = peers // steps
    span = group * width
    far = peers // INNER_PEERS
    any_place = pl.BlockSpec(memory_space=pl.ANY)
    hbm = pl.BlockSpec(memory_space=pltpu.HBM)
    bf16, f32 = jnp.bfloat16, jnp.float32
    shape = jax.ShapeDtypeStruct
    skip_row = skip_gain.reshape(1, channels)
    ahead, back = (jnp.asarray(t) for t in spectrum_tables(outer))

    flat = pl.BlockSpec((rows, span), lambda i: (0, i))
    owned = pl.BlockSpec((group, rows, width), lambda i: (i, 0, 0))
    edge_spec = pl.BlockSpec((2, span), lambda i: (0, i))
    tail_spec = pl.BlockSpec((16, span), lambda i: (0, i))
    short_spec = pl.BlockSpec((3, span), lambda i: (0, i))

    gated, last = pl.pallas_call(
        functools.partial(gate_kernel, width=width),
        grid=(steps,),
        in_specs=[flat, flat, pl.BlockSpec((16, span), lambda i: (rows // 16 - 1, i))],
        out_specs=[owned, edge_spec],
        out_shape=[shape((peers, rows, width), bf16), shape((2, channels), f32)],
        compiler_params=params(),
        cost_estimate=cost(rows * channels, 6 * rows * channels),
        name="gate",
    )(out_grad, query_feat, value_raw)

    gated_got = exchanged(gated.reshape(seq, width))

    spec_shape = shape((bins, 2 * INNER, width), bf16)
    z_scratch = pltpu.VMEM((bins, 2 * INNER, width), bf16)
    u_scratch = pltpu.VMEM((bins, 2 * INNER, width), f32)
    table_scratch = pltpu.VMEM((bins, 2 * INNER, 2 * INNER), bf16)
    table_bytes = 8 * bins * INNER * INNER
    spec_bytes = 4 * bins * INNER * width
    work = 2 * bins * (2 * INNER) ** 2 * width
    edge = passed_along(last, "ctx", 1)
    whole = lambda size: pl.BlockSpec((size, channels), lambda i: (0, 0))
    shift_scratch = pltpu.VMEM((2, rows + 8, 128), f32)
    near_spec = pl.BlockSpec((far, rows, width), lambda i: (0, 0, 0))
    far_spec = pl.BlockSpec((INNER_PEERS - 1, rows, width), lambda i: (0, 0, 0))
    place_spec = pl.BlockSpec((rows, width), lambda i: (0, 0))
    *mixed, query_grad = pl.pallas_call(
        functools.partial(mix_kernel, width=width),
        grid=(steps,),
        in_specs=[flat, flat, edge_spec, short_spec, flat, flat],
        out_specs=[near_spec] * (INNER_PEERS - 1) + [place_spec] * far + [flat],
        out_shape=[shape((far, rows, width), bf16)] * (INNER_PEERS - 1)
        + [shape((rows, width), bf16)] * far
        + [shape((rows, channels), bf16)],
        scratch_shapes=[shift_scratch, pltpu.VMEM((peers, rows, width), bf16)],
        compiler_params=params(),
        cost_estimate=cost(BESIDE_EXCHANGE, 12 * rows * channels),
        name="mix",
    )(key_feat, value_raw, edge, short_filter, out_grad, conv_out)
    near = [paired(mixed[e - 1], e) for e in range(1, INNER_PEERS)]
    placed = mixed[INNER_PEERS - 1 :]
    placed = [placed[0]] + [paired(placed[d], d * INNER_PEERS) for d in range(1, far)]
    across = pl.pallas_call(
        regroup_kernel,
        grid=(1,),
        in_specs=[near_spec] * (INNER_PEERS - 1),
        out_specs=[far_spec] * (far - 1),
        out_shape=[shape((INNER_PEERS - 1, rows, width), bf16)] * (far - 1),
        compiler_params=params(),
        cost_estimate=cost(0, 4 * seq * width),
        name="regroup",
    )(*near)
    filter_taps, query_grad = lax.optimization_barrier((filter_taps, query_grad))
    filter_spec = pl.pallas_call(
        functools.partial(filter_kernel, outer=outer, width=width),
        out_shape=spec_shape,
        scratch_shapes=[pltpu.VMEM((seq, width), f32), z_scratch],
        compiler_params=params(),
        cost_estimate=cost(BESIDE_EXCHANGE, table_bytes + spec_bytes + 2 * seq * width),
        name="filter_spectrum",
    )(filter_taps, ahead)


    *across, gated_got = lax.optimization_barrier((*across, gated_got))
    across = [paired(across[d - 1], d * INNER_PEERS) for d in range(1, far)]

    conv_back, gated_spec = pl.pallas_call(
        functools.partial(conv_kernel, outer=outer, width=width),
        in_specs=[hbm] * 4 + [pl.BlockSpec(memory_space=pltpu.VMEM)],
        out_specs=[pl.BlockSpec(memory_space=pltpu.VMEM), hbm],
        out_shape=(shape((seq, width), bf16), spec_shape),
        scratch_shapes=[pltpu.VMEM((seq, width), bf16), z_scratch, table_scratch, table_scratch, z_scratch]
        + [z_scratch, u_scratch, pltpu.SemaphoreType.DMA((5,))],
        compiler_params=params(),
        cost_estimate=cost(BESIDE_EXCHANGE, 2 * table_bytes + 2 * spec_bytes + 4 * seq * width),
        name="conv_back",
    )(gated_got, filter_spec, ahead, back, skip_row)

    back_got = exchanged(conv_back).reshape(peers, rows, width)

    filter_grad, skip_grad = pl.pallas_call(
        functools.partial(grad_kernel, outer=outer, width=width),
        in_specs=[hbm] * (INNER_PEERS + 2 * far + 2),
        out_shape=[shape((width, seq), bf16), shape((1, width), f32)],
        scratch_shapes=[
            pltpu.VMEM((peers, rows, width), bf16),
            pltpu.VMEM((seq, width), bf16),
            z_scratch,
            table_scratch,
            table_scratch,
            z_scratch,
            u_scratch,
            pltpu.VMEM((seq, width), f32),
            pltpu.SemaphoreType.DMA((peers + 4,)),
        ],
        compiler_params=params(30),
        cost_estimate=cost(WHOLE_EXCHANGE, 2 * table_bytes + spec_bytes),
        name="filter_grad",
    )(*in_hbm(*placed, *near, *across, gated_got, gated_spec, ahead, back))
    back_got, filter_grad, skip_grad = lax.optimization_barrier((back_got, filter_grad, skip_grad))

    head, tail, *short_parts = pl.pallas_call(
        functools.partial(sums_kernel, width=width),
        grid=(steps,),
        in_specs=[owned, flat, flat, edge_spec],
        out_specs=[edge_spec, tail_spec]
        + [pl.BlockSpec((INNER_PEERS, 8, width), lambda i: (0, 0, 0))] * far,
        out_shape=[pltpu.HBM((2, channels), f32), pltpu.HBM((16, channels), bf16)]
        + [pltpu.HBM((INNER_PEERS, 8, width), f32)] * far,
        scratch_shapes=[shift_scratch, pltpu.VMEM((peers, 8, width), f32)],
        compiler_params=params(30),
        cost_estimate=cost(20 * rows * channels, 8 * rows * channels),
        name="sums",
    )(*in_hbm(back_got), key_feat, value_raw, edge)

    key_grad, value_grad = pl.pallas_call(
        functools.partial(finish_kernel, width=width),
        grid=(steps,),
        in_specs=[owned, flat, flat, edge_spec, short_spec],
        out_specs=[flat, flat],
        out_shape=[pltpu.HBM((rows, channels), bf16)] * 2,
        scratch_shapes=[shift_scratch] * 2,
        compiler_params=params(30),
        cost_estimate=cost(30 * rows * channels, 12 * rows * channels),
        name="finish",
    )(*in_hbm(back_got), key_feat, value_raw, edge, short_filter)

    head_got = passed_along(head, "ctx", -1)
    short_grad, head_got, value_grad = summed_at_owner(short_parts, head_got, value_grad)
    value_grad = pl.pallas_call(
        seam_kernel,
        grid=(1,),
        in_specs=[whole(16), whole(2), whole(3), hbm],
        out_specs=pl.BlockSpec((16, channels), lambda i: (rows // 16 - 1, 0)),
        out_shape=shape((rows, channels), bf16),
        input_output_aliases={3: 0},
        compiler_params=params(),
        cost_estimate=cost(5 * 16 * channels, 6 * 16 * channels),
        name="seam",
    )(tail, head_got, short_filter, value_grad)
    return query_grad, key_grad, value_grad, filter_grad, skip_grad.reshape(width), short_grad[:3]


def per_device(query_feat, key_feat, value_raw, conv_out, out_grad, filter_taps, short_filter, skip_gain):
    rows, channels = query_feat.shape
    peers = lax.axis_size("ctx")
    width = channels // peers
    fits = (
        peers % INNER_PEERS == 0
        and peers & (peers - 1) == 0
        and rows == INNER
        and width % 256 == 0
        and peers in (8, 16)
    )
    plan = kernel_plan if fits else general_plan
    return plan(query_feat, key_feat, value_raw, conv_out, out_grad, filter_taps, short_filter, skip_gain)


def solution(mesh):
    in_specs = (
        P(("groups", "ctx"), None),
        P(("groups", "ctx"), None),
        P(("groups", "ctx"), None),
        P(("groups", "ctx"), None),
        P(("groups", "ctx"), None),
        P("ctx", None),
        P(),
        P(),
    )
    out_specs = (
        P(("groups", "ctx"), None),
        P(("groups", "ctx"), None),
        P(("groups", "ctx"), None),
        P(("groups", "ctx"), None),
        P(("groups", "ctx")),
        P(None, ("groups", "ctx")),
    )
    return jax.shard_map(
        per_device, mesh=mesh, in_specs=in_specs, out_specs=out_specs, check_vma=False
    )
```

```python
import functools
import math

import jax
import jax.numpy as jnp
import numpy as np
from jax import lax
from jax.experimental import pallas as pl
from jax.experimental.pallas import tpu as pltpu
from jax.sharding import PartitionSpec as P

PRECISE = lax.Precision.HIGH


def passed_along(block, axis, distance):
    devices = range(lax.axis_size(axis))
    route = [(i - distance, i) for i in devices if i - distance in devices]
    return lax.ppermute(block, axis, route)


def dft_pair(row_count, col_count, period):
    row_index = lax.iota(jnp.int32, row_count)[:, None]
    col_index = lax.iota(jnp.int32, col_count)[None, :]
    phase = (row_index * col_index % period).astype(jnp.float32) * (-2.0 * math.pi / period)
    return (jnp.cos(phase), jnp.sin(phase))


def make_tables(inner, outer):
    half = outer // 2
    outer_cos, outer_sin = dft_pair(outer, half, outer)
    twist_cos, twist_sin = dft_pair(outer, inner, outer * inner)
    inner_cos, inner_sin = dft_pair(inner, inner, inner)
    real_outer = jnp.stack([outer_cos, outer_sin], 1)
    complex_outer = jnp.stack(
        [jnp.stack([outer_cos, -outer_sin], 1), jnp.stack([outer_sin, outer_cos], 1)], 1
    )
    inner_ahead = jnp.block([[inner_cos, inner_sin], [-inner_sin, inner_cos]])
    inner_back = jnp.block([[inner_cos, -inner_sin], [inner_sin, inner_cos]])
    outer_back = jnp.stack(
        [jnp.stack([outer_cos, outer_sin], 0), jnp.stack([-outer_sin, outer_cos], 0)], 0
    )
    return (real_outer, complex_outer, twist_cos, twist_sin, inner_ahead, inner_back, outer_back)


def twist_ahead(values, twist_cos, twist_sin):
    real_part = values[:, :, 0]
    imag_part = values[:, :, 1]
    return jnp.stack(
        [
            real_part * twist_cos - imag_part * twist_sin,
            real_part * twist_sin + imag_part * twist_cos,
        ],
        2,
    )


def twist_back(values, twist_cos, twist_sin):
    real_part = values[:, :, 0]
    imag_part = values[:, :, 1]
    return jnp.stack(
        [
            real_part * twist_cos + imag_part * twist_sin,
            imag_part * twist_cos - real_part * twist_sin,
        ],
        2,
    )


def inner_section(values, table):
    width, outer = (values.shape[0], values.shape[1])
    flat = values.reshape(width, outer, table.shape[0])
    return jnp.einsum(
        "wkc,cd->wkd", flat, table, precision=PRECISE, preferred_element_type=jnp.float32
    )


def real_spectrum(signal, tables):
    real_outer, complex_outer, twist_cos, twist_sin, inner_ahead, inner_back, outer_back = tables
    half = real_outer.shape[2]
    inner = twist_cos.shape[1]
    blocked = signal.reshape(signal.shape[0], half, inner)
    first = jnp.einsum(
        "wab,kra->wkrb", blocked, real_outer, precision=PRECISE, preferred_element_type=jnp.float32
    )
    return inner_section(twist_ahead(first, twist_cos, twist_sin), inner_ahead)


def complex_spectrum(signal_re, signal_im, tables):
    real_outer, complex_outer, twist_cos, twist_sin, inner_ahead, inner_back, outer_back = tables
    half = real_outer.shape[2]
    inner = twist_cos.shape[1]
    width = signal_re.shape[0]
    stacked = jnp.stack(
        [signal_re.reshape(width, half, inner), signal_im.reshape(width, half, inner)], 1
    )
    first = jnp.einsum(
        "wsab,krsa->wkrb",
        stacked,
        complex_outer,
        precision=PRECISE,
        preferred_element_type=jnp.float32,
    )
    return inner_section(twist_ahead(first, twist_cos, twist_sin), inner_ahead)


def inverse_spectrum(packed, tables):
    real_outer, complex_outer, twist_cos, twist_sin, inner_ahead, inner_back, outer_back = tables
    outer = twist_cos.shape[0]
    inner = twist_cos.shape[1]
    half = real_outer.shape[2]
    width = packed.shape[0]
    back = inner_section(packed, inner_back).reshape(width, outer, 2, inner)
    turned = twist_back(back, twist_cos, twist_sin)
    result = jnp.einsum(
        "wksb,rska->wrab", turned, outer_back, precision=PRECISE, preferred_element_type=jnp.float32
    )
    scale = 1.0 / (outer * inner)
    return (
        (result[:, 0] * scale).reshape(width, half * inner),
        (result[:, 1] * scale).reshape(width, half * inner),
    )


def spectral_block(gated_rows, mixed_rows, filter_rows, tables):
    inner = tables[2].shape[1]
    gated_spec = real_spectrum(gated_rows.astype(jnp.float32), tables)
    joint_spec = complex_spectrum(
        filter_rows.astype(jnp.float32), -mixed_rows.astype(jnp.float32), tables
    )
    gated_re = gated_spec[:, :, :inner]
    gated_im = gated_spec[:, :, inner:]
    joint_re = joint_spec[:, :, :inner]
    joint_im = joint_spec[:, :, inner:]
    product_re = joint_re * gated_re + joint_im * gated_im
    product_im = joint_re * gated_im - joint_im * gated_re
    product = jnp.concatenate([product_re, product_im], 2)
    result_re, result_im = inverse_spectrum(product, tables)
    return (result_re.astype(jnp.bfloat16), result_im.astype(jnp.bfloat16))


def general_plan(
    query_feat, key_feat, value_raw, conv_out, out_grad, filter_taps, short_filter, skip_gain
):
    rows = query_feat.shape[0]
    peers = lax.axis_size("ctx")
    before = passed_along(value_raw[rows - 2 :], "ctx", 1)
    padded = jnp.concatenate([before, value_raw], 0).astype(jnp.float32)
    value_conv = (
        short_filter[0] * padded[2:]
        + short_filter[1] * padded[1:-1]
        + short_filter[2] * padded[:-2]
    )
    mixed = (key_feat.astype(jnp.float32) * value_conv).astype(jnp.bfloat16)
    gated = (out_grad.astype(jnp.float32) * query_feat.astype(jnp.float32)).astype(jnp.bfloat16)
    query_grad = (out_grad.astype(jnp.float32) * conv_out.astype(jnp.float32)).astype(jnp.bfloat16)
    skip_part = jnp.sum(gated.astype(jnp.float32) * mixed.astype(jnp.float32), axis=0)
    tables = make_tables(rows, 2 * peers)
    gated_chan = gated.T
    mixed_chan = mixed.T
    sent_gated, sent_mixed = (
        lax.all_to_all(gated_chan, "ctx", split_axis=0, concat_axis=1, tiled=True),
        lax.all_to_all(mixed_chan, "ctx", split_axis=0, concat_axis=1, tiled=True),
    )
    back_rows, filter_grad = spectral_block(sent_gated, sent_mixed, filter_taps, tables)
    back_chan = lax.all_to_all(back_rows, "ctx", split_axis=1, concat_axis=0, tiled=True)
    conv_back = back_chan.T
    mixed_grad = conv_back.astype(jnp.float32) + skip_gain * gated.astype(jnp.float32)
    key_grad = (mixed_grad * value_conv).astype(jnp.bfloat16)
    feature_grad = (mixed_grad * key_feat.astype(jnp.float32)).astype(jnp.bfloat16)
    after = passed_along(feature_grad[:2], "ctx", -1)
    extended = jnp.concatenate([feature_grad, after], 0).astype(jnp.float32)
    value_grad = (
        short_filter[0] * extended[:-2]
        + short_filter[1] * extended[1:-1]
        + short_filter[2] * extended[2:]
    ).astype(jnp.bfloat16)
    feature_wide = extended[:-2]
    short_part = jnp.stack(
        [
            jnp.sum(feature_wide * padded[2:], axis=0),
            jnp.sum(feature_wide * padded[1:-1], axis=0),
            jnp.sum(feature_wide * padded[:-2], axis=0),
        ]
    )
    skip_grad, short_grad = (
        lax.psum_scatter(skip_part, "ctx", scatter_dimension=0, tiled=True),
        lax.psum_scatter(short_part, "ctx", scatter_dimension=1, tiled=True),
    )
    return (query_grad, key_grad, value_grad, filter_grad, skip_grad, short_grad)


INNER = 128
INNER_PEERS = 4


def half_spectrum(values, length):
    if length == 2:
        return [(values[0], None), (values[0], None)]
    even = half_spectrum(values[0::2], length // 2)
    odd = half_spectrum(values[1::2], length // 2)
    quarter = length // 4
    bins = [None] * (length // 2 + 1)
    bins[0] = (even[0][0] + odd[0][0], None)
    bins[length // 2] = (even[0][0] - odd[0][0], None)
    bins[quarter] = (even[quarter][0], -odd[quarter][0])
    for k in range(1, quarter):
        c = math.cos(2.0 * math.pi * k / length)
        s = math.sin(2.0 * math.pi * k / length)
        odd_re, odd_im = odd[k]
        even_re, even_im = even[k]
        if 2 * k == quarter:
            turn_re = (odd_re + odd_im) * c
            turn_im = (odd_im - odd_re) * c
        else:
            turn_re = odd_re * c + odd_im * s
            turn_im = odd_im * c - odd_re * s
        bins[k] = (even_re + turn_re, even_im + turn_im)
        bins[length // 2 - k] = (even_re - turn_re, turn_im - even_im)
    return bins


def first_half(bins, length):
    if length == 2:
        return [bins[0][0] + bins[1][0]]
    half = length // 2
    quarter = length // 4
    even = [None] * (quarter + 1)
    odd = [None] * (quarter + 1)
    even[0] = (bins[0][0] + bins[half][0], None)
    odd[0] = (bins[0][0] - bins[half][0], None)
    even[quarter] = (2.0 * bins[quarter][0], None)
    odd[quarter] = (-2.0 * bins[quarter][1], None)
    for k in range(1, quarter):
        c = math.cos(2.0 * math.pi * k / length)
        s = math.sin(2.0 * math.pi * k / length)
        near_re, near_im = bins[k]
        far_re, far_im = bins[half - k]
        even[k] = (near_re + far_re, near_im - far_im)
        gap_re = near_re - far_re
        gap_im = near_im + far_im
        if 2 * k == quarter:
            odd[k] = ((gap_re - gap_im) * c, (gap_re + gap_im) * c)
        else:
            odd[k] = (gap_re * c - gap_im * s, gap_re * s + gap_im * c)
    result = [None] * half
    result[0::2] = first_half(even, half)
    result[1::2] = first_half(odd, half)
    return result


def spectrum_tables(outer):
    size = outer * INNER
    near = np.arange(outer // 2 + 1)[:, None, None]
    place = np.arange(INNER)
    angle = -2.0 * np.pi * (
        (near * place[None, None, :]) / size + place[None, :, None] * place[None, None, :] / INNER
    )
    c, s = np.cos(angle), np.sin(angle)
    ahead = np.concatenate(
        [np.concatenate([c, -s], 2), np.concatenate([s, c], 2)], 1
    )
    back = np.swapaxes(ahead, 1, 2) / size
    return ahead.astype(jnp.bfloat16), back.astype(jnp.bfloat16)


def outer_ahead(load, z_ref, outer, width):
    def step(chunk, carry):
        row = pl.multiple_of(chunk * 16, 16)
        for lane in range(0, width, 128):
            values = [load(a, row, lane).astype(jnp.float32) for a in range(outer // 2)]
            bins = half_spectrum(values, outer)
            for k, (re, im) in enumerate(bins):
                im = jnp.zeros_like(re) if im is None else im
                z_ref[k, pl.ds(row, 16), lane : lane + 128] = re.astype(jnp.bfloat16)
                z_ref[k, pl.ds(INNER + row, 16), lane : lane + 128] = im.astype(jnp.bfloat16)
        return carry

    lax.fori_loop(0, INNER // 16, step, 0)


def outer_back(u_ref, store, outer, width):
    def step(chunk, carry):
        row = pl.multiple_of(chunk * 16, 16)
        for lane in range(0, width, 128):
            bins = []
            for k in range(outer // 2 + 1):
                re = u_ref[k, pl.ds(row, 16), lane : lane + 128]
                im = u_ref[k, pl.ds(INNER + row, 16), lane : lane + 128]
                bins.append((re, im))
            for a, value in enumerate(first_half(bins, outer)):
                store(a, row, lane, value)
        return carry

    lax.fori_loop(0, INNER // 16, step, 0)


def correlate_bin(first, gated):
    first_re, first_im = first[:INNER], first[INNER:]
    gated_re, gated_im = gated[:INNER], gated[INNER:]
    return jnp.concatenate(
        [
            first_re * gated_re + first_im * gated_im,
            first_re * gated_im - first_im * gated_re,
        ],
        0,
    ).astype(jnp.bfloat16)


def dot32(a, b):
    return jnp.dot(a, b, preferred_element_type=jnp.float32)


def filter_kernel(taps_ref, ahead_ref, spec_ref, rows_ref, z_ref, *, outer, width):
    for a in range(outer // 2):
        piece = taps_ref[:, a * INNER : (a + 1) * INNER].astype(jnp.float32)
        rows_ref[a * INNER : (a + 1) * INNER, :] = piece.T
    outer_ahead(
        lambda a, row, lane: rows_ref[pl.ds(a * INNER + row, 16), lane : lane + 128],
        z_ref, outer, width,
    )

    for k in range(outer // 2 + 1):
        spec_ref[k] = dot32(ahead_ref[k], z_ref[k]).astype(jnp.bfloat16)


def begun(source, target, semaphore):
    copy = pltpu.make_async_copy(source, target, semaphore)
    copy.start()
    return copy


def conv_kernel(
    gated_hbm, filter_hbm, ahead_hbm, back_hbm, skip_ref, conv_ref, spec_hbm,
    gated_ref, filter_ref, ahead_ref, back_ref, spec_ref, z_ref, u_ref, sems, *, outer, width,
):
    gated_in = begun(gated_hbm, gated_ref, sems.at[0])
    ahead_in = begun(ahead_hbm, ahead_ref, sems.at[1])
    filter_in = begun(filter_hbm, filter_ref, sems.at[2])
    back_in = begun(back_hbm, back_ref, sems.at[3])
    gated_in.wait()
    outer_ahead(
        lambda a, row, lane: gated_ref[pl.ds(a * INNER + row, 16), lane : lane + 128],
        z_ref, outer, width,
    )
    ahead_in.wait()
    filter_in.wait()
    for k in range(outer // 2 + 1):
        gated = dot32(ahead_ref[k], z_ref[k])
        spec_ref[k] = gated.astype(jnp.bfloat16)
        z_ref[k] = correlate_bin(filter_ref[k].astype(jnp.float32), gated)
    spec_out = begun(spec_ref, spec_hbm, sems.at[4])
    back_in.wait()
    for k in range(outer // 2 + 1):
        u_ref[k] = dot32(back_ref[k], z_ref[k])

    first = lax.axis_index("ctx") * width

    def store(a, row, lane, value):
        place = pl.ds(a * INNER + row, 16)
        skip = skip_ref[:, pl.ds(pl.multiple_of(first + lane, 128), 128)]
        gated = gated_ref[place, lane : lane + 128].astype(jnp.float32)
        conv_ref[place, lane : lane + 128] = (value + skip * gated).astype(jnp.bfloat16)

    outer_back(u_ref, store, outer, width)
    spec_out.wait()


def grad_kernel(*refs, outer, width):
    far = outer // 2 // INNER_PEERS
    place_hbm, refs = refs[:far], refs[far:]
    near_hbm, refs = refs[: INNER_PEERS - 1], refs[INNER_PEERS - 1 :]
    far_hbm, refs = refs[: far - 1], refs[far - 1 :]
    gated_hbm, spec_hbm, ahead_hbm, back_hbm, grad_ref, skip_ref = refs[:6]
    mixed_ref, gated_ref, spec_ref, ahead_ref, back_ref, z_ref, u_ref, rows_ref, sems = refs[6:]
    slabs = outer // 2
    me = lax.axis_index("ctx")
    own_row, own_place = me // INNER_PEERS, me % INNER_PEERS
    mixed_in = []
    for d in range(far):
        for e in range(INNER_PEERS):
            if e == 0:
                source = place_hbm[d]
            elif d == 0:
                source = near_hbm[e - 1].at[own_row]
            else:
                source = far_hbm[d - 1].at[e - 1]
            slab = (own_row ^ d) * INNER_PEERS + (own_place ^ e)
            mixed_in.append(begun(source, mixed_ref.at[slab], sems.at[4 + len(mixed_in)]))
    ahead_in = begun(ahead_hbm, ahead_ref, sems.at[0])
    spec_in = begun(spec_hbm, spec_ref, sems.at[1])
    back_in = begun(back_hbm, back_ref, sems.at[2])
    gated_in = begun(gated_hbm, gated_ref, sems.at[3])
    for copy in mixed_in:
        copy.wait()
    outer_ahead(
        lambda a, row, lane: mixed_ref[a, pl.ds(row, 16), lane : lane + 128],
        z_ref, outer, width,
    )
    ahead_in.wait()
    spec_in.wait()
    for k in range(outer // 2 + 1):
        mixed = dot32(ahead_ref[k], z_ref[k])
        z_ref[k] = correlate_bin(mixed, spec_ref[k].astype(jnp.float32))
    back_in.wait()
    for k in range(outer // 2 + 1):
        u_ref[k] = dot32(back_ref[k], z_ref[k])

    def store(a, row, lane, value):
        rows_ref[pl.ds(a * INNER + row, 16), lane : lane + 128] = value

    outer_back(u_ref, store, outer, width)
    for a in range(slabs):
        grad_ref[:, a * INNER : (a + 1) * INNER] = rows_ref[
            a * INNER : (a + 1) * INNER, :
        ].T.astype(jnp.bfloat16)
    gated_in.wait()

    def add(a, total):
        place = pl.ds(pl.multiple_of(a * INNER, INNER), INNER)
        part = gated_ref[place, :].astype(jnp.float32) * mixed_ref[a].astype(jnp.float32)
        return total + jnp.sum(part.reshape(INNER // 8, 8, width), axis=0)

    total = lax.fori_loop(0, slabs, add, jnp.zeros((8, width), jnp.float32))
    skip_ref[...] = jnp.sum(total, axis=0, keepdims=True)


def regroup_kernel(*refs):
    near, far = refs[: INNER_PEERS - 1], refs[INNER_PEERS - 1 :]
    own_row = lax.axis_index("ctx") // INNER_PEERS
    for d in range(1, len(far) + 1):
        for e in range(1, INNER_PEERS):
            far[d - 1][e - 1] = near[e - 1][own_row ^ d]


def gate_kernel(grad_ref, query_ref, value_ref, gated_ref, last_ref, *, width):
    last_ref[...] = value_ref[...].astype(jnp.float32)[value_ref.shape[0] - 2 :]
    for j in range(gated_ref.shape[0]):
        cols = slice(j * width, (j + 1) * width)
        gated_ref[j] = (
            grad_ref[:, cols].astype(jnp.float32) * query_ref[:, cols].astype(jnp.float32)
        ).astype(jnp.bfloat16)


def mix_kernel(key_ref, value_ref, edge_ref, short_ref, grad_ref, conv_ref, *rest, width):
    near_refs, place_refs = rest[: INNER_PEERS - 1], rest[INNER_PEERS - 1 : -3]
    query_grad_ref, behind, mixed_ref = rest[-3:]
    rows = key_ref.shape[0]
    owners = key_ref.shape[1] // width
    step = pl.program_id(0)
    for j in range(owners):
        for lane in range(0, width, 128):
            slot = (j * width + lane) // 128 % 2
            cols = slice(j * width + lane, j * width + lane + 128)
            value = value_ref[:, cols].astype(jnp.float32)
            behind[slot, 6:8] = edge_ref[:, cols]
            behind[slot, 8 : 8 + rows] = value
            conv = (
                short_ref[0:1, cols] * value
                + short_ref[1:2, cols] * behind[slot, 7 : 7 + rows]
                + short_ref[2:3, cols] * behind[slot, 6 : 6 + rows]
            )
            mixed_ref[step * owners + j, :, lane : lane + 128] = (
                key_ref[:, cols].astype(jnp.float32) * conv
            ).astype(jnp.bfloat16)
            query_grad_ref[:, cols] = (
                grad_ref[:, cols].astype(jnp.float32) * conv_ref[:, cols].astype(jnp.float32)
            ).astype(jnp.bfloat16)

    @pl.when(step == pl.num_programs(0) - 1)
    def _():
        me = lax.axis_index("ctx")
        own_row, place = me // INNER_PEERS, me % INNER_PEERS
        for e, near_ref in enumerate(near_refs, 1):
            for row in range(near_ref.shape[0]):
                near_ref[row] = mixed_ref[row * INNER_PEERS + (place ^ e)]
        for d, place_ref in enumerate(place_refs):
            place_ref[...] = mixed_ref[(own_row ^ d) * INNER_PEERS + place]


def sums_kernel(
    back_ref, key_ref, value_ref, edge_ref, head_ref, *rest, width
):
    part_refs, behind, sums_ref = rest[:-2], rest[-2], rest[-1]
    rows = key_ref.shape[0]
    owners = back_ref.shape[0]
    step = pl.program_id(0)
    for j in range(owners):
        for lane in range(0, width, 128):
            slot = (j * width + lane) // 128 % 2
            cols = slice(j * width + lane, j * width + lane + 128)
            lanes = slice(lane, lane + 128)
            value = value_ref[:, cols].astype(jnp.float32)
            behind[slot, 6:8] = edge_ref[:, cols]
            behind[slot, 8 : 8 + rows] = value
            mixed_grad = back_ref[j, :, lanes].astype(jnp.float32)
            feature = (mixed_grad * key_ref[:, cols].astype(jnp.float32)).astype(jnp.bfloat16)
            feature = feature.astype(jnp.float32)
            head_ref[:, cols] = feature[:2]
            shifted = (value, behind[slot, 7 : 7 + rows], behind[slot, 6 : 6 + rows])
            sums_ref[step * owners + j, :, lanes] = jnp.concatenate(
                [jnp.sum(feature * other, axis=0, keepdims=True) for other in shifted]
                + [jnp.zeros((5, 128), jnp.float32)],
                0,
            )

    @pl.when(step == pl.num_programs(0) - 1)
    def _():
        own = lax.axis_index("ctx") // INNER_PEERS
        for d, part_ref in enumerate(part_refs):
            part_ref[...] = sums_ref[pl.ds((own ^ d) * INNER_PEERS, INNER_PEERS)]


def finish_kernel(
    back_ref, key_ref, value_ref, edge_ref, next_ref, short_ref,
    key_grad_ref, value_grad_ref, behind, ahead, *, width,
):
    rows = key_ref.shape[0]
    for j in range(back_ref.shape[0]):
        for lane in range(0, width, 128):
            slot = (j * width + lane) // 128 % 2
            cols = slice(j * width + lane, j * width + lane + 128)
            lanes = slice(lane, lane + 128)
            short = [short_ref[i : i + 1, cols] for i in range(3)]
            value = value_ref[:, cols].astype(jnp.float32)
            behind[slot, 6:8] = edge_ref[:, cols]
            behind[slot, 8 : 8 + rows] = value
            mixed_grad = back_ref[j, :, lanes].astype(jnp.float32)
            conv = (
                short[0] * value
                + short[1] * behind[slot, 7 : 7 + rows]
                + short[2] * behind[slot, 6 : 6 + rows]
            )
            key_grad_ref[:, cols] = (mixed_grad * conv).astype(jnp.bfloat16)
            feature = (mixed_grad * key_ref[:, cols].astype(jnp.float32)).astype(jnp.bfloat16)
            feature = feature.astype(jnp.float32)
            ahead[slot, 0:rows] = feature
            ahead[slot, rows : rows + 2] = next_ref[:, cols]
            value_grad_ref[:, cols] = (
                short[0] * feature
                + short[1] * ahead[slot, 1 : 1 + rows]
                + short[2] * ahead[slot, 2 : 2 + rows]
            ).astype(jnp.bfloat16)


def exchanged(block):
    return lax.all_to_all(block, "ctx", split_axis=0, concat_axis=0, tiled=True)


def paired(block, distance):
    return lax.ppermute(block, "ctx", [(i, i ^ distance) for i in range(lax.axis_size("ctx"))])


def summed_at_owner(parts, *beside):
    place = lax.axis_index("ctx") % INNER_PEERS
    got = [parts[0]] + [paired(parts[d], d * INNER_PEERS) for d in range(1, len(parts))]
    rows = sum(got[1:], got[0])
    rows, beside = lax.optimization_barrier((rows, beside))
    total = lax.dynamic_index_in_dim(rows, place, 0, keepdims=False)
    for distance in range(1, INNER_PEERS):
        other = lax.dynamic_index_in_dim(rows, place ^ distance, 0, keepdims=False)
        total = total + paired(other, distance)
    return total, *beside


def after(value, *others):
    return lax.optimization_barrier((value,) + others)[0]


def in_hbm(*values):
    return [pltpu.with_memory_space_constraint(value, pltpu.HBM) for value in values]


def params(mib=63):
    return pltpu.CompilerParams(vmem_limit_bytes=mib * 1024 * 1024)


BESIDE_EXCHANGE = 40_000_000_000
WHOLE_EXCHANGE = 100_000_000_000


def cost(flops, size):
    return pl.CostEstimate(flops=flops, bytes_accessed=size, transcendentals=0)


def kernel_plan(
    query_feat, key_feat, value_raw, conv_out, out_grad, filter_taps, short_filter, skip_gain
):
    rows, channels = query_feat.shape
    peers = lax.axis_size("ctx")
    width = channels // peers
    seq = rows * peers
    outer = 2 * seq // INNER
    bins = outer // 2 + 1
    steps = 2
    group = peers // steps
    span = group * width
    far = peers // INNER_PEERS
    any_place = pl.BlockSpec(memory_space=pl.ANY)
    hbm = pl.BlockSpec(memory_space=pltpu.HBM)
    bf16, f32 = jnp.bfloat16, jnp.float32
    shape = jax.ShapeDtypeStruct
    skip_row = skip_gain.reshape(1, channels)
    ahead, back = (jnp.asarray(t) for t in spectrum_tables(outer))

    flat = pl.BlockSpec((rows, span), lambda i: (0, i))
    owned = pl.BlockSpec((group, rows, width), lambda i: (i, 0, 0))
    edge_spec = pl.BlockSpec((2, span), lambda i: (0, i))
    short_spec = pl.BlockSpec((3, span), lambda i: (0, i))

    gated, last = pl.pallas_call(
        functools.partial(gate_kernel, width=width),
        grid=(steps,),
        in_specs=[flat, flat, pl.BlockSpec((16, span), lambda i: (rows // 16 - 1, i))],
        out_specs=[owned, edge_spec],
        out_shape=[shape((peers, rows, width), bf16), shape((2, channels), f32)],
        compiler_params=params(),
        cost_estimate=cost(rows * channels, 6 * rows * channels),
        name="gate",
    )(out_grad, query_feat, value_raw)

    gated_got = exchanged(gated.reshape(seq, width))

    spec_shape = shape((bins, 2 * INNER, width), bf16)
    z_scratch = pltpu.VMEM((bins, 2 * INNER, width), bf16)
    u_scratch = pltpu.VMEM((bins, 2 * INNER, width), f32)
    table_scratch = pltpu.VMEM((bins, 2 * INNER, 2 * INNER), bf16)
    table_bytes = 8 * bins * INNER * INNER
    spec_bytes = 4 * bins * INNER * width
    work = 2 * bins * (2 * INNER) ** 2 * width
    edge = passed_along(last, "ctx", 1)
    shift_scratch = pltpu.VMEM((2, rows + 8, 128), f32)
    near_spec = pl.BlockSpec((far, rows, width), lambda i: (0, 0, 0))
    far_spec = pl.BlockSpec((INNER_PEERS - 1, rows, width), lambda i: (0, 0, 0))
    place_spec = pl.BlockSpec((rows, width), lambda i: (0, 0))
    *mixed, query_grad = pl.pallas_call(
        functools.partial(mix_kernel, width=width),
        grid=(steps,),
        in_specs=[flat, flat, edge_spec, short_spec, flat, flat],
        out_specs=[near_spec] * (INNER_PEERS - 1) + [place_spec] * far + [flat],
        out_shape=[shape((far, rows, width), bf16)] * (INNER_PEERS - 1)
        + [shape((rows, width), bf16)] * far
        + [shape((rows, channels), bf16)],
        scratch_shapes=[shift_scratch, pltpu.VMEM((peers, rows, width), bf16)],
        compiler_params=params(),
        cost_estimate=cost(BESIDE_EXCHANGE, 12 * rows * channels),
        name="mix",
    )(key_feat, value_raw, edge, short_filter, out_grad, conv_out)
    near = [paired(mixed[e - 1], e) for e in range(1, INNER_PEERS)]
    placed = mixed[INNER_PEERS - 1 :]
    placed = [placed[0]] + [paired(placed[d], d * INNER_PEERS) for d in range(1, far)]
    across = pl.pallas_call(
        regroup_kernel,
        grid=(1,),
        in_specs=[near_spec] * (INNER_PEERS - 1),
        out_specs=[far_spec] * (far - 1),
        out_shape=[shape((INNER_PEERS - 1, rows, width), bf16)] * (far - 1),
        compiler_params=params(),
        cost_estimate=cost(0, 4 * seq * width),
        name="regroup",
    )(*near)
    filter_taps, query_grad = lax.optimization_barrier((filter_taps, query_grad))
    filter_spec = pl.pallas_call(
        functools.partial(filter_kernel, outer=outer, width=width),
        out_shape=spec_shape,
        scratch_shapes=[pltpu.VMEM((seq, width), f32), z_scratch],
        compiler_params=params(),
        cost_estimate=cost(BESIDE_EXCHANGE, table_bytes + spec_bytes + 2 * seq * width),
        name="filter_spectrum",
    )(filter_taps, ahead)


    *across, gated_got = lax.optimization_barrier((*across, gated_got))
    across = [paired(across[d - 1], d * INNER_PEERS) for d in range(1, far)]

    conv_back, gated_spec = pl.pallas_call(
        functools.partial(conv_kernel, outer=outer, width=width),
        in_specs=[hbm] * 4 + [pl.BlockSpec(memory_space=pltpu.VMEM)],
        out_specs=[pl.BlockSpec(memory_space=pltpu.VMEM), hbm],
        out_shape=(shape((seq, width), bf16), spec_shape),
        scratch_shapes=[pltpu.VMEM((seq, width), bf16), z_scratch, table_scratch, table_scratch, z_scratch]
        + [z_scratch, u_scratch, pltpu.SemaphoreType.DMA((5,))],
        compiler_params=params(),
        cost_estimate=cost(BESIDE_EXCHANGE, 2 * table_bytes + 2 * spec_bytes + 4 * seq * width),
        name="conv_back",
    )(gated_got, filter_spec, ahead, back, skip_row)

    back_got = exchanged(conv_back).reshape(peers, rows, width)

    filter_grad, skip_grad = pl.pallas_call(
        functools.partial(grad_kernel, outer=outer, width=width),
        in_specs=[hbm] * (INNER_PEERS + 2 * far + 2),
        out_shape=[shape((width, seq), bf16), shape((1, width), f32)],
        scratch_shapes=[
            pltpu.VMEM((peers, rows, width), bf16),
            pltpu.VMEM((seq, width), bf16),
            z_scratch,
            table_scratch,
            table_scratch,
            z_scratch,
            u_scratch,
            pltpu.VMEM((seq, width), f32),
            pltpu.SemaphoreType.DMA((peers + 4,)),
        ],
        compiler_params=params(30),
        cost_estimate=cost(WHOLE_EXCHANGE, 2 * table_bytes + spec_bytes),
        name="filter_grad",
    )(*in_hbm(*placed, *near, *across, gated_got, gated_spec, ahead, back))
    back_got, filter_grad, skip_grad = lax.optimization_barrier((back_got, filter_grad, skip_grad))

    head, *short_parts = pl.pallas_call(
        functools.partial(sums_kernel, width=width),
        grid=(steps,),
        in_specs=[owned, flat, flat, edge_spec],
        out_specs=[edge_spec]
        + [pl.BlockSpec((INNER_PEERS, 8, width), lambda i: (0, 0, 0))] * far,
        out_shape=[pltpu.HBM((2, channels), f32)]
        + [pltpu.HBM((INNER_PEERS, 8, width), f32)] * far,
        scratch_shapes=[shift_scratch, pltpu.VMEM((peers, 8, width), f32)],
        compiler_params=params(30),
        cost_estimate=cost(20 * rows * channels, 8 * rows * channels),
        name="sums",
    )(back_got, key_feat, value_raw, edge)

    head_got = passed_along(head, "ctx", -1)
    short_grad, head_got = summed_at_owner(short_parts, head_got)
    key_grad, value_grad = pl.pallas_call(
        functools.partial(finish_kernel, width=width),
        grid=(steps,),
        in_specs=[owned, flat, flat, edge_spec, edge_spec, short_spec],
        out_specs=[flat, flat],
        out_shape=[pltpu.HBM((rows, channels), bf16)] * 2,
        scratch_shapes=[shift_scratch] * 2,
        compiler_params=params(30),
        cost_estimate=cost(30 * rows * channels, 12 * rows * channels),
        name="finish",
    )(back_got, key_feat, value_raw, edge, head_got, short_filter)
    return query_grad, key_grad, value_grad, filter_grad, skip_grad.reshape(width), short_grad[:3]


def per_device(query_feat, key_feat, value_raw, conv_out, out_grad, filter_taps, short_filter, skip_gain):
    rows, channels = query_feat.shape
    peers = lax.axis_size("ctx")
    width = channels // peers
    fits = (
        peers % INNER_PEERS == 0
        and peers & (peers - 1) == 0
        and rows == INNER
        and width % 256 == 0
        and peers in (8, 16)
    )
    plan = kernel_plan if fits else general_plan
    return plan(query_feat, key_feat, value_raw, conv_out, out_grad, filter_taps, short_filter, skip_gain)


def solution(mesh):
    in_specs = (
        P(("groups", "ctx"), None),
        P(("groups", "ctx"), None),
        P(("groups", "ctx"), None),
        P(("groups", "ctx"), None),
        P(("groups", "ctx"), None),
        P("ctx", None),
        P(),
        P(),
    )
    out_specs = (
        P(("groups", "ctx"), None),
        P(("groups", "ctx"), None),
        P(("groups", "ctx"), None),
        P(("groups", "ctx"), None),
        P(("groups", "ctx")),
        P(None, ("groups", "ctx")),
    )
    return jax.shard_map(
        per_device, mesh=mesh, in_specs=in_specs, out_specs=out_specs, check_vma=False
    )
```

```python
import functools
import math

import jax
import jax.numpy as jnp
import numpy as np
from jax import lax
from jax.experimental import pallas as pl
from jax.experimental.pallas import tpu as pltpu
from jax.sharding import PartitionSpec as P

PRECISE = lax.Precision.HIGH


def passed_along(block, axis, distance):
    devices = range(lax.axis_size(axis))
    route = [(i - distance, i) for i in devices if i - distance in devices]
    return lax.ppermute(block, axis, route)


def dft_pair(row_count, col_count, period):
    row_index = lax.iota(jnp.int32, row_count)[:, None]
    col_index = lax.iota(jnp.int32, col_count)[None, :]
    phase = (row_index * col_index % period).astype(jnp.float32) * (-2.0 * math.pi / period)
    return (jnp.cos(phase), jnp.sin(phase))


def make_tables(inner, outer):
    half = outer // 2
    outer_cos, outer_sin = dft_pair(outer, half, outer)
    twist_cos, twist_sin = dft_pair(outer, inner, outer * inner)
    inner_cos, inner_sin = dft_pair(inner, inner, inner)
    real_outer = jnp.stack([outer_cos, outer_sin], 1)
    complex_outer = jnp.stack(
        [jnp.stack([outer_cos, -outer_sin], 1), jnp.stack([outer_sin, outer_cos], 1)], 1
    )
    inner_ahead = jnp.block([[inner_cos, inner_sin], [-inner_sin, inner_cos]])
    inner_back = jnp.block([[inner_cos, -inner_sin], [inner_sin, inner_cos]])
    outer_back = jnp.stack(
        [jnp.stack([outer_cos, outer_sin], 0), jnp.stack([-outer_sin, outer_cos], 0)], 0
    )
    return (real_outer, complex_outer, twist_cos, twist_sin, inner_ahead, inner_back, outer_back)


def twist_ahead(values, twist_cos, twist_sin):
    real_part = values[:, :, 0]
    imag_part = values[:, :, 1]
    return jnp.stack(
        [
            real_part * twist_cos - imag_part * twist_sin,
            real_part * twist_sin + imag_part * twist_cos,
        ],
        2,
    )


def twist_back(values, twist_cos, twist_sin):
    real_part = values[:, :, 0]
    imag_part = values[:, :, 1]
    return jnp.stack(
        [
            real_part * twist_cos + imag_part * twist_sin,
            imag_part * twist_cos - real_part * twist_sin,
        ],
        2,
    )


def inner_section(values, table):
    width, outer = (values.shape[0], values.shape[1])
    flat = values.reshape(width, outer, table.shape[0])
    return jnp.einsum(
        "wkc,cd->wkd", flat, table, precision=PRECISE, preferred_element_type=jnp.float32
    )


def real_spectrum(signal, tables):
    real_outer, complex_outer, twist_cos, twist_sin, inner_ahead, inner_back, outer_back = tables
    half = real_outer.shape[2]
    inner = twist_cos.shape[1]
    blocked = signal.reshape(signal.shape[0], half, inner)
    first = jnp.einsum(
        "wab,kra->wkrb", blocked, real_outer, precision=PRECISE, preferred_element_type=jnp.float32
    )
    return inner_section(twist_ahead(first, twist_cos, twist_sin), inner_ahead)


def complex_spectrum(signal_re, signal_im, tables):
    real_outer, complex_outer, twist_cos, twist_sin, inner_ahead, inner_back, outer_back = tables
    half = real_outer.shape[2]
    inner = twist_cos.shape[1]
    width = signal_re.shape[0]
    stacked = jnp.stack(
        [signal_re.reshape(width, half, inner), signal_im.reshape(width, half, inner)], 1
    )
    first = jnp.einsum(
        "wsab,krsa->wkrb",
        stacked,
        complex_outer,
        precision=PRECISE,
        preferred_element_type=jnp.float32,
    )
    return inner_section(twist_ahead(first, twist_cos, twist_sin), inner_ahead)


def inverse_spectrum(packed, tables):
    real_outer, complex_outer, twist_cos, twist_sin, inner_ahead, inner_back, outer_back = tables
    outer = twist_cos.shape[0]
    inner = twist_cos.shape[1]
    half = real_outer.shape[2]
    width = packed.shape[0]
    back = inner_section(packed, inner_back).reshape(width, outer, 2, inner)
    turned = twist_back(back, twist_cos, twist_sin)
    result = jnp.einsum(
        "wksb,rska->wrab", turned, outer_back, precision=PRECISE, preferred_element_type=jnp.float32
    )
    scale = 1.0 / (outer * inner)
    return (
        (result[:, 0] * scale).reshape(width, half * inner),
        (result[:, 1] * scale).reshape(width, half * inner),
    )


def spectral_block(gated_rows, mixed_rows, filter_rows, tables):
    inner = tables[2].shape[1]
    gated_spec = real_spectrum(gated_rows.astype(jnp.float32), tables)
    joint_spec = complex_spectrum(
        filter_rows.astype(jnp.float32), -mixed_rows.astype(jnp.float32), tables
    )
    gated_re = gated_spec[:, :, :inner]
    gated_im = gated_spec[:, :, inner:]
    joint_re = joint_spec[:, :, :inner]
    joint_im = joint_spec[:, :, inner:]
    product_re = joint_re * gated_re + joint_im * gated_im
    product_im = joint_re * gated_im - joint_im * gated_re
    product = jnp.concatenate([product_re, product_im], 2)
    result_re, result_im = inverse_spectrum(product, tables)
    return (result_re.astype(jnp.bfloat16), result_im.astype(jnp.bfloat16))


def general_plan(
    query_feat, key_feat, value_raw, conv_out, out_grad, filter_taps, short_filter, skip_gain
):
    rows = query_feat.shape[0]
    peers = lax.axis_size("ctx")
    before = passed_along(value_raw[rows - 2 :], "ctx", 1)
    padded = jnp.concatenate([before, value_raw], 0).astype(jnp.float32)
    value_conv = (
        short_filter[0] * padded[2:]
        + short_filter[1] * padded[1:-1]
        + short_filter[2] * padded[:-2]
    )
    mixed = (key_feat.astype(jnp.float32) * value_conv).astype(jnp.bfloat16)
    gated = (out_grad.astype(jnp.float32) * query_feat.astype(jnp.float32)).astype(jnp.bfloat16)
    query_grad = (out_grad.astype(jnp.float32) * conv_out.astype(jnp.float32)).astype(jnp.bfloat16)
    skip_part = jnp.sum(gated.astype(jnp.float32) * mixed.astype(jnp.float32), axis=0)
    tables = make_tables(rows, 2 * peers)
    gated_chan = gated.T
    mixed_chan = mixed.T
    sent_gated, sent_mixed = (
        lax.all_to_all(gated_chan, "ctx", split_axis=0, concat_axis=1, tiled=True),
        lax.all_to_all(mixed_chan, "ctx", split_axis=0, concat_axis=1, tiled=True),
    )
    back_rows, filter_grad = spectral_block(sent_gated, sent_mixed, filter_taps, tables)
    back_chan = lax.all_to_all(back_rows, "ctx", split_axis=1, concat_axis=0, tiled=True)
    conv_back = back_chan.T
    mixed_grad = conv_back.astype(jnp.float32) + skip_gain * gated.astype(jnp.float32)
    key_grad = (mixed_grad * value_conv).astype(jnp.bfloat16)
    feature_grad = (mixed_grad * key_feat.astype(jnp.float32)).astype(jnp.bfloat16)
    after = passed_along(feature_grad[:2], "ctx", -1)
    extended = jnp.concatenate([feature_grad, after], 0).astype(jnp.float32)
    value_grad = (
        short_filter[0] * extended[:-2]
        + short_filter[1] * extended[1:-1]
        + short_filter[2] * extended[2:]
    ).astype(jnp.bfloat16)
    feature_wide = extended[:-2]
    short_part = jnp.stack(
        [
            jnp.sum(feature_wide * padded[2:], axis=0),
            jnp.sum(feature_wide * padded[1:-1], axis=0),
            jnp.sum(feature_wide * padded[:-2], axis=0),
        ]
    )
    skip_grad, short_grad = (
        lax.psum_scatter(skip_part, "ctx", scatter_dimension=0, tiled=True),
        lax.psum_scatter(short_part, "ctx", scatter_dimension=1, tiled=True),
    )
    return (query_grad, key_grad, value_grad, filter_grad, skip_grad, short_grad)


INNER = 128
INNER_PEERS = 4


def half_spectrum(values, length):
    if length == 2:
        return [(values[0], None), (values[0], None)]
    even = half_spectrum(values[0::2], length // 2)
    odd = half_spectrum(values[1::2], length // 2)
    quarter = length // 4
    bins = [None] * (length // 2 + 1)
    bins[0] = (even[0][0] + odd[0][0], None)
    bins[length // 2] = (even[0][0] - odd[0][0], None)
    bins[quarter] = (even[quarter][0], -odd[quarter][0])
    for k in range(1, quarter):
        c = math.cos(2.0 * math.pi * k / length)
        s = math.sin(2.0 * math.pi * k / length)
        odd_re, odd_im = odd[k]
        even_re, even_im = even[k]
        if 2 * k == quarter:
            turn_re = (odd_re + odd_im) * c
            turn_im = (odd_im - odd_re) * c
        else:
            turn_re = odd_re * c + odd_im * s
            turn_im = odd_im * c - odd_re * s
        bins[k] = (even_re + turn_re, even_im + turn_im)
        bins[length // 2 - k] = (even_re - turn_re, turn_im - even_im)
    return bins


def first_half(bins, length):
    if length == 2:
        return [bins[0][0] + bins[1][0]]
    half = length // 2
    quarter = length // 4
    even = [None] * (quarter + 1)
    odd = [None] * (quarter + 1)
    even[0] = (bins[0][0] + bins[half][0], None)
    odd[0] = (bins[0][0] - bins[half][0], None)
    even[quarter] = (2.0 * bins[quarter][0], None)
    odd[quarter] = (-2.0 * bins[quarter][1], None)
    for k in range(1, quarter):
        c = math.cos(2.0 * math.pi * k / length)
        s = math.sin(2.0 * math.pi * k / length)
        near_re, near_im = bins[k]
        far_re, far_im = bins[half - k]
        even[k] = (near_re + far_re, near_im - far_im)
        gap_re = near_re - far_re
        gap_im = near_im + far_im
        if 2 * k == quarter:
            odd[k] = ((gap_re - gap_im) * c, (gap_re + gap_im) * c)
        else:
            odd[k] = (gap_re * c - gap_im * s, gap_re * s + gap_im * c)
    result = [None] * half
    result[0::2] = first_half(even, half)
    result[1::2] = first_half(odd, half)
    return result


def spectrum_tables(outer):
    size = outer * INNER
    near = np.arange(outer // 2 + 1)[:, None, None]
    place = np.arange(INNER)
    angle = -2.0 * np.pi * (
        (near * place[None, None, :]) / size + place[None, :, None] * place[None, None, :] / INNER
    )
    c, s = np.cos(angle), np.sin(angle)
    ahead = np.concatenate(
        [np.concatenate([c, -s], 2), np.concatenate([s, c], 2)], 1
    )
    back = np.swapaxes(ahead, 1, 2) / size
    return ahead.astype(jnp.bfloat16), back.astype(jnp.bfloat16)


def outer_ahead(load, z_ref, outer, width):
    def step(chunk, carry):
        row = pl.multiple_of(chunk * 16, 16)
        for lane in range(0, width, 128):
            values = [load(a, row, lane).astype(jnp.float32) for a in range(outer // 2)]
            bins = half_spectrum(values, outer)
            for k, (re, im) in enumerate(bins):
                im = jnp.zeros_like(re) if im is None else im
                z_ref[k, pl.ds(row, 16), lane : lane + 128] = re.astype(jnp.bfloat16)
                z_ref[k, pl.ds(INNER + row, 16), lane : lane + 128] = im.astype(jnp.bfloat16)
        return carry

    lax.fori_loop(0, INNER // 16, step, 0)


def outer_back(u_ref, store, outer, width):
    def step(chunk, carry):
        row = pl.multiple_of(chunk * 16, 16)
        for lane in range(0, width, 128):
            bins = []
            for k in range(outer // 2 + 1):
                re = u_ref[k, pl.ds(row, 16), lane : lane + 128]
                im = u_ref[k, pl.ds(INNER + row, 16), lane : lane + 128]
                bins.append((re, im))
            for a, value in enumerate(first_half(bins, outer)):
                store(a, row, lane, value)
        return carry

    lax.fori_loop(0, INNER // 16, step, 0)


def correlate_bin(first, gated):
    first_re, first_im = first[:INNER], first[INNER:]
    gated_re, gated_im = gated[:INNER], gated[INNER:]
    return jnp.concatenate(
        [
            first_re * gated_re + first_im * gated_im,
            first_re * gated_im - first_im * gated_re,
        ],
        0,
    ).astype(jnp.bfloat16)


def dot32(a, b):
    return jnp.dot(a, b, preferred_element_type=jnp.float32)


def filter_kernel(taps_ref, ahead_ref, spec_ref, rows_ref, z_ref, *, outer, width):
    for a in range(outer // 2):
        piece = taps_ref[:, a * INNER : (a + 1) * INNER].astype(jnp.float32)
        rows_ref[a * INNER : (a + 1) * INNER, :] = piece.T
    outer_ahead(
        lambda a, row, lane: rows_ref[pl.ds(a * INNER + row, 16), lane : lane + 128],
        z_ref, outer, width,
    )

    for k in range(outer // 2 + 1):
        spec_ref[k] = dot32(ahead_ref[k], z_ref[k]).astype(jnp.bfloat16)


def begun(source, target, semaphore):
    copy = pltpu.make_async_copy(source, target, semaphore)
    copy.start()
    return copy


def conv_kernel(
    gated_hbm, filter_hbm, ahead_hbm, back_hbm, skip_ref, conv_ref, spec_hbm,
    gated_ref, filter_ref, ahead_ref, back_ref, spec_ref, z_ref, u_ref, sems, *, outer, width,
):
    gated_in = begun(gated_hbm, gated_ref, sems.at[0])
    ahead_in = begun(ahead_hbm, ahead_ref, sems.at[1])
    filter_in = begun(filter_hbm, filter_ref, sems.at[2])
    back_in = begun(back_hbm, back_ref, sems.at[3])
    gated_in.wait()
    outer_ahead(
        lambda a, row, lane: gated_ref[pl.ds(a * INNER + row, 16), lane : lane + 128],
        z_ref, outer, width,
    )
    ahead_in.wait()
    filter_in.wait()
    for k in range(outer // 2 + 1):
        gated = dot32(ahead_ref[k], z_ref[k])
        spec_ref[k] = gated.astype(jnp.bfloat16)
        z_ref[k] = correlate_bin(filter_ref[k].astype(jnp.float32), gated)
    spec_out = begun(spec_ref, spec_hbm, sems.at[4])
    back_in.wait()
    for k in range(outer // 2 + 1):
        u_ref[k] = dot32(back_ref[k], z_ref[k])

    first = lax.axis_index("ctx") * width

    def store(a, row, lane, value):
        place = pl.ds(a * INNER + row, 16)
        skip = skip_ref[:, pl.ds(pl.multiple_of(first + lane, 128), 128)]
        gated = gated_ref[place, lane : lane + 128].astype(jnp.float32)
        conv_ref[place, lane : lane + 128] = (value + skip * gated).astype(jnp.bfloat16)

    outer_back(u_ref, store, outer, width)
    spec_out.wait()


def grad_kernel(*refs, outer, width):
    far = outer // 2 // INNER_PEERS
    place_hbm, refs = refs[:far], refs[far:]
    near_hbm, refs = refs[: INNER_PEERS - 1], refs[INNER_PEERS - 1 :]
    far_hbm, refs = refs[: far - 1], refs[far - 1 :]
    gated_hbm, spec_hbm, ahead_hbm, back_hbm, grad_ref, skip_ref = refs[:6]
    mixed_ref, gated_ref, spec_ref, ahead_ref, back_ref, z_ref, u_ref, rows_ref, sems = refs[6:]
    slabs = outer // 2
    me = lax.axis_index("ctx")
    own_row, own_place = me // INNER_PEERS, me % INNER_PEERS
    mixed_in = []
    for d in range(far):
        for e in range(INNER_PEERS):
            if e == 0:
                source = place_hbm[d]
            elif d == 0:
                source = near_hbm[e - 1].at[own_row]
            else:
                source = far_hbm[d - 1].at[e - 1]
            slab = (own_row ^ d) * INNER_PEERS + (own_place ^ e)
            mixed_in.append(begun(source, mixed_ref.at[slab], sems.at[4 + len(mixed_in)]))
    ahead_in = begun(ahead_hbm, ahead_ref, sems.at[0])
    spec_in = begun(spec_hbm, spec_ref, sems.at[1])
    back_in = begun(back_hbm, back_ref, sems.at[2])
    gated_in = begun(gated_hbm, gated_ref, sems.at[3])
    for copy in mixed_in:
        copy.wait()
    outer_ahead(
        lambda a, row, lane: mixed_ref[a, pl.ds(row, 16), lane : lane + 128],
        z_ref, outer, width,
    )
    ahead_in.wait()
    spec_in.wait()
    for k in range(outer // 2 + 1):
        mixed = dot32(ahead_ref[k], z_ref[k])
        z_ref[k] = correlate_bin(mixed, spec_ref[k].astype(jnp.float32))
    back_in.wait()
    for k in range(outer // 2 + 1):
        u_ref[k] = dot32(back_ref[k], z_ref[k])

    def store(a, row, lane, value):
        rows_ref[pl.ds(a * INNER + row, 16), lane : lane + 128] = value

    outer_back(u_ref, store, outer, width)
    for a in range(slabs):
        grad_ref[:, a * INNER : (a + 1) * INNER] = rows_ref[
            a * INNER : (a + 1) * INNER, :
        ].T.astype(jnp.bfloat16)
    gated_in.wait()

    def add(a, total):
        place = pl.ds(pl.multiple_of(a * INNER, INNER), INNER)
        part = gated_ref[place, :].astype(jnp.float32) * mixed_ref[a].astype(jnp.float32)
        return total + jnp.sum(part.reshape(INNER // 8, 8, width), axis=0)

    total = lax.fori_loop(0, slabs, add, jnp.zeros((8, width), jnp.float32))
    skip_ref[...] = jnp.sum(total, axis=0, keepdims=True)


def regroup_kernel(*refs):
    near, far = refs[: INNER_PEERS - 1], refs[INNER_PEERS - 1 :]
    own_row = lax.axis_index("ctx") // INNER_PEERS
    for d in range(1, len(far) + 1):
        for e in range(1, INNER_PEERS):
            far[d - 1][e - 1] = near[e - 1][own_row ^ d]


def gate_kernel(grad_ref, query_ref, value_ref, gated_ref, last_ref, *, width):
    last_ref[...] = value_ref[...].astype(jnp.float32)[value_ref.shape[0] - 2 :]
    for j in range(gated_ref.shape[0]):
        cols = slice(j * width, (j + 1) * width)
        gated_ref[j] = (
            grad_ref[:, cols].astype(jnp.float32) * query_ref[:, cols].astype(jnp.float32)
        ).astype(jnp.bfloat16)


def mix_kernel(key_ref, value_ref, edge_ref, short_ref, grad_ref, conv_ref, *rest, width):
    near_refs, place_refs = rest[: INNER_PEERS - 1], rest[INNER_PEERS - 1 : -3]
    query_grad_ref, behind, mixed_ref = rest[-3:]
    rows = key_ref.shape[0]
    owners = key_ref.shape[1] // width
    step = pl.program_id(0)
    for j in range(owners):
        for lane in range(0, width, 128):
            slot = (j * width + lane) // 128 % 2
            cols = slice(j * width + lane, j * width + lane + 128)
            value = value_ref[:, cols].astype(jnp.float32)
            behind[slot, 6:8] = edge_ref[:, cols]
            behind[slot, 8 : 8 + rows] = value
            conv = (
                short_ref[0:1, cols] * value
                + short_ref[1:2, cols] * behind[slot, 7 : 7 + rows]
                + short_ref[2:3, cols] * behind[slot, 6 : 6 + rows]
            )
            mixed_ref[step * owners + j, :, lane : lane + 128] = (
                key_ref[:, cols].astype(jnp.float32) * conv
            ).astype(jnp.bfloat16)
            query_grad_ref[:, cols] = (
                grad_ref[:, cols].astype(jnp.float32) * conv_ref[:, cols].astype(jnp.float32)
            ).astype(jnp.bfloat16)

    @pl.when(step == pl.num_programs(0) - 1)
    def _():
        me = lax.axis_index("ctx")
        own_row, place = me // INNER_PEERS, me % INNER_PEERS
        for e, near_ref in enumerate(near_refs, 1):
            for row in range(near_ref.shape[0]):
                near_ref[row] = mixed_ref[row * INNER_PEERS + (place ^ e)]
        for d, place_ref in enumerate(place_refs):
            place_ref[...] = mixed_ref[(own_row ^ d) * INNER_PEERS + place]


def sums_kernel(
    back_ref, key_ref, value_ref, edge_ref, head_ref, *rest, width
):
    part_refs, behind, sums_ref = rest[:-2], rest[-2], rest[-1]
    rows = key_ref.shape[0]
    owners = back_ref.shape[0]
    step = pl.program_id(0)
    for j in range(owners):
        for lane in range(0, width, 128):
            slot = (j * width + lane) // 128 % 2
            cols = slice(j * width + lane, j * width + lane + 128)
            lanes = slice(lane, lane + 128)
            value = value_ref[:, cols].astype(jnp.float32)
            behind[slot, 6:8] = edge_ref[:, cols]
            behind[slot, 8 : 8 + rows] = value
            mixed_grad = back_ref[j, :, lanes].astype(jnp.float32)
            feature = (mixed_grad * key_ref[:, cols].astype(jnp.float32)).astype(jnp.bfloat16)
            feature = feature.astype(jnp.float32)
            head_ref[:, cols] = feature[:2]
            shifted = (value, behind[slot, 7 : 7 + rows], behind[slot, 6 : 6 + rows])
            sums_ref[step * owners + j, :, lanes] = jnp.concatenate(
                [jnp.sum(feature * other, axis=0, keepdims=True) for other in shifted]
                + [jnp.zeros((5, 128), jnp.float32)],
                0,
            )

    @pl.when(step == pl.num_programs(0) - 1)
    def _():
        own = lax.axis_index("ctx") // INNER_PEERS
        for d, part_ref in enumerate(part_refs):
            part_ref[...] = sums_ref[pl.ds((own ^ d) * INNER_PEERS, INNER_PEERS)]


def finish_kernel(
    back_ref, key_ref, value_ref, edge_ref, next_ref, short_ref,
    key_grad_ref, value_grad_ref, behind, ahead, *, width,
):
    rows = key_ref.shape[0]
    for j in range(back_ref.shape[0]):
        for lane in range(0, width, 128):
            slot = (j * width + lane) // 128 % 2
            cols = slice(j * width + lane, j * width + lane + 128)
            lanes = slice(lane, lane + 128)
            short = [short_ref[i : i + 1, cols] for i in range(3)]
            value = value_ref[:, cols].astype(jnp.float32)
            behind[slot, 6:8] = edge_ref[:, cols]
            behind[slot, 8 : 8 + rows] = value
            mixed_grad = back_ref[j, :, lanes].astype(jnp.float32)
            conv = (
                short[0] * value
                + short[1] * behind[slot, 7 : 7 + rows]
                + short[2] * behind[slot, 6 : 6 + rows]
            )
            key_grad_ref[:, cols] = (mixed_grad * conv).astype(jnp.bfloat16)
            feature = (mixed_grad * key_ref[:, cols].astype(jnp.float32)).astype(jnp.bfloat16)
            feature = feature.astype(jnp.float32)
            ahead[slot, 0:rows] = feature
            ahead[slot, rows : rows + 2] = next_ref[:, cols]
            value_grad_ref[:, cols] = (
                short[0] * feature
                + short[1] * ahead[slot, 1 : 1 + rows]
                + short[2] * ahead[slot, 2 : 2 + rows]
            ).astype(jnp.bfloat16)


def exchanged(block):
    return lax.all_to_all(block, "ctx", split_axis=0, concat_axis=0, tiled=True)


def paired(block, distance):
    return lax.ppermute(block, "ctx", [(i, i ^ distance) for i in range(lax.axis_size("ctx"))])


def summed_at_owner(parts):
    place = lax.axis_index("ctx") % INNER_PEERS
    got = [parts[0]] + [paired(parts[d], d * INNER_PEERS) for d in range(1, len(parts))]
    rows = sum(got[1:], got[0])
    total = lax.dynamic_index_in_dim(rows, place, 0, keepdims=False)
    for distance in range(1, INNER_PEERS):
        other = lax.dynamic_index_in_dim(rows, place ^ distance, 0, keepdims=False)
        total = total + paired(other, distance)
    return total


def after(value, *others):
    return lax.optimization_barrier((value,) + others)[0]


def in_hbm(*values):
    return [pltpu.with_memory_space_constraint(value, pltpu.HBM) for value in values]


def params(mib=63):
    return pltpu.CompilerParams(vmem_limit_bytes=mib * 1024 * 1024)


BESIDE_EXCHANGE = 40_000_000_000
WHOLE_EXCHANGE = 100_000_000_000


def cost(flops, size):
    return pl.CostEstimate(flops=flops, bytes_accessed=size, transcendentals=0)


def kernel_plan(
    query_feat, key_feat, value_raw, conv_out, out_grad, filter_taps, short_filter, skip_gain
):
    rows, channels = query_feat.shape
    peers = lax.axis_size("ctx")
    width = channels // peers
    seq = rows * peers
    outer = 2 * seq // INNER
    bins = outer // 2 + 1
    steps = 2
    group = peers // steps
    span = group * width
    far = peers // INNER_PEERS
    any_place = pl.BlockSpec(memory_space=pl.ANY)
    hbm = pl.BlockSpec(memory_space=pltpu.HBM)
    bf16, f32 = jnp.bfloat16, jnp.float32
    shape = jax.ShapeDtypeStruct
    skip_row = skip_gain.reshape(1, channels)
    ahead, back = (jnp.asarray(t) for t in spectrum_tables(outer))

    flat = pl.BlockSpec((rows, span), lambda i: (0, i))
    owned = pl.BlockSpec((group, rows, width), lambda i: (i, 0, 0))
    edge_spec = pl.BlockSpec((2, span), lambda i: (0, i))
    short_spec = pl.BlockSpec((3, span), lambda i: (0, i))

    gated, last = pl.pallas_call(
        functools.partial(gate_kernel, width=width),
        grid=(steps,),
        in_specs=[flat, flat, pl.BlockSpec((16, span), lambda i: (rows // 16 - 1, i))],
        out_specs=[owned, edge_spec],
        out_shape=[shape((peers, rows, width), bf16), shape((2, channels), f32)],
        compiler_params=params(),
        cost_estimate=cost(rows * channels, 6 * rows * channels),
        name="gate",
    )(out_grad, query_feat, value_raw)

    gated_got = exchanged(gated.reshape(seq, width))

    spec_shape = shape((bins, 2 * INNER, width), bf16)
    z_scratch = pltpu.VMEM((bins, 2 * INNER, width), bf16)
    u_scratch = pltpu.VMEM((bins, 2 * INNER, width), f32)
    table_scratch = pltpu.VMEM((bins, 2 * INNER, 2 * INNER), bf16)
    table_bytes = 8 * bins * INNER * INNER
    spec_bytes = 4 * bins * INNER * width
    work = 2 * bins * (2 * INNER) ** 2 * width
    edge = passed_along(last, "ctx", 1)
    shift_scratch = pltpu.VMEM((2, rows + 8, 128), f32)
    near_spec = pl.BlockSpec((far, rows, width), lambda i: (0, 0, 0))
    far_spec = pl.BlockSpec((INNER_PEERS - 1, rows, width), lambda i: (0, 0, 0))
    place_spec = pl.BlockSpec((rows, width), lambda i: (0, 0))
    *mixed, query_grad = pl.pallas_call(
        functools.partial(mix_kernel, width=width),
        grid=(steps,),
        in_specs=[flat, flat, edge_spec, short_spec, flat, flat],
        out_specs=[near_spec] * (INNER_PEERS - 1) + [place_spec] * far + [flat],
        out_shape=[shape((far, rows, width), bf16)] * (INNER_PEERS - 1)
        + [shape((rows, width), bf16)] * far
        + [shape((rows, channels), bf16)],
        scratch_shapes=[shift_scratch, pltpu.VMEM((peers, rows, width), bf16)],
        compiler_params=params(),
        cost_estimate=cost(BESIDE_EXCHANGE, 12 * rows * channels),
        name="mix",
    )(key_feat, value_raw, edge, short_filter, out_grad, conv_out)
    near = [paired(mixed[e - 1], e) for e in range(1, INNER_PEERS)]
    placed = mixed[INNER_PEERS - 1 :]
    placed = [placed[0]] + [paired(placed[d], d * INNER_PEERS) for d in range(1, far)]
    across = pl.pallas_call(
        regroup_kernel,
        grid=(1,),
        in_specs=[near_spec] * (INNER_PEERS - 1),
        out_specs=[far_spec] * (far - 1),
        out_shape=[shape((INNER_PEERS - 1, rows, width), bf16)] * (far - 1),
        compiler_params=params(),
        cost_estimate=cost(0, 4 * seq * width),
        name="regroup",
    )(*near)
    filter_taps, query_grad = lax.optimization_barrier((filter_taps, query_grad))
    filter_spec = pl.pallas_call(
        functools.partial(filter_kernel, outer=outer, width=width),
        out_shape=spec_shape,
        scratch_shapes=[pltpu.VMEM((seq, width), f32), z_scratch],
        compiler_params=params(),
        cost_estimate=cost(BESIDE_EXCHANGE, table_bytes + spec_bytes + 2 * seq * width),
        name="filter_spectrum",
    )(filter_taps, ahead)


    *across, gated_got = lax.optimization_barrier((*across, gated_got))
    across = [paired(across[d - 1], d * INNER_PEERS) for d in range(1, far)]

    conv_back, gated_spec = pl.pallas_call(
        functools.partial(conv_kernel, outer=outer, width=width),
        in_specs=[hbm] * 4 + [pl.BlockSpec(memory_space=pltpu.VMEM)],
        out_specs=[pl.BlockSpec(memory_space=pltpu.VMEM), hbm],
        out_shape=(shape((seq, width), bf16), spec_shape),
        scratch_shapes=[pltpu.VMEM((seq, width), bf16), z_scratch, table_scratch, table_scratch, z_scratch]
        + [z_scratch, u_scratch, pltpu.SemaphoreType.DMA((5,))],
        compiler_params=params(),
        cost_estimate=cost(BESIDE_EXCHANGE, 2 * table_bytes + 2 * spec_bytes + 4 * seq * width),
        name="conv_back",
    )(gated_got, filter_spec, ahead, back, skip_row)

    back_got = exchanged(conv_back).reshape(peers, rows, width)

    filter_grad, skip_grad = pl.pallas_call(
        functools.partial(grad_kernel, outer=outer, width=width),
        in_specs=[hbm] * (INNER_PEERS + 2 * far + 2),
        out_shape=[shape((width, seq), bf16), shape((1, width), f32)],
        scratch_shapes=[
            pltpu.VMEM((peers, rows, width), bf16),
            pltpu.VMEM((seq, width), bf16),
            z_scratch,
            table_scratch,
            table_scratch,
            z_scratch,
            u_scratch,
            pltpu.VMEM((seq, width), f32),
            pltpu.SemaphoreType.DMA((peers + 4,)),
        ],
        compiler_params=params(30),
        cost_estimate=cost(WHOLE_EXCHANGE, 2 * table_bytes + spec_bytes),
        name="filter_grad",
    )(*in_hbm(*placed, *near, *across, gated_got, gated_spec, ahead, back))
    back_got, filter_grad, skip_grad = lax.optimization_barrier((back_got, filter_grad, skip_grad))

    head, *short_parts = pl.pallas_call(
        functools.partial(sums_kernel, width=width),
        grid=(steps,),
        in_specs=[owned, flat, flat, edge_spec],
        out_specs=[edge_spec]
        + [pl.BlockSpec((INNER_PEERS, 8, width), lambda i: (0, 0, 0))] * far,
        out_shape=[pltpu.HBM((2, channels), f32)]
        + [pltpu.HBM((INNER_PEERS, 8, width), f32)] * far,
        scratch_shapes=[shift_scratch, pltpu.VMEM((peers, 8, width), f32)],
        compiler_params=params(30),
        cost_estimate=cost(20 * rows * channels, 8 * rows * channels),
        name="sums",
    )(back_got, key_feat, value_raw, edge)

    head_got = passed_along(head, "ctx", -1)
    short_grad = summed_at_owner(short_parts)
    key_grad, value_grad = pl.pallas_call(
        functools.partial(finish_kernel, width=width),
        grid=(steps,),
        in_specs=[owned, flat, flat, edge_spec, edge_spec, short_spec],
        out_specs=[flat, flat],
        out_shape=[pltpu.HBM((rows, channels), bf16)] * 2,
        scratch_shapes=[shift_scratch] * 2,
        compiler_params=params(30),
        cost_estimate=cost(30 * rows * channels, 12 * rows * channels),
        name="finish",
    )(back_got, key_feat, value_raw, edge, head_got, short_filter)
    return query_grad, key_grad, value_grad, filter_grad, skip_grad.reshape(width), short_grad[:3]


def per_device(query_feat, key_feat, value_raw, conv_out, out_grad, filter_taps, short_filter, skip_gain):
    rows, channels = query_feat.shape
    peers = lax.axis_size("ctx")
    width = channels // peers
    fits = (
        peers % INNER_PEERS == 0
        and peers & (peers - 1) == 0
        and rows == INNER
        and width % 256 == 0
        and peers in (8, 16)
    )
    plan = kernel_plan if fits else general_plan
    return plan(query_feat, key_feat, value_raw, conv_out, out_grad, filter_taps, short_filter, skip_gain)


def solution(mesh):
    in_specs = (
        P(("groups", "ctx"), None),
        P(("groups", "ctx"), None),
        P(("groups", "ctx"), None),
        P(("groups", "ctx"), None),
        P(("groups", "ctx"), None),
        P("ctx", None),
        P(),
        P(),
    )
    out_specs = (
        P(("groups", "ctx"), None),
        P(("groups", "ctx"), None),
        P(("groups", "ctx"), None),
        P(("groups", "ctx"), None),
        P(("groups", "ctx")),
        P(None, ("groups", "ctx")),
    )
    return jax.shard_map(
        per_device, mesh=mesh, in_specs=in_specs, out_specs=out_specs, check_vma=False
    )
```
